32 devices in a mesh: seq: 8 (over z, y), enc: 4 (over x, core).
Axes of the slice: x: 2, y: 2, z: 4, core: 2. Of those that a mesh axis runs over, the one named last changes fastest.
Arguments:
- source_ids: int32 [8, 1024], P('seq', 'enc'), may hold values from 0 to 25599
- target_ids: int32 [8, 1024], P('seq', 'enc'), may hold values from 0 to 25599
- labels: int32 [8, 1024], P('seq', 'enc'), may hold values from 0 to 25599
- lengths: int32 [8, 2], P('seq'), may hold values from 170 to 1024, as said below
- embedding: bfloat16 [25600, 1024], P('enc'), may hold values from -0.375 to 0.375
- positions: bfloat16 [2, 1024, 1024], P(None, 'enc'), may hold values from -0.375 to 0.375
- attention_in: bfloat16 [3, 1024, 3072], P(None, ('seq', 'enc')), may hold values from -0.1875 to 0.1875
- attention_out: bfloat16 [3, 1024, 1024], P(None, ('seq', 'enc')), may hold values from -6 to 6
- feed_in: bfloat16 [2, 1024, 4096], P(None, ('seq', 'enc')), may hold values from -0.1875 to 0.1875
- feed_out: bfloat16 [2, 4096, 1024], P(None, ('seq', 'enc')), may hold values from -0.09375 to 0.09375
- adapter_down: float32 [2, 1024, 512], P(None, ('seq', 'enc')), may hold values from -0.1875 to 0.1875
- adapter_up: float32 [2, 512, 1024], P(None, ('seq', 'enc')), may hold values from -0.25 to 0.25
- norm_params: float32 [2, 7, 1024], P(None, None, ('seq', 'enc')), may hold values from -0.9 to 2.25
- down_moment: float32 [2, 1024, 512], P(None, ('seq', 'enc')), may hold values from -0.00030517578 to 0.00030517578
- down_second: float32 [2, 1024, 512], P(None, ('seq', 'enc')), may hold values from 2.959998e-11 to 1.1839991e-10
- up_moment: float32 [2, 512, 1024], P(None, ('seq', 'enc')), may hold values from -0.00030517578 to 0.00030517578
- up_second: float32 [2, 512, 1024], P(None, ('seq', 'enc')), may hold values from 2.959998e-11 to 1.1839991e-10
- norm_moment: float32 [2, 7, 1024], P(None, None, ('seq', 'enc')), may hold values from -0.0008544922 to 0.0008544922
- norm_second: float32 [2, 7, 1024], P(None, None, ('seq', 'enc')), may hold values from 2.6521582e-10 to 1.0655993e-09
Outputs:
- loss_sum: float32 [], replicated
- token_count: float32 [], replicated
- grad_norm: float32 [], replicated
- moment_down: float32 [2, 1024, 512], P(None, ('seq', 'enc'))
- second_down: float32 [2, 1024, 512], P(None, ('seq', 'enc'))
- updated_down: float32 [2, 1024, 512], P(None, ('seq', 'enc'))
- moment_up: float32 [2, 512, 1024], P(None, ('seq', 'enc'))
- second_up: float32 [2, 512, 1024], P(None, ('seq', 'enc'))
- updated_up: float32 [2, 512, 1024], P(None, ('seq', 'enc'))
- moment_norms: float32 [2, 7, 1024], P(None, None, ('seq', 'enc'))
- second_norms: float32 [2, 7, 1024], P(None, None, ('seq', 'enc'))
- updated_norms: float32 [2, 7, 1024], P(None, None, ('seq', 'enc'))
The draws below stay inside these ranges and needn't reach their ends.
Inputs may be any that keep to these rules, and one draw needn't show every extreme that they name: Group g lies in bucket b = 3 g // 8; both of its lengths lie in 1024 (2 b + 1) // 6 to 1024 (2 b + 2) // 6, except in one group drawn from the seed whose two lengths are both 1024.
All inputs are finite; a program needn't handle non-finite values.
Results may differ from the reference program's by a relative error of at most 0.005.
The reference program's roundings to bfloat16 on the way count: a program that leaves them out, or rounds other values in their place, can miss the bound.
Values may be sent and summed in bfloat16 or wider, within the bound.
No kernel may reach another device: no remote copies, remote signals or barrier semaphores. Data moves between devices by JAX's collectives and lax.ppermute only.
A program may use at most 640 MiB of HBM per device.

```python
import math
import jax
import jax.numpy as jnp
import numpy as np
from jax import lax

D = 1024
HEADS = 16
HEAD_DIM = 64
FF = 4096
ADAPT = 512
ROWS = 256
STEP = 10
VOCAB = 25600
LENGTH = 1024
GROUPS = 8
N_ENC = 4


def draw_lengths(key, part):
    key = jax.random.fold_in(key, 11)
    keys = jax.random.split(key, 2)
    groups = jnp.arange(GROUPS)
    bucket = 3 * groups // GROUPS
    lower = LENGTH * (2 * bucket + 1) // 6
    upper = LENGTH * (2 * bucket + 2) // 6
    drawn = jax.random.randint(keys[0], (GROUPS, 2), lower[:, None], upper[:, None] + 1)
    chosen = jax.random.randint(keys[1], (), 0, GROUPS)
    drawn = jnp.where((groups == chosen)[:, None], LENGTH, drawn)
    return drawn.astype(jnp.int32)


def draw_embedding(key, part):
    key = jax.random.fold_in(key, 12)
    ramp = jnp.arange(VOCAB, dtype=jnp.float32)[:, None] / VOCAB
    noise = jnp.clip(jax.random.normal(key, (VOCAB, D), jnp.float32), -4.0, 4.0)
    scale = 1.0 + 2.0 * ramp
    return (noise * scale / math.sqrt(D)).astype(jnp.bfloat16)


def draw_norm_params(key, part):
    key = jax.random.fold_in(key, 13)
    keys = jax.random.split(key, 2)
    ramp = 0.6 + 1.2 * jnp.arange(D, dtype=jnp.float32) / D
    spread = 1.0 + 0.1 * jnp.clip(jax.random.normal(keys[0], (7, D), jnp.float32), -2.5, 2.5)
    shifted = 0.3 * jnp.clip(jax.random.normal(keys[1], (7, D), jnp.float32), -3.0, 3.0)
    return jnp.stack([ramp[None, :] * spread, shifted]).astype(jnp.float32)


def plant(entries, rng, smallest, top_value):
    shape = entries.shape
    spot = [jax.random.randint(jax.random.fold_in(rng, axis), (), 0, shape[axis]) for axis in range(len(shape))]
    entries = entries.at[tuple(spot)].set(smallest)
    longest = shape.index(max(shape))
    spot[longest] = (spot[longest] + 1) % shape[longest]
    return entries.at[tuple(spot)].set(top_value)


def level_of(stream_key, dims, cuts, smallest, high):
    factor_of, own = 1.0, jax.random.fold_in(stream_key, 6)
    for position, blocks in cuts:
        heights = jnp.exp(jax.random.uniform(jax.random.fold_in(own, position), (blocks,), jnp.float32, smallest / len(cuts), high / len(cuts)))
        factor_of = factor_of * jnp.repeat(heights, dims[position] // blocks).reshape([-1 if axis == position else 1 for axis in range(len(dims))])
    return factor_of


def rank_bounds(number_of, slope):
    portions = [(1 << 20) // math.isqrt(grade ** slope) + 1 for grade in range(1, number_of + 1)]
    scale = 1 + sum(portions) // (1 << 30)
    return np.cumsum(np.array([max(1, weight // scale) for weight in portions]))


def ranked(key, dims, count, lean):
    grid = rank_bounds(count, lean)
    pick = jax.random.randint(jax.random.fold_in(key, 1), dims, 0, int(grid[count - 1]))
    grade = jnp.searchsorted(jnp.asarray(grid, jnp.int32), pick, side="right")
    return jax.random.permutation(jax.random.fold_in(key, 2), count)[grade].astype(jnp.int32)


def gaussian(key, extent, deviation, reach, shards=(), kind=jnp.bfloat16):
    values = deviation * jax.random.normal(key, extent, jnp.float32)
    if shards:
        values = values * level_of(key, extent, shards, -0.22, 0.18)
    return jnp.clip(values, -reach, reach).astype(kind)


def setup_inputs(seed: int = 0) -> dict:
    key_list = jax.random.split(jax.random.key(seed), 20)
    return {
        "source_ids": plant(ranked(key_list[0], (GROUPS, LENGTH), VOCAB, 2), jax.random.fold_in(key_list[0], 3), 0, VOCAB - 1).astype(jnp.int32),
        "target_ids": plant(ranked(key_list[1], (GROUPS, LENGTH), VOCAB, 2), jax.random.fold_in(key_list[1], 3), 0, VOCAB - 1).astype(jnp.int32),
        "labels": plant(ranked(key_list[2], (GROUPS, LENGTH), VOCAB, 2), jax.random.fold_in(key_list[2], 3), 0, VOCAB - 1).astype(jnp.int32),
        "lengths": draw_lengths(jax.random.fold_in(key_list[19], 71), 0),
        "embedding": draw_embedding(jax.random.fold_in(key_list[19], 71), 0),
        "positions": gaussian(key_list[5], (2, LENGTH, D), (D // 4) ** -0.5, 0.375, ((1, 4),)),
        "attention_in": gaussian(key_list[6], (3, D, 3 * D), D ** -0.5, 0.1875, ((1, 32),)),
        "attention_out": gaussian(key_list[7], (3, D, D), (max(1, D // (ROWS * N_ENC))) ** -0.5, 6.0, ((1, 32),)),
        "feed_in": gaussian(key_list[8], (2, D, FF), D ** -0.5, 0.1875, ((1, 32),)),
        "feed_out": gaussian(key_list[9], (2, FF, D), FF ** -0.5, 0.09375, ((1, 32),)),
        "adapter_down": gaussian(key_list[10], (2, D, ADAPT), D ** -0.5, 0.1875, ((1, 32),), jnp.float32),
        "adapter_up": gaussian(key_list[11], (2, ADAPT, D), ADAPT ** -0.5, 0.25, ((1, 32),), jnp.float32),
        "norm_params": draw_norm_params(jax.random.fold_in(key_list[19], 71), 0),
        "down_moment": gaussian(key_list[13], (2, D, ADAPT), (0.02775 / (4 * D * ADAPT + 14 * D) ** 0.5), 0.00030517578, ((1, 32),), jnp.float32),
        "down_second": jnp.clip(jnp.exp(math.log(1.1839991487239132e-10) - 1.3862944 * jax.random.uniform(key_list[14], (2, D, ADAPT), jnp.float32) ** level_of(key_list[14], (2, D, ADAPT), ((1, 32),), -0.2, 0.2)), 2.959997871809783e-11, 1.1839991487239132e-10),
        "up_moment": gaussian(key_list[15], (2, ADAPT, D), (0.02775 / (4 * D * ADAPT + 14 * D) ** 0.5), 0.00030517578, ((1, 32),), jnp.float32),
        "up_second": jnp.clip(jnp.exp(math.log(1.1839991487239132e-10) - 1.3862944 * jax.random.uniform(key_list[16], (2, ADAPT, D), jnp.float32) ** level_of(key_list[16], (2, ADAPT, D), ((1, 32),), -0.2, 0.2)), 2.959997871809783e-11, 1.1839991487239132e-10),
        "norm_moment": gaussian(key_list[17], (2, 7, D), (0.0833 / (4 * D * ADAPT + 14 * D) ** 0.5), 0.0008544922, ((2, 32),), jnp.float32),
        "norm_second": jnp.clip(jnp.exp(math.log(1.0655992754848853e-09) - 1.3907487 * jax.random.uniform(key_list[18], (2, 7, D), jnp.float32) ** level_of(key_list[18], (2, 7, D), ((2, 32),), -0.2, 0.2)), 2.6521582152660983e-10, 1.0655992754848853e-09),
    }


EPSILON = 1e-05
ADAPTER_SCALE = 4.0
CLIP_NORM = 0.25
RATE_ADAPTER = 0.05
RATE_NORMS = 0.5
BETA_FIRST = 0.9
BETA_SECOND = 0.999
ADAM_EPSILON = 1e-08
DECAY_ADAPTER = 0.01
MASKED_SCORE = -1000000000.0

@jax.custom_vjp
def low(v):
    return lax.optimization_barrier(v.astype(jnp.bfloat16)).astype(jnp.float32)

@jax.custom_vjp
def low_back(v):
    return v

def low_keep(v):
    return (low(v), None)

def low_pass(kept, grad):
    return (grad,)

def back_keep(v):
    return (v, None)

def back_low(kept, grad):
    return (low(grad),)
low.defvjp(low_keep, low_pass)
low_back.defvjp(back_keep, back_low)

def matmul_high(left, right):
    return jnp.dot(left, right, precision=lax.Precision.HIGHEST, preferred_element_type=jnp.float32)

def smooth(values):
    return jax.nn.gelu(values, approximate=False)

def layer_norm(values, gain, shift):
    middle = lax.optimization_barrier(jnp.mean(values, -1, keepdims=True))
    centred = values - middle
    variance = lax.optimization_barrier(jnp.mean(centred * centred, -1, keepdims=True))
    return centred * lax.rsqrt(variance + EPSILON) * gain + shift

def attention(source_rows, key_rows, block_weights, out_weights, allowed):
    queries = low_back(low(matmul_high(source_rows, block_weights[:, :D])))
    pairs = low_back(low(matmul_high(key_rows, block_weights[:, D:])))

    def split_heads(matrix):
        return matrix.reshape(LENGTH, HEADS, HEAD_DIM).transpose(1, 0, 2)

    def one_head(triple):
        query_head, key_head, value_head = triple
        scores = low_back(matmul_high(query_head, key_head.T) * 0.125)
        scores = jnp.where(allowed, scores, MASKED_SCORE)
        highest = lax.optimization_barrier(jnp.max(scores, -1, keepdims=True))
        exponent = jnp.exp(scores - highest)
        soft_weights = exponent / lax.optimization_barrier(jnp.sum(exponent, -1, keepdims=True))
        return matmul_high(low(soft_weights), value_head)
    context = lax.map(jax.checkpoint(one_head), (split_heads(queries), split_heads(pairs[:, :D]), split_heads(pairs[:, D:])))
    context = low(low_back(context.transpose(1, 0, 2).reshape(LENGTH, D)))
    return low_back(matmul_high(context, out_weights))

def branch(rows, expand_weights, reduce_weights, down_weights, up_weights):
    rows_low = low(rows)
    hidden = low(smooth(low_back(matmul_high(rows_low, expand_weights))))
    adapted = low(smooth(low_back(matmul_high(rows_low, down_weights))))
    return low_back(matmul_high(hidden, reduce_weights)) + ADAPTER_SCALE * low_back(matmul_high(adapted, up_weights))

def group_loss(trained, frozen, source_row, target_row, label_row, length_pair):
    down_weights = low(trained[0])
    up_weights = low(trained[1])
    norms = low(trained[2])
    table, places, attend_in, attend_out, expand_weights, reduce_weights = frozen
    spots = jnp.arange(LENGTH)
    source_mask = jnp.broadcast_to(spots[None, :] < length_pair[0], (LENGTH, LENGTH))
    causal_mask = (spots[None, :] <= spots[:, None]) & (spots[None, :] < length_pair[1])

    def normed(values, index):
        return layer_norm(values, norms[0, index], norms[1, index])
    encoder_in = normed(table[source_row] + places[0], 0)
    encoder_low = low(encoder_in)
    after_self = normed(encoder_in + attention(encoder_low, encoder_low, attend_in[0], attend_out[0], source_mask), 1)
    encoded = normed(after_self + branch(after_self, expand_weights[0], reduce_weights[0], down_weights[0], up_weights[0]), 2)
    encoded_low = low(encoded)
    decoder_in = normed(table[target_row] + places[1], 3)
    decoder_low = low(decoder_in)
    after_causal = normed(decoder_in + attention(decoder_low, decoder_low, attend_in[1], attend_out[1], causal_mask), 4)
    after_cross = normed(after_causal + attention(low(after_causal), encoded_low, attend_in[2], attend_out[2], source_mask), 5)
    decoded = normed(after_cross + branch(after_cross, expand_weights[1], reduce_weights[1], down_weights[1], up_weights[1]), 6)
    decoded_low = low(decoded)
    valid = (spots < length_pair[1]).astype(jnp.float32)
    block_rows = min(512, LENGTH)

    def head_block(triple):
        rows, marks, keep = triple
        logits = low_back(matmul_high(rows, table.T))
        highest = lax.optimization_barrier(jnp.max(logits, -1, keepdims=True))
        log_total = highest[:, 0] + jnp.log(lax.optimization_barrier(jnp.sum(jnp.exp(logits - highest), -1)))
        picked = jnp.take_along_axis(logits, marks[:, None], 1)[:, 0]
        return jnp.sum((log_total - picked) * keep)
    losses = lax.map(jax.checkpoint(head_block), (decoded_low.reshape(-1, block_rows, D), label_row.reshape(-1, block_rows), valid.reshape(-1, block_rows)))
    return jnp.sum(losses)

def adamw(grad, moment, second, weight, rate, decay):
    moment = BETA_FIRST * moment + (1.0 - BETA_FIRST) * grad
    second = BETA_SECOND * second + (1.0 - BETA_SECOND) * grad * grad
    corrected = moment / (1.0 - BETA_FIRST ** STEP)
    scale_two = jnp.sqrt(second / (1.0 - BETA_SECOND ** STEP))
    return (moment, second, weight - rate * (corrected / (scale_two + ADAM_EPSILON) + decay * weight))

def reference(source_ids, target_ids, labels, lengths, embedding, positions, attention_in, attention_out, feed_in, feed_out, adapter_down, adapter_up, norm_params, down_moment, down_second, up_moment, up_second, norm_moment, norm_second):
    frozen = tuple((entry.astype(jnp.float32) for entry in (embedding, positions, attention_in, attention_out, feed_in, feed_out)))
    trained = (adapter_down, adapter_up, norm_params)

    def step(carry, group):
        loss_total, grads = carry
        source_row, target_row, label_row, length_pair = group

        def loss_of(weights):
            return group_loss(weights, frozen, source_row, target_row, label_row, length_pair)
        loss_value, pull = jax.vjp(loss_of, trained)
        partial_grads, = pull(jnp.ones((), jnp.float32))
        return ((loss_total + loss_value, jax.tree.map(jnp.add, grads, partial_grads)), None)
    start = (jnp.zeros((), jnp.float32), jax.tree.map(jnp.zeros_like, trained))
    (loss_sum, grads), _ = lax.scan(step, start, (source_ids, target_ids, labels, lengths))
    token_count = jnp.sum(lengths[:, 1]).astype(jnp.float32)
    grads = jax.tree.map(lambda entry: entry / token_count, grads)
    squares = jnp.sum(grads[0] * grads[0]) + jnp.sum(grads[1] * grads[1]) + jnp.sum(grads[2] * grads[2])
    grad_norm = jnp.sqrt(squares)
    factor = jnp.minimum(1.0, CLIP_NORM / grad_norm)
    moment_down, second_down, updated_down = adamw(grads[0] * factor, down_moment, down_second, adapter_down, RATE_ADAPTER, DECAY_ADAPTER)
    moment_up, second_up, updated_up = adamw(grads[1] * factor, up_moment, up_second, adapter_up, RATE_ADAPTER, DECAY_ADAPTER)
    moment_norms, second_norms, updated_norms = adamw(grads[2] * factor, norm_moment, norm_second, norm_params, RATE_NORMS, 0.0)
    return (loss_sum, token_count, grad_norm, moment_down, second_down, updated_down, moment_up, second_up, updated_up, moment_norms, second_norms, updated_norms)
```

```python
import jax
import jax.numpy as jnp
from jax import lax
from jax.experimental import pallas as pl
from jax.experimental.pallas import tpu as pltpu
from jax.sharding import PartitionSpec as P

HEAD_DIM = 64
STEP = 10

EPSILON = 1e-05
ADAPTER_SCALE = 4.0
CLIP_NORM = 0.25
RATE_ADAPTER = 0.05
RATE_NORMS = 0.5
BETA_FIRST = 0.9
BETA_SECOND = 0.999
ADAM_EPSILON = 1e-08
DECAY_ADAPTER = 0.01
MASKED_SCORE = -1000000000.0

LOW = jnp.bfloat16
F32 = jnp.float32
MIB = 1024 * 1024


def flip(value, axis, mask):
    count = lax.axis_size(axis)
    return lax.ppermute(value, axis, [(i, i ^ mask) for i in range(count)])


def bits(axis):
    count = lax.axis_size(axis)
    return [1 << i for i in range(count.bit_length() - 1)]


def unxor(blocks, me):
    blocks = list(blocks)
    mask = 1
    while mask < len(blocks):
        bit = (me & mask) != 0
        blocks = [jnp.where(bit, blocks[i ^ mask], blocks[i]) for i in range(len(blocks))]
        mask *= 2
    return blocks


def gather_enc(value):
    found = {0: value}
    for mask in bits("enc")[1:]:
        found.update({j | mask: flip(v, "enc", mask) for j, v in list(found.items())})
    found.update({j | 1: flip(v, "enc", 1) for j, v in list(found.items())})
    return [found[j] for j in range(len(found))]


def scatter_enc(blocks):
    held = dict(enumerate(blocks))
    for mask in bits("enc"):
        away = [j for j in held if j & mask]
        sent = [flip(held[j].astype(LOW), "enc", mask) for j in away]
        for j, part in zip(away, sent):
            held[j ^ mask] = held[j ^ mask].astype(F32) + part.astype(F32)
            del held[j]
    return held[0]


def swap_blocks(blocks):
    return [blocks[0]] + [flip(blocks[j], "enc", j) for j in range(1, len(blocks))]


def pair_split(shard, core):
    half = shard.shape[1] // 2
    first = core == 0
    low, high = shard[:, :half], shard[:, half:]
    keep = jnp.where(first, low, high)
    came = flip(jnp.where(first, high, low), "enc", 1)
    return jnp.concatenate([jnp.where(first, keep, came), jnp.where(first, came, keep)], 0)


def gather_first(value):
    stacked, offsets = value[None], [0]
    for mask in bits("seq")[1:]:
        stacked = jnp.concatenate([stacked, flip(stacked, "seq", mask)], 0)
        offsets = offsets + [o ^ mask for o in offsets]
    return stacked, offsets


def replicate(value, chips_last):
    stacked, offsets = gather_first(value)
    found = {(0, 0): stacked}
    near = [("seq", 1)]
    across = [("enc", mask) for mask in bits("enc")[1:]]
    for axis, mask in near + across if chips_last else across + near:
        fresh = {}
        for (s, e), v in found.items():
            fresh[(s ^ mask, e) if axis == "seq" else (s, e ^ mask)] = flip(v, axis, mask)
        found.update(fresh)
    return [(s, e, v) for (s, e), v in found.items()], offsets


def assemble(sources, pieces, places, outs):
    count = len(pieces)
    n_src, n_out = len(sources), len(outs)

    def kernel(*refs):
        table = refs[0]
        given = refs[1 : 1 + n_src]
        results = refs[1 + n_src : 1 + n_src + n_out]
        stage = refs[1 + n_src + n_out : 1 + n_src + n_out + count]
        sem_in, sem_out = refs[-2:]
        copies_in, copies_out = [], []
        for i, (src, block, row, column, rows, columns, out) in enumerate(pieces):
            copies_in.append(
                pltpu.make_async_copy(
                    given[src].at[block, pl.ds(row, rows), pl.ds(column, columns)],
                    stage[i],
                    sem_in.at[i],
                )
            )
            to_row = pl.multiple_of(table[2 * i], rows)
            to_column = pl.multiple_of(table[2 * i + 1], columns)
            copies_out.append(
                pltpu.make_async_copy(
                    stage[i],
                    results[out].at[pl.ds(to_row, rows), pl.ds(to_column, columns)],
                    sem_out.at[i],
                )
            )
        for copy in copies_in:
            copy.start()
        for i in range(count):
            copies_in[i].wait()
            copies_out[i].start()
        for copy in copies_out:
            copy.wait()

    size = sum(p[4] * p[5] * 2 for p in pieces)
    return pl.pallas_call(
        kernel,
        out_shape=[jax.ShapeDtypeStruct(shape, LOW) for shape in outs],
        in_specs=[pl.BlockSpec(memory_space=pltpu.SMEM)]
        + [pl.BlockSpec(memory_space=pl.ANY)] * n_src,
        out_specs=[pl.BlockSpec(memory_space=pl.ANY)] * n_out,
        scratch_shapes=[pltpu.VMEM((p[4], p[5]), LOW) for p in pieces]
        + [pltpu.SemaphoreType.DMA((count,)), pltpu.SemaphoreType.DMA((count,))],
        compiler_params=pltpu.CompilerParams(vmem_limit_bytes=size + 8 * MIB),
        cost_estimate=pl.CostEstimate(flops=0, bytes_accessed=2 * size, transcendentals=0),
    )(places, *sources)


def spread_matrix(shards, chips_last, layout, outs, seq, enc):
    n_enc = lax.axis_size("enc")
    core = enc & 1
    buffers, offsets = replicate(pair_split(shards, core), chips_last)
    sources, pieces, places = [], [], []
    for s_off, e_off, buffer in buffers:
        for mine, v in ((True, buffer), (False, flip(buffer, "enc", 1))):
            half = core if mine else 1 - core
            for n, o in enumerate(offsets):
                device = (seq ^ s_off ^ o) * n_enc + (enc ^ e_off)
                for row, column, rows, columns, out, to_row, to_column in layout(device >> 1, half):
                    pieces.append((len(sources), n, row, column, rows, columns, out))
                    places += [to_row, to_column]
            sources.append(v)
    return assemble(sources, pieces, jnp.stack([jnp.asarray(p, jnp.int32) for p in places]), outs)


def dense(left, right):
    return jnp.dot(left, right, preferred_element_type=F32)


def dense_back(left, right):
    return lax.dot_general(left, right, (((1,), (1,)), ((), ())), preferred_element_type=F32)


def inner_rows(left, right):
    return lax.dot_general(left, right, (((0,), (0,)), ((), ())), preferred_element_type=F32)


def layer_norm(values, gain, shift):
    middle = jnp.mean(values, -1, keepdims=True)
    centred = values - middle
    variance = jnp.mean(centred * centred, -1, keepdims=True)
    return centred * lax.rsqrt(variance + EPSILON) * gain + shift


def norm_forward(values, norms, index):
    return jax.vjp(layer_norm, values, norms[0, index], norms[1, index])


def adamw(grad, moment, second, weight, rate, decay):
    moment = BETA_FIRST * moment + (1.0 - BETA_FIRST) * grad
    second = BETA_SECOND * second + (1.0 - BETA_SECOND) * grad * grad
    corrected = moment / (1.0 - BETA_FIRST**STEP)
    scale_two = jnp.sqrt(second / (1.0 - BETA_SECOND**STEP))
    return (
        moment,
        second,
        weight - rate * (corrected / (scale_two + ADAM_EPSILON) + decay * weight),
    )


def masked_scores(query, key, spots, limit):
    raw = lax.dot_general(query, key, (((1,), (1,)), ((), ())), preferred_element_type=F32)
    return jnp.where(spots < limit, raw, MASKED_SCORE)


def attend_kernel(limit_ref, spot_ref, q_ref, k_ref, v_ref, context_ref, total_ref):
    scaled = q_ref[...] * jnp.asarray(0.125, LOW)
    key, value = k_ref[...], v_ref[...]
    side = lax.broadcasted_iota(jnp.int32, scaled.shape, 1) // HEAD_DIM
    context = jnp.zeros(scaled.shape, F32)
    total = jnp.zeros(scaled.shape, F32)
    for head in range(scaled.shape[1] // HEAD_DIM):
        own = side == head
        query = jnp.where(own, scaled, jnp.zeros((), LOW))
        scores = masked_scores(query, key, spot_ref[...], limit_ref[...])
        highest = jnp.max(scores, -1, keepdims=True)
        exponent = jnp.exp(scores - highest)
        summed = jnp.sum(exponent, -1, keepdims=True)
        mixed = jnp.dot(exponent.astype(LOW), value, preferred_element_type=F32) / summed
        context = jnp.where(own, mixed, context)
        total = jnp.where(own, highest + jnp.log(summed), total)
    context_ref[...] = context.astype(LOW)
    total_ref[...] = total


def attend(query, keys, key_at, value_at, limit, spots, rows):
    length = query.shape[0]
    width = keys.shape[1] // (2 if key_at == 0 else 3)
    pairs = width // 128
    steps = length // rows
    return pl.pallas_call(
        attend_kernel,
        grid=(pairs, steps),
        out_shape=[
            jax.ShapeDtypeStruct((length, width), LOW),
            jax.ShapeDtypeStruct((length, width), F32),
        ],
        in_specs=[
            pl.BlockSpec((rows, 1), lambda p, j: (j, 0)),
            pl.BlockSpec((1, length), lambda p, j: (0, 0)),
            pl.BlockSpec((rows, 128), lambda p, j: (j, p)),
            pl.BlockSpec((length, 128), lambda p, j: (0, key_at + p)),
            pl.BlockSpec((length, 128), lambda p, j: (0, value_at + p)),
        ],
        out_specs=[
            pl.BlockSpec((rows, 128), lambda p, j: (j, p)),
            pl.BlockSpec((rows, 128), lambda p, j: (j, p)),
        ],
        compiler_params=pltpu.CompilerParams(vmem_limit_bytes=48 * MIB),
        cost_estimate=pl.CostEstimate(
            flops=8 * length * length * width,
            bytes_accessed=8 * length * width,
            transcendentals=length * length * width // HEAD_DIM,
        ),
    )(limit, spots, query, keys, keys)


def attend_back_kernel(
    limit_ref, spot_ref, q_ref, k_ref, v_ref, grad_ref, total_ref, out_ref, dk_sum, dv_sum
):
    pair, step = pl.program_id(0), pl.program_id(1)
    pairs, steps = pl.num_programs(0), pl.num_programs(1)
    rows = q_ref.shape[0]

    @pl.when(step == 0)
    def _():
        dk_sum[...] = jnp.zeros_like(dk_sum)
        dv_sum[...] = jnp.zeros_like(dv_sum)

    scaled = q_ref[...] * jnp.asarray(0.125, LOW)
    key, value = k_ref[...], v_ref[...]
    grads, totals = grad_ref[...], total_ref[...]
    side = lax.broadcasted_iota(jnp.int32, scaled.shape, 1) // HEAD_DIM
    grad_query = jnp.zeros(scaled.shape, F32)
    nought = jnp.zeros((), LOW)
    for head in range(scaled.shape[1] // HEAD_DIM):
        own = side == head
        query = jnp.where(own, scaled, nought)
        grad = jnp.where(own, grads, nought)
        scores = masked_scores(query, key, spot_ref[...], limit_ref[...])
        soft = jnp.exp(scores - totals[:, head * HEAD_DIM : head * HEAD_DIM + 1])
        grad_soft = lax.dot_general(
            grad, value, (((1,), (1,)), ((), ())), preferred_element_type=F32
        )
        weighted = jnp.sum(soft * grad_soft, -1, keepdims=True)
        grad_scores = (soft * (grad_soft - weighted)).astype(LOW)
        grad_query = jnp.where(
            own, jnp.dot(grad_scores, key, preferred_element_type=F32), grad_query
        )
        dk_sum[...] += inner_rows(grad_scores, query)
        dv_sum[...] += inner_rows(soft.astype(LOW), grad)
    column = pl.multiple_of(pair * 128, 128)
    out_ref[pl.ds(pl.multiple_of(step * rows, rows), rows), pl.ds(column, 128)] = (
        grad_query * 0.125
    ).astype(LOW)

    @pl.when(step == steps - 1)
    def _():
        out_ref[:, pl.ds(pl.multiple_of((pairs + pair) * 128, 128), 128)] = dk_sum[...].astype(LOW)
        out_ref[:, pl.ds(pl.multiple_of((2 * pairs + pair) * 128, 128), 128)] = dv_sum[...].astype(
            LOW
        )


def attend_back(query, keys, key_at, value_at, limit, spots, rows, grads, totals):
    length, width = grads.shape
    pairs = width // 128
    steps = length // rows
    return pl.pallas_call(
        attend_back_kernel,
        grid=(pairs, steps),
        out_shape=jax.ShapeDtypeStruct((length, 3 * width), LOW),
        in_specs=[
            pl.BlockSpec((rows, 1), lambda p, j: (j, 0)),
            pl.BlockSpec((1, length), lambda p, j: (0, 0)),
            pl.BlockSpec((rows, 128), lambda p, j: (j, p)),
            pl.BlockSpec((length, 128), lambda p, j: (0, key_at + p)),
            pl.BlockSpec((length, 128), lambda p, j: (0, value_at + p)),
            pl.BlockSpec((rows, 128), lambda p, j: (j, p)),
            pl.BlockSpec((rows, 128), lambda p, j: (j, p)),
        ],
        out_specs=pl.BlockSpec((length, 3 * width), lambda p, j: (0, 0)),
        scratch_shapes=[pltpu.VMEM((length, 128), F32), pltpu.VMEM((length, 128), F32)],
        compiler_params=pltpu.CompilerParams(vmem_limit_bytes=56 * MIB),
        cost_estimate=pl.CostEstimate(
            flops=20 * length * length * width,
            bytes_accessed=16 * length * width,
            transcendentals=length * length * width // HEAD_DIM,
        ),
    )(limit, spots, query, keys, keys, grads, totals)


def gelu_both(values):
    below = 0.5 * (1.0 + lax.erf(values * 0.7071067811865476))
    bell = jnp.exp(values * values * -0.5) * 0.3989422804014327
    return values * below, below + values * bell


def branch_kernel(x_ref, in_ref, out_ref, down_ref, up_ref, y_ref, slope_ref, act_ref, bend_ref, total):
    step = pl.program_id(0)

    @pl.when(step == 0)
    def _():
        act, slope = gelu_both(jnp.dot(x_ref[...], down_ref[...], preferred_element_type=F32))
        act = act.astype(LOW)
        act_ref[...] = act
        bend_ref[...] = slope
        total[...] = ADAPTER_SCALE * jnp.dot(act, up_ref[...], preferred_element_type=F32)

    act, slope = gelu_both(jnp.dot(x_ref[...], in_ref[...], preferred_element_type=F32))
    slope_ref[...] = slope
    total[...] += jnp.dot(act.astype(LOW), out_ref[...], preferred_element_type=F32)

    @pl.when(step == pl.num_programs(0) - 1)
    def _():
        y_ref[...] = total[...]


def branch(rows_low, expand, reduce, down, up, layer, tile=512):
    rows, width = rows_low.shape
    hidden = expand.shape[1]
    small = down.shape[1]
    return pl.pallas_call(
        branch_kernel,
        grid=(hidden // tile,),
        out_shape=[
            jax.ShapeDtypeStruct((rows, width), F32),
            jax.ShapeDtypeStruct((rows, hidden), F32),
            jax.ShapeDtypeStruct((rows, small), LOW),
            jax.ShapeDtypeStruct((rows, small), F32),
        ],
        in_specs=[
            pl.BlockSpec((rows, width), lambda j: (0, 0)),
            pl.BlockSpec((width, tile), lambda j: (0, j)),
            pl.BlockSpec((tile, width), lambda j: (j, 0)),
            pl.BlockSpec((width, small), lambda j: (layer, 0)),
            pl.BlockSpec((small, width), lambda j: (layer, 0)),
        ],
        out_specs=[
            pl.BlockSpec((rows, width), lambda j: (0, 0)),
            pl.BlockSpec((rows, tile), lambda j: (0, j)),
            pl.BlockSpec((rows, small), lambda j: (0, 0)),
            pl.BlockSpec((rows, small), lambda j: (0, 0)),
        ],
        scratch_shapes=[pltpu.VMEM((rows, width), F32)],
        compiler_params=pltpu.CompilerParams(vmem_limit_bytes=48 * MIB),
        cost_estimate=pl.CostEstimate(
            flops=4 * rows * width * (hidden + small),
            bytes_accessed=4 * width * (hidden + small) + 4 * rows * hidden,
            transcendentals=2 * rows * hidden,
        ),
    )(rows_low, expand, reduce, down, up)


def branch_back_kernel(g_ref, ga_ref, in_ref, out_ref, down_ref, up_ref, slope_ref, bend_ref, dx_ref, dpre_ref, total):
    step = pl.program_id(0)

    @pl.when(step == 0)
    def _():
        grad = dense_back(ga_ref[...], up_ref[...])
        pre = (grad * bend_ref[...]).astype(LOW)
        dpre_ref[...] = pre
        total[...] = dense_back(pre, down_ref[...])

    grad = dense_back(g_ref[...], out_ref[...])
    total[...] += dense_back((grad * slope_ref[...]).astype(LOW), in_ref[...])

    @pl.when(step == pl.num_programs(0) - 1)
    def _():
        dx_ref[...] = total[...]


def branch_back(grad_out, kept, expand, reduce, down, up, layer, tile=512):
    rows_low, slope, act, bend = kept
    rows, width = rows_low.shape
    hidden = expand.shape[1]
    small = down.shape[1]
    grad_low = grad_out.astype(LOW)
    grad_adapter = (ADAPTER_SCALE * grad_out).astype(LOW)
    grad_rows, grad_pre = pl.pallas_call(
        branch_back_kernel,
        grid=(hidden // tile,),
        out_shape=[
            jax.ShapeDtypeStruct((rows, width), F32),
            jax.ShapeDtypeStruct((rows, small), LOW),
        ],
        in_specs=[
            pl.BlockSpec((rows, width), lambda j: (0, 0)),
            pl.BlockSpec((rows, width), lambda j: (0, 0)),
            pl.BlockSpec((width, tile), lambda j: (0, j)),
            pl.BlockSpec((tile, width), lambda j: (j, 0)),
            pl.BlockSpec((width, small), lambda j: (layer, 0)),
            pl.BlockSpec((small, width), lambda j: (layer, 0)),
            pl.BlockSpec((rows, tile), lambda j: (0, j)),
            pl.BlockSpec((rows, small), lambda j: (0, 0)),
        ],
        out_specs=[
            pl.BlockSpec((rows, width), lambda j: (0, 0)),
            pl.BlockSpec((rows, small), lambda j: (0, 0)),
        ],
        scratch_shapes=[pltpu.VMEM((rows, width), F32)],
        compiler_params=pltpu.CompilerParams(vmem_limit_bytes=48 * MIB),
        cost_estimate=pl.CostEstimate(
            flops=4 * rows * width * (hidden + small),
            bytes_accessed=4 * width * (hidden + small) + 4 * rows * hidden,
            transcendentals=0,
        ),
    )(grad_low, grad_adapter, expand, reduce, down, up, slope, bend)
    return grad_rows, inner_rows(rows_low, grad_pre), inner_rows(act, grad_adapter)


def head_kernel(o_ref, e_ref, g_ref, lse_ref, acc, peak, mass):
    step = pl.program_id(0)
    part = 256

    @pl.when(step == 0)
    def _():
        acc[...] = jnp.zeros_like(acc)
        peak[...] = jnp.full_like(peak, -1e30)
        mass[...] = jnp.zeros_like(mass)

    table = e_ref[...]
    for start in range(0, o_ref.shape[0], part):
        at = pl.ds(start, part)
        logits = dense_back(o_ref[at, :], table)
        before = peak[at, :1]
        highest = jnp.maximum(before, jnp.max(logits, -1, keepdims=True))
        exponent = jnp.exp(logits - highest)
        fade = jnp.exp(before - highest)
        mass[at, :] = mass[at, :] * fade + jnp.sum(exponent, -1, keepdims=True)
        acc[at, :] = acc[at, :] * fade + jnp.dot(
            exponent.astype(LOW), table, preferred_element_type=F32
        )
        peak[at, :] = jnp.broadcast_to(highest, (part, 128))

    @pl.when(step == pl.num_programs(0) - 1)
    def _():
        g_ref[...] = (acc[...] / mass[:, :1]).astype(LOW)
        lse_ref[...] = peak[...] + jnp.log(mass[...])


def head(rows_low, table):
    rows, width = rows_low.shape
    entries = table.shape[0]
    tile = next(t for t in (1280, 1024, 640, 512, 256, 128) if entries % t == 0)
    return pl.pallas_call(
        head_kernel,
        grid=(entries // tile,),
        out_shape=[
            jax.ShapeDtypeStruct((rows, width), LOW),
            jax.ShapeDtypeStruct((rows, 128), F32),
        ],
        in_specs=[
            pl.BlockSpec((rows, width), lambda j: (0, 0)),
            pl.BlockSpec((tile, width), lambda j: (j, 0)),
        ],
        out_specs=[
            pl.BlockSpec((rows, width), lambda j: (0, 0)),
            pl.BlockSpec((rows, 128), lambda j: (0, 0)),
        ],
        scratch_shapes=[
            pltpu.VMEM((rows, width), F32),
            pltpu.VMEM((rows, 128), F32),
            pltpu.VMEM((rows, 128), F32),
        ],
        compiler_params=pltpu.CompilerParams(vmem_limit_bytes=56 * MIB),
        cost_estimate=pl.CostEstimate(
            flops=4 * rows * width * entries,
            bytes_accessed=2 * width * entries,
            transcendentals=rows * entries,
        ),
    )(rows_low, table)


def reduce_shards(grad, seq, enc, order):
    n_seq, n_enc = lax.axis_size("seq"), lax.axis_size("enc")
    shard = grad.shape[0] // (n_seq * n_enc)
    seq_bits, enc_bits = len(bits("seq")), len(bits("enc"))
    held = grad.reshape((2,) * (seq_bits + enc_bits) + (shard, grad.shape[1]))
    left = [("seq", 1 << i) for i in reversed(range(seq_bits))]
    left += [("enc", 1 << i) for i in reversed(range(enc_bits))]
    for axis, mask in order:
        where = left.index((axis, mask))
        left.pop(where)
        bit = ((seq if axis == "seq" else enc) & mask) != 0
        low = lax.index_in_dim(held, 0, where, keepdims=False)
        high = lax.index_in_dim(held, 1, where, keepdims=False)
        keep = jnp.where(bit, high, low)
        send = jnp.where(bit, low, high)
        if axis == "enc" and mask == 1:
            held = keep + flip(send, axis, mask)
        else:
            held = keep + flip(send.astype(LOW), axis, mask).astype(F32)
    return held


def shards(
    source_ids,
    target_ids,
    labels,
    lengths,
    embedding,
    positions,
    attention_in,
    attention_out,
    feed_in,
    feed_out,
    adapter_down,
    adapter_up,
    norm_params,
    down_moment,
    down_second,
    up_moment,
    up_second,
    norm_moment,
    norm_second,
):
    n_seq, n_enc = lax.axis_size("seq"), lax.axis_size("enc")
    n_all = n_seq * n_enc
    seq, enc = lax.axis_index("seq"), lax.axis_index("enc")
    core = enc & 1
    own_rows = source_ids.shape[1]
    width = embedding.shape[1]
    entries = embedding.shape[0]
    length = own_rows * n_enc
    share = width // n_enc
    source_length, target_length = lengths[0, 0], lengths[0, 1]

    norms = norm_params.astype(LOW).reshape(1, 14, -1)
    for axis in ("enc", "seq"):
        for mask in bits(axis):
            norms = jnp.concatenate([norms, flip(norms, axis, mask)], 0)
    order = jnp.arange(n_all) ^ (seq * n_enc + enc)
    norms = jnp.take(norms, order, axis=0).transpose(1, 0, 2).reshape(2, 7, width).astype(F32)

    ids = jnp.concatenate([source_ids, target_ids, labels], 0)
    all_ids = jnp.stack(gather_enc(ids)) - enc * entries

    def lookup(which):
        local = all_ids[:, which]
        inside = (local >= 0) & (local < entries)
        found = jnp.take(embedding, jnp.clip(local, 0, entries - 1), axis=0)
        found = jnp.where(inside[:, :, None], found, jnp.zeros((), LOW))
        return scatter_enc([found[j] for j in range(n_enc)])

    source_rows = lookup(0) + positions[0].astype(F32)
    target_rows = lookup(1) + positions[1].astype(F32)
    label_rows = lookup(2)

    triple = attention_in.reshape(3, -1, 3, n_enc, share).transpose(3, 1, 0, 2, 4)
    triple = triple.reshape(n_enc, triple.shape[1], 9 * share)
    shard_rows = triple.shape[1]
    swapped = swap_blocks(
        [lax.dynamic_index_in_dim(triple, enc ^ j, 0, keepdims=False) for j in range(n_enc)]
    )
    strip = jnp.concatenate(unxor(swapped, enc), 0)
    strip_rows = n_enc * shard_rows
    stacked, offsets = gather_first(strip)
    strips = [(0, stacked), (1, flip(stacked, "seq", 1))]
    sources, pieces, places = [], [], []
    for s_off, buffer in strips:
        for n, o in enumerate(offsets):
            for k in range(3):
                pieces.append((len(sources), n, 0, k * 3 * share, strip_rows, 3 * share, k))
                places += [(seq ^ s_off ^ o) * strip_rows, 0]
        sources.append(buffer)
    attend_in = assemble(
        sources,
        pieces,
        jnp.stack([jnp.asarray(p, jnp.int32) for p in places]),
        [(width, 3 * share)] * 3,
    )

    half = width // 2
    packed = jnp.concatenate(
        [attention_out[k][:, h * half : (h + 1) * half] for h in range(2) for k in range(3)], 1
    )
    pair_rows = 2 * shard_rows

    def out_layout(pair, side):
        row = pair * pair_rows
        block = (row // share) ^ enc
        return [
            (0, k * half, pair_rows, half, k, block * share + row % share, side * half)
            for k in range(3)
        ]

    attend_out = spread_matrix(packed, True, out_layout, [(width, width)] * 3, seq, enc)

    hidden = feed_in.shape[2]

    def in_layout(pair, side):
        return [(0, 0, pair_rows, hidden // 2, 0, pair * pair_rows, side * (hidden // 2))]

    far_rows = 2 * feed_out.shape[1]

    def reduce_layout(pair, side):
        return [(0, 0, far_rows, half, 0, pair * far_rows, side * half)]

    expand = [
        spread_matrix(feed_in[k], True, in_layout, [(width, hidden)], seq, enc)[0] for k in range(2)
    ]
    reduce = [
        spread_matrix(feed_out[k], False, reduce_layout, [(hidden, width)], seq, enc)[0]
        for k in range(2)
    ]

    small = adapter_down.shape[2]
    up_rows = adapter_up.shape[1]
    down_shard = adapter_down.astype(LOW).transpose(1, 0, 2).reshape(shard_rows, 2 * small)
    up_shard = adapter_up.astype(LOW).reshape(2 * up_rows, width)
    both = unxor(gather_enc(jnp.concatenate([down_shard, up_shard], 0)), enc)
    downs = jnp.concatenate([v[:shard_rows] for v in both], 0)
    ups = [
        jnp.concatenate(
            [v[shard_rows + k * up_rows : shard_rows + (k + 1) * up_rows] for v in both], 0
        )
        for k in range(2)
    ]
    both = jnp.concatenate([downs] + ups, 0)
    both = jnp.where(core == 0, both[:, : width // 2], both[:, width // 2 :])
    stacked, offsets = gather_first(both)
    sources, pieces, places = [], [], []
    for s_off, buffer in [(0, stacked), (1, flip(stacked, "seq", 1))]:
        for side, v in ((core, buffer), (1 - core, flip(buffer, "enc", 1))):
            for n, o in enumerate(offsets):
                at = seq ^ s_off ^ o
                pieces.append((len(sources), n, 0, 0, strip_rows, small, 0))
                places += [side * width + at * strip_rows, 0]
                for k in range(2):
                    pieces.append(
                        (len(sources), n, strip_rows + k * n_enc * up_rows, 0, n_enc * up_rows, half, 1)
                    )
                    places += [k * small + at * n_enc * up_rows, side * half]
            sources.append(v)
    down_all, up_all = assemble(
        sources,
        pieces,
        jnp.stack([jnp.asarray(p, jnp.int32) for p in places]),
        [(2 * width, small), (2 * small, width)],
    )

    blocks = jnp.arange(n_enc) ^ enc
    spots = (blocks[:, None] * own_rows + jnp.arange(own_rows)[None, :]).reshape(length)
    spots = spots.astype(jnp.int32)
    source_limit = jnp.broadcast_to(source_length, (length, 1)).astype(jnp.int32)
    causal_limit = jnp.minimum(spots + 1, target_length)[:, None].astype(jnp.int32)
    spots = spots[None, :]
    in_strip = share // 128

    def gather_rows(rows_low):
        return jnp.concatenate(gather_enc(rows_low), 0)

    def finish_attention(context, k):
        parts = swap_blocks([context[j * own_rows : (j + 1) * own_rows] for j in range(n_enc)])
        return dense(jnp.concatenate(parts, 1), attend_out[k])

    def begin_attention_back(grad, k):
        spread = dense_back(grad.astype(LOW), attend_out[k]).astype(LOW)
        parts = swap_blocks([spread[:, j * share : (j + 1) * share] for j in range(n_enc)])
        return jnp.concatenate(parts, 0)

    def scatter_rows(partial):
        return scatter_enc([partial[j * own_rows : (j + 1) * own_rows] for j in range(n_enc)])

    encoder_in, pull_zero = norm_forward(source_rows, norms, 0)
    triple_encoder = dense(gather_rows(encoder_in.astype(LOW)), attend_in[0]).astype(LOW)
    enc_args = (triple_encoder, triple_encoder, in_strip, 2 * in_strip, source_limit, spots, own_rows)
    context, total_encoder = attend(*enc_args)
    after_self, pull_one = norm_forward(encoder_in + finish_attention(context, 0), norms, 1)
    after_self_low = after_self.astype(LOW)
    branched, *kept_enc = branch(after_self_low, expand[0], reduce[0], down_all, up_all, 0)
    encoded, pull_two = norm_forward(after_self + branched, norms, 2)
    encoded_all = gather_rows(encoded.astype(LOW))

    decoder_in, pull_three = norm_forward(target_rows, norms, 3)
    triple_decoder = dense(gather_rows(decoder_in.astype(LOW)), attend_in[1]).astype(LOW)
    dec_args = (triple_decoder, triple_decoder, in_strip, 2 * in_strip, causal_limit, spots, own_rows)
    context, total_decoder = attend(*dec_args)
    after_causal, pull_four = norm_forward(decoder_in + finish_attention(context, 1), norms, 4)
    query_cross = dense(gather_rows(after_causal.astype(LOW)), attend_in[2][:, :share]).astype(LOW)
    pairs_cross = dense(encoded_all, attend_in[2][:, share:]).astype(LOW)
    cross_args = (query_cross, pairs_cross, 0, in_strip, source_limit, spots, own_rows)
    context, total_cross = attend(*cross_args)
    after_cross, pull_five = norm_forward(after_causal + finish_attention(context, 2), norms, 5)
    after_cross_low = after_cross.astype(LOW)
    branched, *kept_dec = branch(after_cross_low, expand[1], reduce[1], down_all, up_all, 1)
    decoded, pull_six = norm_forward(after_cross + branched, norms, 6)

    decoded_low = decoded.astype(LOW)
    pulled, totals = head(gather_rows(decoded_low), embedding)
    totals = totals[:, :1]
    came = swap_blocks([totals[j * own_rows : (j + 1) * own_rows] for j in range(n_enc)])
    highest = came[0]
    for v in came[1:]:
        highest = jnp.maximum(highest, v)
    log_total = highest + jnp.log(sum(jnp.exp(v - highest) for v in came))
    row_spots = enc * own_rows + jnp.arange(own_rows)
    valid = (row_spots < target_length).astype(F32)[:, None]
    picked = jnp.sum(decoded_low.astype(F32) * label_rows, -1, keepdims=True)
    loss_own = jnp.sum((log_total - picked) * valid)
    all_totals = jnp.concatenate(gather_enc(log_total), 0)
    weight = jnp.exp(totals - all_totals)
    grad_decoded = (scatter_rows(pulled.astype(F32) * weight) - label_rows) * valid

    grad_res, gain_six, shift_six = pull_six(grad_decoded)
    grad_rows, down_dec, up_dec = branch_back(
        grad_res, [after_cross_low] + kept_dec, expand[1], reduce[1], down_all, up_all, 1
    )
    grad_res, gain_five, shift_five = pull_five(grad_res + grad_rows)
    grads = attend_back(*cross_args, begin_attention_back(grad_res, 2), total_cross)
    grad_encoded = scatter_rows(dense_back(grads[:, share:], attend_in[2][:, share:]))
    grad_causal = grad_res + scatter_rows(dense_back(grads[:, :share], attend_in[2][:, :share]))
    grad_res, gain_four, shift_four = pull_four(grad_causal)
    grads = attend_back(*dec_args, begin_attention_back(grad_res, 1), total_decoder)
    grad_decoder = grad_res + scatter_rows(dense_back(grads, attend_in[1]))
    grad_unused, gain_three, shift_three = pull_three(grad_decoder)
    grad_res, gain_two, shift_two = pull_two(grad_encoded)
    grad_rows, down_enc, up_enc = branch_back(
        grad_res, [after_self_low] + kept_enc, expand[0], reduce[0], down_all, up_all, 0
    )
    grad_res, gain_one, shift_one = pull_one(grad_res + grad_rows)
    grads = attend_back(*enc_args, begin_attention_back(grad_res, 0), total_encoder)
    grad_encoder = grad_res + scatter_rows(dense_back(grads, attend_in[0]))
    grad_unused, gain_zero, shift_zero = pull_zero(grad_encoder)

    near, across = [("seq", 1)], [("enc", mask) for mask in bits("enc")[1:]]
    slow = [("seq", mask) for mask in bits("seq")[1:]]
    pair = [("enc", 1)]
    grad_down = jnp.stack(
        [reduce_shards(g, seq, enc, pair + across + near + slow) for g in (down_enc, down_dec)]
    )
    grad_up = jnp.stack(
        [reduce_shards(g, seq, enc, pair + near + across + slow) for g in (up_enc, up_dec)]
    )
    count_own = jnp.clip(target_length - enc * own_rows, 0, own_rows).astype(F32)
    squares_own = jnp.sum(grad_down * grad_down) + jnp.sum(grad_up * grad_up)
    lanes = jnp.arange(width)
    scalars = jnp.where(
        lanes == 0, loss_own, jnp.where(lanes == 1, count_own, jnp.where(lanes == 2, squares_own, 0.0))
    )
    summed = jnp.stack(
        [gain_zero, gain_one, gain_two, gain_three, gain_four, gain_five, gain_six]
        + [shift_zero, shift_one, shift_two, shift_three, shift_four, shift_five, shift_six]
        + [scalars, jnp.zeros_like(scalars)]
    )
    for axis, mask in pair + across + near + slow:
        summed = summed + flip(summed, axis, mask)
    loss_sum, token_total = summed[14, 0], summed[14, 1]
    norm_grads = summed[:14]
    squares = summed[14, 2] + jnp.sum(norm_grads * norm_grads)
    per = width // n_all
    grad_norms = lax.dynamic_slice_in_dim(norm_grads, (seq * n_enc + enc) * per, per, 1)
    grad_norms = grad_norms.reshape(2, 7, per)

    grad_norm = jnp.sqrt(squares) / token_total
    factor = jnp.minimum(1.0, CLIP_NORM / grad_norm) / token_total
    moment_down, second_down, updated_down = adamw(
        grad_down * factor, down_moment, down_second, adapter_down, RATE_ADAPTER, DECAY_ADAPTER
    )
    moment_up, second_up, updated_up = adamw(
        grad_up * factor, up_moment, up_second, adapter_up, RATE_ADAPTER, DECAY_ADAPTER
    )
    moment_norms, second_norms, updated_norms = adamw(
        grad_norms * factor, norm_moment, norm_second, norm_params, RATE_NORMS, 0.0
    )
    return (
        loss_sum,
        token_total,
        grad_norm,
        moment_down,
        second_down,
        updated_down,
        moment_up,
        second_up,
        updated_up,
        moment_norms,
        second_norms,
        updated_norms,
    )


def solution(mesh):
    everywhere = P(None, ("seq", "enc"), None)
    columns = P(None, None, ("seq", "enc"))
    return jax.shard_map(
        shards,
        mesh=mesh,
        in_specs=(
            P("seq", "enc"),
            P("seq", "enc"),
            P("seq", "enc"),
            P("seq", None),
            P("enc", None),
            P(None, "enc", None),
            everywhere,
            everywhere,
            everywhere,
            everywhere,
            everywhere,
            everywhere,
            columns,
            everywhere,
            everywhere,
            everywhere,
            everywhere,
            columns,
            columns,
        ),
        out_specs=(
            P(),
            P(),
            P(),
            everywhere,
            everywhere,
            everywhere,
            everywhere,
            everywhere,
            everywhere,
            columns,
            columns,
            columns,
        ),
        check_vma=False,
    )
```

```python
import jax
import jax.numpy as jnp
from jax import lax
from jax.experimental import pallas as pl
from jax.experimental.pallas import tpu as pltpu
from jax.sharding import PartitionSpec as P

HEAD_DIM = 64
STEP = 10

EPSILON = 1e-05
ADAPTER_SCALE = 4.0
CLIP_NORM = 0.25
RATE_ADAPTER = 0.05
RATE_NORMS = 0.5
BETA_FIRST = 0.9
BETA_SECOND = 0.999
ADAM_EPSILON = 1e-08
DECAY_ADAPTER = 0.01
MASKED_SCORE = -1000000000.0

LOW = jnp.bfloat16
F32 = jnp.float32
MIB = 1024 * 1024


def flip(value, axis, mask):
    count = lax.axis_size(axis)
    return lax.ppermute(value, axis, [(i, i ^ mask) for i in range(count)])


def bits(axis):
    count = lax.axis_size(axis)
    return [1 << i for i in range(count.bit_length() - 1)]


def unxor(blocks, me):
    blocks = list(blocks)
    mask = 1
    while mask < len(blocks):
        bit = (me & mask) != 0
        blocks = [jnp.where(bit, blocks[i ^ mask], blocks[i]) for i in range(len(blocks))]
        mask *= 2
    return blocks


def gather_enc(value):
    found = {0: value}
    for mask in bits("enc")[1:]:
        found.update({j | mask: flip(v, "enc", mask) for j, v in list(found.items())})
    found.update({j | 1: flip(v, "enc", 1) for j, v in list(found.items())})
    return [found[j] for j in range(len(found))]


def scatter_steps(blocks):
    held = dict(enumerate(blocks))
    middle = []
    for mask in bits("enc"):
        away = [j for j in held if j & mask]
        parts = [held[j].astype(LOW) for j in away]
        if mask > 1:
            middle += parts
        sent = [flip(part, "enc", mask) for part in parts]
        for j, part in zip(away, sent):
            held[j ^ mask] = held[j ^ mask].astype(F32) + part.astype(F32)
            del held[j]
    return held[0], middle


def scatter_enc(blocks):
    return scatter_steps(blocks)[0]


def merge_enc(blocks, totals):
    held = {j: (b, t) for j, (b, t) in enumerate(zip(blocks, totals))}
    for mask in bits("enc"):
        away = [j for j in held if j & mask]
        sent = [(flip(held[j][0].astype(LOW), "enc", mask), flip(held[j][1], "enc", mask)) for j in away]
        for j, (mean, total) in zip(away, sent):
            own_mean, own_total = held[j ^ mask]
            highest = jnp.maximum(own_total, total)
            first, second = jnp.exp(own_total - highest), jnp.exp(total - highest)
            both = first + second
            mean = (own_mean.astype(F32) * first + mean.astype(F32) * second) / both
            held[j ^ mask] = (mean, highest + jnp.log(both))
            del held[j]
    return held[0]


def swap_blocks(blocks):
    return [blocks[0]] + [flip(blocks[j], "enc", j) for j in range(1, len(blocks))]


def pair_split(shard, core):
    half = shard.shape[1] // 2
    first = core == 0
    low, high = shard[:, :half], shard[:, half:]
    keep = jnp.where(first, low, high)
    came = flip(jnp.where(first, high, low), "enc", 1)
    return jnp.concatenate([jnp.where(first, keep, came), jnp.where(first, came, keep)], 0)


def gate(arrays):
    def kernel(*refs):
        pass

    return pl.pallas_call(
        kernel,
        out_shape=[jax.ShapeDtypeStruct(v.shape, v.dtype) for v in arrays],
        in_specs=[pl.BlockSpec(memory_space=pl.ANY)] * len(arrays),
        out_specs=[pl.BlockSpec(memory_space=pl.ANY)] * len(arrays),
        input_output_aliases={i: i for i in range(len(arrays))},
        cost_estimate=pl.CostEstimate(flops=0, bytes_accessed=0, transcendentals=0),
    )(*arrays)


def flip_both(value, seq_mask, enc_mask):
    n_enc = lax.axis_size("enc")
    perm = []
    for i in range(lax.axis_size("seq") * n_enc):
        s, e = divmod(i, n_enc)
        perm.append((i, (s ^ seq_mask) * n_enc + (e ^ enc_mask)))
    return lax.ppermute(value, ("seq", "enc"), perm)


def tree_sum(values):
    values = list(values)
    while len(values) > 1:
        values = [values[i] + values[i + 1] for i in range(0, len(values), 2)]
    return values[0]


def plane_offsets():
    near = lax.axis_size("seq") // 4
    return [(s, e) for e in range(0, lax.axis_size("enc"), 2) for s in range(near)]


def line_offsets():
    return [k * (lax.axis_size("seq") // 4) for k in range(4)]


def mixed_flip(value, for_even, for_odd):
    n_enc = lax.axis_size("enc")
    perm = []
    for i in range(lax.axis_size("seq") * n_enc):
        s, e = divmod(i, n_enc)
        axis, mask = for_odd if e & 1 else for_even
        perm.append((i, (s ^ mask) * n_enc + e if axis == "seq" else s * n_enc + (e ^ mask)))
    return lax.ppermute(value, ("seq", "enc"), perm)


def near_bits():
    return [("seq", mask) for mask in bits("seq") if mask < lax.axis_size("seq") // 4]


def across_bits():
    return [("enc", mask) for mask in bits("enc")[1:]]


def moved(offset, step):
    return (offset[0] ^ step[1], offset[1]) if step[0] == "seq" else (offset[0], offset[1] ^ step[1])


def slow_flips(value):
    return [flip(value, "seq", o) for o in line_offsets()[1:]]


def plane_steps():
    return list(zip(near_bits() + across_bits(), across_bits() + near_bits()))


def plane_start(stacked):
    return [mixed_flip(stacked, *step) for step in plane_steps()]


def plane_finish(stacked, singles, core):
    found = [((0, 0), (0, 0), stacked)]
    for step, single in zip(plane_steps(), singles):
        fresh = [(moved((0, 0), step[0]), moved((0, 0), step[1]), single)]
        fresh += [
            (moved(o, step[0]), moved(p, step[1]), mixed_flip(v, *step)) for o, p, v in found[1:]
        ]
        found += fresh
    own = [tuple(jnp.where(core == 0, i, k) for i, k in zip(o, p)) for o, p, _ in found]
    other = [tuple(jnp.where(core == 0, k, i) for i, k in zip(o, p)) for o, p, _ in found]
    return own, other, [v for _, _, v in found]


def near_flips(stacked):
    found = [(0, stacked)]
    for _, mask in near_bits():
        found += [(o ^ mask, flip(v, "seq", mask)) for o, v in found]
    return [o for o, _ in found], [v for _, v in found]


def assemble(sources, pieces, places, outs):
    count = len(pieces)
    n_src, n_out = len(sources), len(outs)

    def kernel(*refs):
        table = refs[0]
        given = refs[1 : 1 + n_src]
        results = refs[1 + n_src : 1 + n_src + n_out]
        stage = refs[1 + n_src + n_out : 1 + n_src + n_out + count]
        sem_in, sem_out = refs[-2:]
        copies_in, copies_out = [], []
        for i, (src, block, row, column, rows, columns, out) in enumerate(pieces):
            copies_in.append(
                pltpu.make_async_copy(
                    given[src].at[block, pl.ds(row, rows), pl.ds(column, columns)],
                    stage[i],
                    sem_in.at[i],
                )
            )
            to_row = pl.multiple_of(table[2 * i], rows)
            to_column = pl.multiple_of(table[2 * i + 1], columns)
            copies_out.append(
                pltpu.make_async_copy(
                    stage[i],
                    results[out].at[pl.ds(to_row, rows), pl.ds(to_column, columns)],
                    sem_out.at[i],
                )
            )
        for copy in copies_in:
            copy.start()
        for i in range(count):
            copies_in[i].wait()
            copies_out[i].start()
        for copy in copies_out:
            copy.wait()

    size = sum(p[4] * p[5] * 2 for p in pieces)
    return pl.pallas_call(
        kernel,
        out_shape=[jax.ShapeDtypeStruct(shape, LOW) for shape in outs],
        in_specs=[pl.BlockSpec(memory_space=pltpu.SMEM)]
        + [pl.BlockSpec(memory_space=pl.ANY)] * n_src,
        out_specs=[pl.BlockSpec(memory_space=pl.ANY)] * n_out,
        scratch_shapes=[pltpu.VMEM((p[4], p[5]), LOW) for p in pieces]
        + [pltpu.SemaphoreType.DMA((count,)), pltpu.SemaphoreType.DMA((count,))],
        compiler_params=pltpu.CompilerParams(vmem_limit_bytes=size + 8 * MIB),
        cost_estimate=pl.CostEstimate(flops=0, bytes_accessed=2 * size, transcendentals=0),
    )(places, *sources)


def place_table(places):
    return jnp.stack([jnp.asarray(p, jnp.int32) for p in places])


def assemble_matrix(own, other, mine, partners, layout, outs, seq, enc):
    n_enc = lax.axis_size("enc")
    core = enc & 1
    sources, pieces, places = [], [], []
    for offsets, half, buffers in ((own, core, mine), (other, 1 - core, partners)):
        for (s_off, e_off), v in zip(offsets, buffers):
            for n, o in enumerate(line_offsets()):
                device = (seq ^ s_off ^ o) * n_enc + (enc ^ e_off)
                for row, column, rows, columns, out, to_row, to_column in layout(device >> 1, half):
                    pieces.append((len(sources), n, row, column, rows, columns, out))
                    places += [to_row, to_column]
            sources.append(v)
    return assemble(sources, pieces, place_table(places), outs)


def assemble_strips(offsets, buffers, count, seq):
    rows, width = buffers[0].shape[1], buffers[0].shape[2] // count
    pieces, places = [], []
    for i, s_off in enumerate(offsets):
        for n, o in enumerate(line_offsets()):
            for k in range(count):
                pieces.append((i, n, 0, k * width, rows, width, k))
                places += [(seq ^ s_off ^ o) * rows, 0]
    total = rows * lax.axis_size("seq")
    return assemble(buffers, pieces, place_table(places), [(total, width)] * count)


def dense(left, right):
    return jnp.dot(left, right, preferred_element_type=F32)


def dense_back(left, right):
    return lax.dot_general(left, right, (((1,), (1,)), ((), ())), preferred_element_type=F32)


def inner_rows(left, right):
    return lax.dot_general(left, right, (((0,), (0,)), ((), ())), preferred_element_type=F32)


def layer_norm(values, gain, shift):
    middle = jnp.mean(values, -1, keepdims=True)
    centred = values - middle
    variance = jnp.mean(centred * centred, -1, keepdims=True)
    return centred * lax.rsqrt(variance + EPSILON) * gain + shift


def norm_forward(values, norms, index):
    return jax.vjp(layer_norm, values, norms[0, index], norms[1, index])


def norm_start(values, norms, index):
    middle = jnp.mean(values, -1, keepdims=True)
    centred = values - middle
    hat = centred * lax.rsqrt(jnp.mean(centred * centred, -1, keepdims=True) + EPSILON)
    return hat * norms[0, index] + norms[1, index], hat


def adamw(grad, moment, second, weight, rate, decay):
    moment = BETA_FIRST * moment + (1.0 - BETA_FIRST) * grad
    second = BETA_SECOND * second + (1.0 - BETA_SECOND) * grad * grad
    corrected = moment / (1.0 - BETA_FIRST**STEP)
    scale_two = jnp.sqrt(second / (1.0 - BETA_SECOND**STEP))
    return (
        moment,
        second,
        weight - rate * (corrected / (scale_two + ADAM_EPSILON) + decay * weight),
    )


def scores_of(left, right):
    return lax.dot_general(left, right, (((1,), (1,)), ((), ())), preferred_element_type=F32)


def head_parts(values):
    side = lax.broadcasted_iota(jnp.int32, values.shape, 1) // HEAD_DIM
    count = values.shape[1] // HEAD_DIM
    return [jnp.where(side == h, values, jnp.zeros((), values.dtype)) for h in range(count)]


def head_join(parts):
    side = lax.broadcasted_iota(jnp.int32, (parts[0].shape[0], 128), 1) // HEAD_DIM
    joined = jnp.broadcast_to(parts[0], side.shape)
    for h in range(1, len(parts)):
        joined = jnp.where(side == h, parts[h], joined)
    return joined


def attend_kernel(limit_ref, spot_ref, q_ref, k_ref, v_ref, *rest):
    context_ref, total_ref = rest[-2:]
    queries = head_parts(q_ref[...] * jnp.asarray(0.125, LOW))
    key, value = k_ref[...], v_ref[...]
    allowed = spot_ref[...] < limit_ref[...]
    raw = [scores_of(query, key) for query in queries]
    contexts, totals = [], []
    for scores in raw:
        scores = jnp.where(allowed, scores, MASKED_SCORE)
        highest = jnp.max(scores, -1, keepdims=True)
        exponent = jnp.exp(scores - highest)
        summed = jnp.sum(exponent, -1, keepdims=True)
        contexts.append(jnp.dot(exponent.astype(LOW), value, preferred_element_type=F32) / summed)
        totals.append(highest + jnp.log(summed))
    context_ref[...] = head_join(contexts).astype(LOW)
    total_ref[...] = head_join(totals)


def attend_specs(rows, length, key_at, value_at, count):
    block = pl.BlockSpec((rows, 128), lambda p, j: (j, p))
    return [
        pl.BlockSpec((rows, 1), lambda p, j: (j, 0)),
        pl.BlockSpec((1, length), lambda p, j: (0, 0)),
        block,
        pl.BlockSpec((length, 128), lambda p, j: (0, key_at + p)),
        pl.BlockSpec((length, 128), lambda p, j: (0, value_at + p)),
    ] + [block] * count


def query_rows(length):
    return 512 if length <= 1024 else 256


def attend(query, keys, key_at, value_at, limit, spots, after=()):
    length = query.shape[0]
    width = keys.shape[1] // (2 if key_at == 0 else 3)
    pairs = width // 128
    rows = query_rows(length)
    block = pl.BlockSpec((rows, 128), lambda p, j: (j, p))
    return pl.pallas_call(
        attend_kernel,
        grid=(pairs, length // rows),
        out_shape=[
            jax.ShapeDtypeStruct((length, width), LOW),
            jax.ShapeDtypeStruct((length, width), F32),
        ],
        in_specs=attend_specs(rows, length, key_at, value_at, 0)
        + [pl.BlockSpec(memory_space=pl.ANY)] * len(after),
        out_specs=[block, block],
        compiler_params=pltpu.CompilerParams(vmem_limit_bytes=56 * MIB),
        cost_estimate=pl.CostEstimate(
            flops=8 * length * length * width,
            bytes_accessed=8 * length * width,
            transcendentals=length * length * width // HEAD_DIM,
        ),
    )(limit, spots, query, keys, keys, *after)


def attend_back_kernel(limit_ref, spot_ref, q_ref, k_ref, v_ref, grad_ref, total_ref, *rest):
    out_ref, dk_sum, dv_sum = rest[-3:]
    pair, step = pl.program_id(0), pl.program_id(1)
    pairs, steps = pl.num_programs(0), pl.num_programs(1)
    rows = q_ref.shape[0]

    @pl.when(step == 0)
    def _():
        dk_sum[...] = jnp.zeros_like(dk_sum)
        dv_sum[...] = jnp.zeros_like(dv_sum)

    queries = head_parts(q_ref[...] * jnp.asarray(0.125, LOW))
    grads = head_parts(grad_ref[...])
    key, value, totals = k_ref[...], v_ref[...], total_ref[...]
    allowed = spot_ref[...] < limit_ref[...]
    raw = [scores_of(query, key) for query in queries]
    grad_softs = [scores_of(grad, value) for grad in grads]
    grad_scores, soft_lows = [], []
    for h, (scores, grad_soft) in enumerate(zip(raw, grad_softs)):
        scores = jnp.where(allowed, scores, MASKED_SCORE)
        soft = jnp.exp(scores - totals[:, h * HEAD_DIM : h * HEAD_DIM + 1])
        weighted = jnp.sum(soft * grad_soft, -1, keepdims=True)
        grad_scores.append((soft * (grad_soft - weighted)).astype(LOW))
        soft_lows.append(soft.astype(LOW))
    dk_sum[...] += inner_rows(jnp.concatenate(grad_scores, 0), jnp.concatenate(queries, 0))
    dv_sum[...] += inner_rows(jnp.concatenate(soft_lows, 0), jnp.concatenate(grads, 0))
    grad_query = head_join([jnp.dot(g, key, preferred_element_type=F32) for g in grad_scores])
    column = pl.multiple_of(pair * 128, 128)
    out_ref[pl.ds(pl.multiple_of(step * rows, rows), rows), pl.ds(column, 128)] = (
        grad_query * 0.125
    ).astype(LOW)

    @pl.when(step == steps - 1)
    def _():
        out_ref[:, pl.ds(pl.multiple_of((pairs + pair) * 128, 128), 128)] = dk_sum[...].astype(LOW)
        out_ref[:, pl.ds(pl.multiple_of((2 * pairs + pair) * 128, 128), 128)] = dv_sum[...].astype(
            LOW
        )


def attend_back(query, keys, key_at, value_at, limit, spots, grads, totals, after=()):
    length, width = grads.shape
    pairs = width // 128
    rows = query_rows(length)
    return pl.pallas_call(
        attend_back_kernel,
        grid=(pairs, length // rows),
        out_shape=jax.ShapeDtypeStruct((length, 3 * width), LOW),
        in_specs=attend_specs(rows, length, key_at, value_at, 2)
        + [pl.BlockSpec(memory_space=pl.ANY)] * len(after),
        out_specs=pl.BlockSpec((length, 3 * width), lambda p, j: (0, 0)),
        scratch_shapes=[pltpu.VMEM((length, 128), F32), pltpu.VMEM((length, 128), F32)],
        compiler_params=pltpu.CompilerParams(vmem_limit_bytes=60 * MIB),
        cost_estimate=pl.CostEstimate(
            flops=20 * length * length * width,
            bytes_accessed=16 * length * width,
            transcendentals=length * length * width // HEAD_DIM,
        ),
    )(limit, spots, query, keys, keys, grads, totals, *after)


def gelu_both(values):
    below = 0.5 * (1.0 + lax.erf(values * 0.7071067811865476))
    bell = jnp.exp(values * values * -0.5) * 0.3989422804014327
    return values * below, below + values * bell


def pack_feed(expand, reduce, down, up):
    rows, width = expand.shape[0], reduce.shape[1]
    parts = [expand[:, q * width : (q + 1) * width] for q in range(4)]
    return jnp.concatenate(
        parts + [reduce, jnp.concatenate([down[: rows // 2], down[rows // 2 :]], 1), up], 0
    )


def gather_feed(expand, reduce, down, up):
    everyone = ("seq", "enc")
    if expand.shape[0] % 32 == 0:
        return lax.all_gather(pack_feed(expand, reduce, down, up), everyone)
    whole = [lax.all_gather(v, everyone, axis=0, tiled=True) for v in (expand, reduce, down, up)]
    return pack_feed(*whole)[None]


def feed_specs(packed, tile):
    count, depth, width = packed.shape
    rows = depth // 9
    per = width // tile
    if 4 * rows <= tile:
        reduce = pl.BlockSpec((tile // (4 * rows), 4 * rows, width), lambda j: (j, 1, 0))
    else:
        first = 4 * rows // tile
        reduce = pl.BlockSpec((1, tile, width), lambda j: (0, first + j, 0))
    return [
        pl.BlockSpec((count, rows, tile), lambda j: (0, j // per, j % per)),
        reduce,
        pl.BlockSpec((count, rows, width), lambda j: (0, 8, 0)),
    ]


def flat(block):
    return block.reshape(block.shape[0] * block.shape[1], block.shape[2])


def adapter_parts(block):
    count, rows, width = block.shape
    half = rows // 2
    down = jnp.stack([block[:, :half, : width // 2], block[:, :half, width // 2 :]], 1)
    return down.reshape(count * rows, width // 2), flat(block[:, half:])


def branch_kernel(
    x_ref, in_ref, out_ref, small_ref, y_ref, slope_ref, act_ref, bend_ref, total
):
    step = pl.program_id(0)

    @pl.when(step == 0)
    def _():
        down, up = adapter_parts(small_ref[...])
        act, slope = gelu_both(jnp.dot(x_ref[...], down, preferred_element_type=F32))
        act = act.astype(LOW)
        act_ref[...] = act
        bend_ref[...] = slope
        total[...] = ADAPTER_SCALE * jnp.dot(act, up, preferred_element_type=F32)

    part = 256
    x = x_ref[...]
    expand, reduce = flat(in_ref[...]), flat(out_ref[...])
    tile = expand.shape[1]
    pre = jnp.dot(x, expand[:, :part], preferred_element_type=F32)
    for start in range(0, tile, part):
        now = pre
        if start + part < tile:
            pre = jnp.dot(x, expand[:, start + part : start + 2 * part], preferred_element_type=F32)
        act, slope = gelu_both(now)
        slope_ref[:, start : start + part] = slope
        total[...] += jnp.dot(
            act.astype(LOW), reduce[start : start + part], preferred_element_type=F32
        )

    @pl.when(step == pl.num_programs(0) - 1)
    def _():
        y_ref[...] = total[...]


def branch(rows_low, packed, tile=1024):
    rows, width = rows_low.shape
    hidden, small = 4 * width, width // 2
    return pl.pallas_call(
        branch_kernel,
        grid=(hidden // tile,),
        out_shape=[
            jax.ShapeDtypeStruct((rows, width), F32),
            jax.ShapeDtypeStruct((rows, hidden), F32),
            jax.ShapeDtypeStruct((rows, small), LOW),
            jax.ShapeDtypeStruct((rows, small), F32),
        ],
        in_specs=[pl.BlockSpec((rows, width), lambda j: (0, 0))] + feed_specs(packed, tile),
        out_specs=[
            pl.BlockSpec((rows, width), lambda j: (0, 0)),
            pl.BlockSpec((rows, tile), lambda j: (0, j)),
            pl.BlockSpec((rows, small), lambda j: (0, 0)),
            pl.BlockSpec((rows, small), lambda j: (0, 0)),
        ],
        scratch_shapes=[pltpu.VMEM((rows, width), F32)],
        compiler_params=pltpu.CompilerParams(vmem_limit_bytes=56 * MIB),
        cost_estimate=pl.CostEstimate(
            flops=4 * rows * width * (hidden + small),
            bytes_accessed=4 * width * (hidden + small) + 4 * rows * hidden,
            transcendentals=2 * rows * hidden,
        ),
    )(rows_low, packed, packed, packed)


def branch_back_kernel(
    g_ref, ga_ref, in_ref, out_ref, small_ref, slope_ref, bend_ref, dx_ref, dpre_ref, total
):
    step = pl.program_id(0)

    @pl.when(step == 0)
    def _():
        down, up = adapter_parts(small_ref[...])
        grad = dense_back(ga_ref[...], up)
        pre = (grad * bend_ref[...]).astype(LOW)
        dpre_ref[...] = pre
        total[...] = dense_back(pre, down)

    part = 256
    g = g_ref[...]
    expand, reduce = flat(in_ref[...]), flat(out_ref[...])
    tile = expand.shape[1]
    grad = dense_back(g, reduce[:part])
    for start in range(0, tile, part):
        now = grad
        if start + part < tile:
            grad = dense_back(g, reduce[start + part : start + 2 * part])
        pre = (now * slope_ref[:, start : start + part]).astype(LOW)
        total[...] += dense_back(pre, expand[:, start : start + part])

    @pl.when(step == pl.num_programs(0) - 1)
    def _():
        dx_ref[...] = total[...]


def branch_back(grad_out, kept, packed, tile=1024):
    rows_low, slope, act, bend = kept
    rows, width = rows_low.shape
    hidden, small = 4 * width, width // 2
    grad_low = grad_out.astype(LOW)
    grad_adapter = (ADAPTER_SCALE * grad_out).astype(LOW)
    whole = pl.BlockSpec((rows, width), lambda j: (0, 0))
    narrow = pl.BlockSpec((rows, small), lambda j: (0, 0))
    grad_rows, grad_pre = pl.pallas_call(
        branch_back_kernel,
        grid=(hidden // tile,),
        out_shape=[
            jax.ShapeDtypeStruct((rows, width), F32),
            jax.ShapeDtypeStruct((rows, small), LOW),
        ],
        in_specs=[whole, whole]
        + feed_specs(packed, tile)
        + [pl.BlockSpec((rows, tile), lambda j: (0, j)), narrow],
        out_specs=[whole, narrow],
        scratch_shapes=[pltpu.VMEM((rows, width), F32)],
        compiler_params=pltpu.CompilerParams(vmem_limit_bytes=56 * MIB),
        cost_estimate=pl.CostEstimate(
            flops=4 * rows * width * (hidden + small),
            bytes_accessed=4 * width * (hidden + small) + 4 * rows * hidden,
            transcendentals=0,
        ),
    )(grad_low, grad_adapter, packed, packed, packed, slope, bend)
    return grad_rows, inner_rows(rows_low, grad_pre), inner_rows(act, grad_adapter)


def head_kernel(o_ref, e_ref, g_ref, lse_ref, acc, peak, mass):
    step = pl.program_id(0)
    part = 512

    @pl.when(step == 0)
    def _():
        acc[...] = jnp.zeros_like(acc)
        peak[...] = jnp.full_like(peak, -1e30)
        mass[...] = jnp.zeros_like(mass)

    table = e_ref[...]
    starts = list(range(0, o_ref.shape[0], part))
    spans = [pl.ds(start, part) for start in starts]
    before = [peak[at, :1] for at in spans]
    held = [mass[at, :] for at in spans]
    coming = scores_of(o_ref[spans[0], :], table)
    highest, summed = [], []
    for h, at in enumerate(spans):
        logits = coming
        if h + 1 < len(spans):
            coming = scores_of(o_ref[spans[h + 1], :], table)
        highest.append(jnp.maximum(before[h], jnp.max(logits, -1, keepdims=True)))
        exponent = jnp.exp(logits - highest[h])
        fade = jnp.exp(before[h] - highest[h])
        summed.append(held[h] * fade + jnp.sum(exponent, -1, keepdims=True))
        acc[at, :] = acc[at, :] * fade + jnp.dot(
            exponent.astype(LOW), table, preferred_element_type=F32
        )
    for h, at in enumerate(spans):
        mass[at, :] = summed[h]
        peak[at, :] = jnp.broadcast_to(highest[h], (part, 128))

    @pl.when(step == pl.num_programs(0) - 1)
    def _():
        g_ref[...] = (acc[...] / mass[:, :1]).astype(LOW)
        lse_ref[...] = peak[...] + jnp.log(mass[...])


def head(rows_low, table):
    rows, width = rows_low.shape
    entries = table.shape[0]
    tile = next(t for t in (1280, 1024, 640, 512, 256, 128) if entries % t == 0)
    return pl.pallas_call(
        head_kernel,
        grid=(entries // tile,),
        out_shape=[
            jax.ShapeDtypeStruct((rows, width), LOW),
            jax.ShapeDtypeStruct((rows, 128), F32),
        ],
        in_specs=[
            pl.BlockSpec((rows, width), lambda j: (0, 0)),
            pl.BlockSpec((tile, width), lambda j: (j, 0)),
        ],
        out_specs=[
            pl.BlockSpec((rows, width), lambda j: (0, 0)),
            pl.BlockSpec((rows, 128), lambda j: (0, 0)),
        ],
        scratch_shapes=[
            pltpu.VMEM((rows, width), F32),
            pltpu.VMEM((rows, 128), F32),
            pltpu.VMEM((rows, 128), F32),
        ],
        compiler_params=pltpu.CompilerParams(vmem_limit_bytes=56 * MIB),
        cost_estimate=pl.CostEstimate(
            flops=4 * rows * width * entries,
            bytes_accessed=2 * width * entries,
            transcendentals=rows * entries,
        ),
    )(rows_low, table)


def reduce_adapters(grad_down, grad_up, seq, enc):
    n_seq, n_enc = lax.axis_size("seq"), lax.axis_size("enc")
    near = n_seq // 4
    width, small = grad_down.shape
    rows = width // (n_seq * n_enc)
    folded = grad_down.reshape(-1, 2, rows // 2, small).transpose(0, 2, 1, 3)
    folded = folded.reshape(-1, rows // 2, 2 * small)
    both = jnp.concatenate([folded, grad_up.reshape(-1, rows // 2, width)], 1)
    both = both.reshape(4, near, n_enc // 2, 2, rows, width)
    first = (enc & 1) == 0
    low, high = both[:, :, :, 0], both[:, :, :, 1]
    held = jnp.where(first, low, high) + flip(jnp.where(first, high, low), "enc", 1)

    def block(s_off, e_off):
        start = (0, (seq & (near - 1)) ^ s_off, (enc >> 1) ^ (e_off >> 1), 0, 0)
        return lax.dynamic_slice(held, start, (4, 1, 1, rows, width))[:, 0, 0]

    parts = [block(0, 0)] + [
        flip_both(block(s, e).astype(LOW), s, e).astype(F32) for s, e in plane_offsets()[1:]
    ]
    held = tree_sum(parts)
    slow = seq // near
    parts = [lax.dynamic_index_in_dim(held, slow ^ k, 0, keepdims=False) for k in range(4)]
    held = tree_sum(
        parts[:1]
        + [flip(p.astype(LOW), "seq", o).astype(F32) for p, o in zip(parts[1:], line_offsets()[1:])]
    )
    down = held[: rows // 2].reshape(rows // 2, 2, small).transpose(1, 0, 2)
    return down.reshape(rows, small), held[rows // 2 :]


def sum_everywhere(values):
    values = values + flip(values, "enc", 1)
    values = tree_sum([values] + [flip_both(values, s, e) for s, e in plane_offsets()[1:]])
    return tree_sum([values] + [flip(values, "seq", o) for o in line_offsets()[1:]])


def shards(
    source_ids,
    target_ids,
    labels,
    lengths,
    embedding,
    positions,
    attention_in,
    attention_out,
    feed_in,
    feed_out,
    adapter_down,
    adapter_up,
    norm_params,
    down_moment,
    down_second,
    up_moment,
    up_second,
    norm_moment,
    norm_second,
):
    n_seq, n_enc = lax.axis_size("seq"), lax.axis_size("enc")
    n_all = n_seq * n_enc
    seq, enc = lax.axis_index("seq"), lax.axis_index("enc")
    core = enc & 1
    own_rows = source_ids.shape[1]
    width = embedding.shape[1]
    entries = embedding.shape[0]
    length = own_rows * n_enc
    share = width // n_enc
    source_length, target_length = lengths[0, 0], lengths[0, 1]

    blocks = jnp.arange(n_enc) ^ enc
    spots = (blocks[:, None] * own_rows + jnp.arange(own_rows)[None, :]).reshape(length)
    spots = spots.astype(jnp.int32)
    source_limit = jnp.broadcast_to(source_length, (length, 1)).astype(jnp.int32)
    causal_limit = jnp.minimum(spots + 1, target_length)[:, None].astype(jnp.int32)
    spots = spots[None, :]
    in_strip = share // 128

    def gather_rows(rows_low):
        return jnp.concatenate(gather_enc(rows_low), 0)

    def lookup(ids):
        inside = (ids >= 0) & (ids < entries)
        found = jnp.take(embedding, jnp.clip(ids, 0, entries - 1), axis=0)
        return jnp.where(inside[:, :, None], found, jnp.zeros((), LOW))

    def rows_of(found):
        return scatter_enc([found[j] for j in range(n_enc)])

    def finish_attention(context, k):
        parts = swap_blocks([context[j * own_rows : (j + 1) * own_rows] for j in range(n_enc)])
        return dense(jnp.concatenate(parts, 1), attend_out[k])

    def begin_attention_back(grad, k):
        spread = dense_back(grad.astype(LOW), attend_out[k]).astype(LOW)
        parts = swap_blocks([spread[:, j * share : (j + 1) * share] for j in range(n_enc)])
        return jnp.concatenate(parts, 0)

    def scatter_rows(partial):
        return scatter_enc([partial[j * own_rows : (j + 1) * own_rows] for j in range(n_enc)])

    def start_grads(grads, k, grad_res, hat, hats):
        partial = dense_back(grads, attend_in[k])
        gain = jnp.sum(partial * hats.astype(F32), 0) + jnp.sum(grad_res * hat, 0)
        return gain, jnp.sum(partial, 0) + jnp.sum(grad_res, 0)

    down_low, up_low = adapter_down.astype(LOW), adapter_up.astype(LOW)
    feeds = [gather_feed(feed_in[k], feed_out[k], down_low[k], up_low[k]) for k in range(2)]

    gains = norm_params.astype(LOW).astype(F32)
    ids = jnp.concatenate([source_ids, target_ids, labels], 0).astype(F32)
    small_own = jnp.concatenate([ids.reshape(1, -1), gains.reshape(1, -1)], 1)
    small_all = unxor([v[0] for v in jnp.split(lax.all_gather(small_own, "enc"), n_enc)], enc)
    small_all = jnp.concatenate(small_all, 0)
    all_ids = small_all[:, : 3 * own_rows].astype(jnp.int32).reshape(n_enc, 3, own_rows)
    all_ids = all_ids - enc * entries
    gains = small_all[:, 3 * own_rows :].astype(LOW)[None]

    triple = attention_in.reshape(3, -1, 3, n_enc, share).transpose(3, 1, 0, 2, 4)
    shard_rows = triple.shape[1]
    strip_rows, pair_rows = n_enc * shard_rows, 2 * shard_rows
    triple = triple.reshape(n_enc, shard_rows, 9 * share)
    strip = lax.all_to_all(triple, "enc", 0, 0, tiled=True).reshape(strip_rows, 9 * share)
    strip, late = strip[:, : 6 * share], strip[:, 6 * share :]
    half = width // 2
    packed = jnp.concatenate(
        [attention_out[k][:, h * half : (h + 1) * half] for h in range(2) for k in range(3)], 1
    )
    pair_out = pair_split(packed, core)

    ids = [all_ids[:, k] for k in range(3)]

    slow = slow_flips(strip)
    for mask in bits("seq"):
        gains = jnp.concatenate([gains, flip(gains, "seq", mask)], 0)
    found = [lookup(ids[0]), lookup(ids[1])]
    pair_out, *slow = gate([pair_out] + slow)
    order_seq, order_enc = jnp.arange(n_seq) ^ seq, jnp.arange(n_enc) ^ enc
    gains = jnp.take(jnp.take(gains, order_seq, axis=0), order_enc, axis=1)
    gains = gains.reshape(n_all, 14, width // n_all).transpose(1, 0, 2)
    norms = gains.reshape(2, 7, width).astype(F32)

    strip_offsets, strips = near_flips(jnp.stack([strip] + slow))
    source_rows, target_rows = rows_of(found[0]), rows_of(found[1])
    slow = slow_flips(pair_out)
    found = lookup(ids[2])
    late, *slow = gate([late] + slow)

    in_enc, in_dec = assemble_strips(strip_offsets, strips, 2, seq)
    encoder_in, encoder_hat = norm_start(source_rows + positions[0].astype(F32), norms, 0)
    decoder_in, decoder_hat = norm_start(target_rows + positions[1].astype(F32), norms, 3)
    encoder_all = gather_rows(encoder_in.astype(LOW))
    decoder_all = gather_rows(decoder_in.astype(LOW))
    stacked = jnp.stack([pair_out] + slow)
    singles = plane_start(stacked)

    own, other, mine = plane_finish(stacked, singles, core)
    partners = [flip(v, "enc", 1) for v in mine]
    slow = slow_flips(late)
    triple_encoder = dense(encoder_all, in_enc).astype(LOW)
    enc_args = (triple_encoder, triple_encoder, in_strip, 2 * in_strip, source_limit, spots)
    context_enc, total_encoder = attend(*enc_args)
    triple_decoder = dense(decoder_all, in_dec).astype(LOW)
    dec_args = (triple_decoder, triple_decoder, in_strip, 2 * in_strip, causal_limit, spots)
    context_dec, total_decoder = attend(*dec_args)

    def out_layout(pair, side):
        row = pair * pair_rows
        block = (row // share) ^ enc
        return [
            (0, k * half, pair_rows, half, k, block * share + row % share, side * half)
            for k in range(3)
        ]

    attend_out = assemble_matrix(
        own, other, mine, partners, out_layout, [(width, width)] * 3, seq, enc
    )
    late_offsets, strips = near_flips(jnp.stack([late] + slow))
    after_self, pull_one = norm_forward(encoder_in + finish_attention(context_enc, 0), norms, 1)
    after_causal, pull_four = norm_forward(decoder_in + finish_attention(context_dec, 1), norms, 4)
    label_rows = rows_of(found)

    in_cross = assemble_strips(late_offsets, strips, 1, seq)[0]
    attend_in = [in_enc, in_dec, in_cross]
    causal_all = gather_rows(after_causal.astype(LOW))
    after_self_low = after_self.astype(LOW)
    branched, *kept_enc = branch(after_self_low, feeds[0])
    encoded, pull_two = norm_forward(after_self + branched, norms, 2)
    encoded_low = encoded.astype(LOW)
    query_cross = dense(causal_all, in_cross[:, :share]).astype(LOW)

    encoded_all = gather_rows(encoded_low)
    pairs_cross = dense(encoded_all, in_cross[:, share:]).astype(LOW)
    cross_args = (query_cross, pairs_cross, 0, in_strip, source_limit, spots)
    context, total_cross = attend(*cross_args)
    after_cross, pull_five = norm_forward(after_causal + finish_attention(context, 2), norms, 5)
    after_cross_low = after_cross.astype(LOW)
    branched, *kept_dec = branch(after_cross_low, feeds[1])
    decoded, pull_six = norm_forward(after_cross + branched, norms, 6)
    decoded_low = decoded.astype(LOW)

    decoded_all, encoder_hat, decoder_hat = gate(
        [gather_rows(decoded_low), encoder_hat, decoder_hat]
    )
    pulled, totals = head(decoded_all, embedding)
    encoder_hats = gather_rows(encoder_hat.astype(LOW))
    decoder_hats = gather_rows(decoder_hat.astype(LOW))
    parts = [slice(j * own_rows, (j + 1) * own_rows) for j in range(n_enc)]
    pulled, log_total = merge_enc([pulled[p] for p in parts], [totals[p, :1] for p in parts])
    row_spots = enc * own_rows + jnp.arange(own_rows)
    valid = (row_spots < target_length).astype(F32)[:, None]
    picked = jnp.sum(decoded_low.astype(F32) * label_rows, -1, keepdims=True)
    loss_own = jnp.sum((log_total - picked) * valid)
    grad_decoded = (pulled - label_rows) * valid

    grad_res, gain_six, shift_six = pull_six(grad_decoded)
    grad_rows, down_dec, up_dec = branch_back(
        grad_res, [after_cross_low] + kept_dec, feeds[1]
    )
    grad_res, gain_five, shift_five = pull_five(grad_res + grad_rows)
    grads = attend_back(*cross_args, begin_attention_back(grad_res, 2), total_cross)
    grad_encoded = scatter_rows(dense_back(grads[:, share:], attend_in[2][:, share:]))
    grad_causal = grad_res + scatter_rows(dense_back(grads[:, :share], attend_in[2][:, :share]))
    grad_res, gain_four, shift_four = pull_four(grad_causal)
    grads = attend_back(*dec_args, begin_attention_back(grad_res, 1), total_decoder)
    gain_three, shift_three = start_grads(grads, 1, grad_res, decoder_hat, decoder_hats)
    grad_res, gain_two, shift_two = pull_two(grad_encoded)
    grad_rows, down_enc, up_enc = branch_back(
        grad_res, [after_self_low] + kept_enc, feeds[0]
    )
    grad_res, gain_one, shift_one = pull_one(grad_res + grad_rows)
    owned_dec = reduce_adapters(down_dec, up_dec, seq, enc)
    owned_enc = reduce_adapters(down_enc, up_enc, seq, enc)
    grads = attend_back(*enc_args, begin_attention_back(grad_res, 0), total_encoder, after=owned_dec)
    gain_zero, shift_zero = start_grads(grads, 0, grad_res, encoder_hat, encoder_hats)

    grad_down = jnp.stack([owned_enc[0], owned_dec[0]])
    grad_up = jnp.stack([owned_enc[1], owned_dec[1]])
    count_own = jnp.clip(target_length - enc * own_rows, 0, own_rows).astype(F32)
    squares_own = jnp.sum(grad_down * grad_down) + jnp.sum(grad_up * grad_up)
    lanes = jnp.arange(width)
    scalars = jnp.where(
        lanes == 0, loss_own, jnp.where(lanes == 1, count_own, jnp.where(lanes == 2, squares_own, 0.0))
    )
    summed = jnp.stack(
        [gain_zero, gain_one, gain_two, gain_three, gain_four, gain_five, gain_six]
        + [shift_zero, shift_one, shift_two, shift_three, shift_four, shift_five, shift_six]
        + [scalars, jnp.zeros_like(scalars)]
    )
    summed = sum_everywhere(summed)
    loss_sum, token_total = summed[14, 0], summed[14, 1]
    norm_grads = summed[:14]
    squares = summed[14, 2] + jnp.sum(norm_grads * norm_grads)
    per = width // n_all
    grad_norms = lax.dynamic_slice_in_dim(norm_grads, (seq * n_enc + enc) * per, per, 1)
    grad_norms = grad_norms.reshape(2, 7, per)

    grad_norm = jnp.sqrt(squares) / token_total
    factor = jnp.minimum(1.0, CLIP_NORM / grad_norm) / token_total
    moment_down, second_down, updated_down = adamw(
        grad_down * factor, down_moment, down_second, adapter_down, RATE_ADAPTER, DECAY_ADAPTER
    )
    moment_up, second_up, updated_up = adamw(
        grad_up * factor, up_moment, up_second, adapter_up, RATE_ADAPTER, DECAY_ADAPTER
    )
    moment_norms, second_norms, updated_norms = adamw(
        grad_norms * factor, norm_moment, norm_second, norm_params, RATE_NORMS, 0.0
    )
    return (
        loss_sum,
        token_total,
        grad_norm,
        moment_down,
        second_down,
        updated_down,
        moment_up,
        second_up,
        updated_up,
        moment_norms,
        second_norms,
        updated_norms,
    )


def solution(mesh):
    everywhere = P(None, ("seq", "enc"), None)
    columns = P(None, None, ("seq", "enc"))
    return jax.shard_map(
        shards,
        mesh=mesh,
        in_specs=(
            P("seq", "enc"),
            P("seq", "enc"),
            P("seq", "enc"),
            P("seq", None),
            P("enc", None),
            P(None, "enc", None),
            everywhere,
            everywhere,
            everywhere,
            everywhere,
            everywhere,
            everywhere,
            columns,
            everywhere,
            everywhere,
            everywhere,
            everywhere,
            columns,
            columns,
        ),
        out_specs=(
            P(),
            P(),
            P(),
            everywhere,
            everywhere,
            everywhere,
            everywhere,
            everywhere,
            everywhere,
            columns,
            columns,
            columns,
        ),
        check_vma=False,
    )
```

```python
import jax
import jax.numpy as jnp
from jax import lax
from jax.experimental import pallas as pl
from jax.experimental.pallas import tpu as pltpu
from jax.sharding import PartitionSpec as P

HEAD_DIM = 64
STEP = 10

EPSILON = 1e-05
ADAPTER_SCALE = 4.0
CLIP_NORM = 0.25
RATE_ADAPTER = 0.05
RATE_NORMS = 0.5
BETA_FIRST = 0.9
BETA_SECOND = 0.999
ADAM_EPSILON = 1e-08
DECAY_ADAPTER = 0.01
MASKED_SCORE = -1000000000.0

LOW = jnp.bfloat16
F32 = jnp.float32
MIB = 1024 * 1024


def flip(value, axis, mask):
    count = lax.axis_size(axis)
    return lax.ppermute(value, axis, [(i, i ^ mask) for i in range(count)])


def bits(axis):
    count = lax.axis_size(axis)
    return [1 << i for i in range(count.bit_length() - 1)]


def unxor(blocks, me):
    blocks = list(blocks)
    mask = 1
    while mask < len(blocks):
        bit = (me & mask) != 0
        blocks = [jnp.where(bit, blocks[i ^ mask], blocks[i]) for i in range(len(blocks))]
        mask *= 2
    return blocks


def gather_across(value):
    found = {0: value}
    for mask in bits("enc")[1:]:
        found.update({j | mask: flip(v, "enc", mask) for j, v in list(found.items())})
    return [found[j] for j in sorted(found)]


def gather_pair(blocks):
    return [v for block in blocks for v in (block, flip(block, "enc", 1))]


def gather_enc(value):
    return gather_pair(gather_across(value))


def scatter_two(blocks):
    held = dict(enumerate(blocks))
    for mask in bits("enc"):
        away = [j for j in held if j & mask]
        sent = [flip(held[j].astype(LOW), "enc", mask) for j in away]
        for j, part in zip(away, sent):
            if len(held) == 2:
                return held[j ^ mask], part
            held[j ^ mask] = held[j ^ mask].astype(F32) + part.astype(F32)
            del held[j]


def scatter_enc(blocks):
    own, came = scatter_two(blocks)
    return own.astype(F32) + came.astype(F32)


def merge_means(first, second):
    (mean, total), (other, other_total) = first, second
    highest = jnp.maximum(total, other_total)
    own, far = jnp.exp(total - highest), jnp.exp(other_total - highest)
    both = own + far
    return (mean.astype(F32) * own + other.astype(F32) * far) / both, highest + jnp.log(both)


def merge_enc(blocks, totals):
    held = {j: (b, t) for j, (b, t) in enumerate(zip(blocks, totals))}
    for mask in bits("enc"):
        away = [j for j in held if j & mask]
        sent = [(flip(held[j][0].astype(LOW), "enc", mask), flip(held[j][1], "enc", mask)) for j in away]
        for j, came in zip(away, sent):
            if len(held) == 2:
                return held[j ^ mask], came
            held[j ^ mask] = merge_means(held[j ^ mask], came)
            del held[j]


def swap_blocks(blocks):
    return [blocks[0]] + [flip(blocks[j], "enc", j) for j in range(1, len(blocks))]


def pair_split(shard, core):
    half = shard.shape[1] // 2
    first = core == 0
    low, high = shard[:, :half], shard[:, half:]
    keep = jnp.where(first, low, high)
    came = flip(jnp.where(first, high, low), "enc", 1)
    return jnp.concatenate([jnp.where(first, keep, came), jnp.where(first, came, keep)], 0)


def gate(arrays):
    def kernel(*refs):
        pass

    return pl.pallas_call(
        kernel,
        out_shape=[jax.ShapeDtypeStruct(v.shape, v.dtype) for v in arrays],
        in_specs=[pl.BlockSpec(memory_space=pl.ANY)] * len(arrays),
        out_specs=[pl.BlockSpec(memory_space=pl.ANY)] * len(arrays),
        input_output_aliases={i: i for i in range(len(arrays))},
        cost_estimate=pl.CostEstimate(flops=0, bytes_accessed=0, transcendentals=0),
    )(*arrays)


def flip_both(value, seq_mask, enc_mask):
    n_enc = lax.axis_size("enc")
    perm = []
    for i in range(lax.axis_size("seq") * n_enc):
        s, e = divmod(i, n_enc)
        perm.append((i, (s ^ seq_mask) * n_enc + (e ^ enc_mask)))
    return lax.ppermute(value, ("seq", "enc"), perm)


def tree_sum(values):
    values = list(values)
    while len(values) > 1:
        values = [values[i] + values[i + 1] for i in range(0, len(values), 2)]
    return values[0]


def plane_offsets():
    near = lax.axis_size("seq") // 4
    return [(s, e) for e in range(0, lax.axis_size("enc"), 2) for s in range(near)]


def line_offsets():
    return [k * (lax.axis_size("seq") // 4) for k in range(4)]


def mixed_flip(value, for_even, for_odd):
    n_enc = lax.axis_size("enc")
    perm = []
    for i in range(lax.axis_size("seq") * n_enc):
        s, e = divmod(i, n_enc)
        axis, mask = for_odd if e & 1 else for_even
        perm.append((i, (s ^ mask) * n_enc + e if axis == "seq" else s * n_enc + (e ^ mask)))
    return lax.ppermute(value, ("seq", "enc"), perm)


def near_bits():
    return [("seq", mask) for mask in bits("seq") if mask < lax.axis_size("seq") // 4]


def across_bits():
    return [("enc", mask) for mask in bits("enc")[1:]]


def moved(offset, step):
    return (offset[0] ^ step[1], offset[1]) if step[0] == "seq" else (offset[0], offset[1] ^ step[1])


def slow_flips(value):
    return [flip(value, "seq", o) for o in line_offsets()[1:]]


def plane_steps():
    return list(zip(near_bits() + across_bits(), across_bits() + near_bits()))


def plane_start(stacked):
    return [mixed_flip(stacked, *step) for step in plane_steps()]


def plane_finish(stacked, singles, core):
    found = [((0, 0), (0, 0), stacked)]
    for step, single in zip(plane_steps(), singles):
        fresh = [(moved((0, 0), step[0]), moved((0, 0), step[1]), single)]
        fresh += [
            (moved(o, step[0]), moved(p, step[1]), mixed_flip(v, *step)) for o, p, v in found[1:]
        ]
        found += fresh
    own = [tuple(jnp.where(core == 0, i, k) for i, k in zip(o, p)) for o, p, _ in found]
    other = [tuple(jnp.where(core == 0, k, i) for i, k in zip(o, p)) for o, p, _ in found]
    return own, other, [v for _, _, v in found]


def near_flips(stacked):
    found = [(0, stacked)]
    for _, mask in near_bits():
        found += [(o ^ mask, flip(v, "seq", mask)) for o, v in found]
    return [o for o, _ in found], [v for _, v in found]


def assemble(sources, pieces, places, outs):
    count = len(pieces)
    n_src, n_out = len(sources), len(outs)

    def kernel(*refs):
        table = refs[0]
        given = refs[1 : 1 + n_src]
        results = refs[1 + n_src : 1 + n_src + n_out]
        stage = refs[1 + n_src + n_out : 1 + n_src + n_out + count]
        sem_in, sem_out = refs[-2:]
        copies_in, copies_out = [], []
        for i, (src, block, row, column, rows, columns, out) in enumerate(pieces):
            copies_in.append(
                pltpu.make_async_copy(
                    given[src].at[block, pl.ds(row, rows), pl.ds(column, columns)],
                    stage[i],
                    sem_in.at[i],
                )
            )
            to_row = pl.multiple_of(table[2 * i], rows)
            to_column = pl.multiple_of(table[2 * i + 1], columns)
            copies_out.append(
                pltpu.make_async_copy(
                    stage[i],
                    results[out].at[pl.ds(to_row, rows), pl.ds(to_column, columns)],
                    sem_out.at[i],
                )
            )
        for copy in copies_in:
            copy.start()
        for i in range(count):
            copies_in[i].wait()
            copies_out[i].start()
        for copy in copies_out:
            copy.wait()

    size = sum(p[4] * p[5] * 2 for p in pieces)
    return pl.pallas_call(
        kernel,
        out_shape=[jax.ShapeDtypeStruct(shape, LOW) for shape in outs],
        in_specs=[pl.BlockSpec(memory_space=pltpu.SMEM)]
        + [pl.BlockSpec(memory_space=pl.ANY)] * n_src,
        out_specs=[pl.BlockSpec(memory_space=pl.ANY)] * n_out,
        scratch_shapes=[pltpu.VMEM((p[4], p[5]), LOW) for p in pieces]
        + [pltpu.SemaphoreType.DMA((count,)), pltpu.SemaphoreType.DMA((count,))],
        compiler_params=pltpu.CompilerParams(vmem_limit_bytes=size + 8 * MIB),
        cost_estimate=pl.CostEstimate(flops=0, bytes_accessed=2 * size, transcendentals=0),
    )(places, *sources)


def place_table(places):
    return jnp.stack([jnp.asarray(p, jnp.int32) for p in places])


def assemble_matrix(own, other, mine, partners, layout, outs, seq, enc):
    n_enc = lax.axis_size("enc")
    core = enc & 1
    sources, pieces, places = [], [], []
    for offsets, half, buffers in ((own, core, mine), (other, 1 - core, partners)):
        for (s_off, e_off), v in zip(offsets, buffers):
            for n, o in enumerate(line_offsets()):
                device = (seq ^ s_off ^ o) * n_enc + (enc ^ e_off)
                for row, column, rows, columns, out, to_row, to_column in layout(device >> 1, half):
                    pieces.append((len(sources), n, row, column, rows, columns, out))
                    places += [to_row, to_column]
            sources.append(v)
    return assemble(sources, pieces, place_table(places), outs)


def assemble_strips(offsets, buffers, count, seq):
    rows, width = buffers[0].shape[1], buffers[0].shape[2] // count
    pieces, places = [], []
    for i, s_off in enumerate(offsets):
        for n, o in enumerate(line_offsets()):
            for k in range(count):
                pieces.append((i, n, 0, k * width, rows, width, k))
                places += [(seq ^ s_off ^ o) * rows, 0]
    total = rows * lax.axis_size("seq")
    return assemble(buffers, pieces, place_table(places), [(total, width)] * count)


def dense(left, right):
    return jnp.dot(left, right, preferred_element_type=F32)


def dense_back(left, right):
    return lax.dot_general(left, right, (((1,), (1,)), ((), ())), preferred_element_type=F32)


def inner_rows(left, right):
    return lax.dot_general(left, right, (((0,), (0,)), ((), ())), preferred_element_type=F32)


def layer_norm(values, gain, shift):
    middle = jnp.mean(values, -1, keepdims=True)
    centred = values - middle
    variance = jnp.mean(centred * centred, -1, keepdims=True)
    return centred * lax.rsqrt(variance + EPSILON) * gain + shift


def norm_start(values, norms, index):
    middle = jnp.mean(values, -1, keepdims=True)
    centred = values - middle
    hat = centred * lax.rsqrt(jnp.mean(centred * centred, -1, keepdims=True) + EPSILON)
    return hat * norms[0, index] + norms[1, index], hat


def adamw(grad, moment, second, weight, rate, decay):
    moment = BETA_FIRST * moment + (1.0 - BETA_FIRST) * grad
    second = BETA_SECOND * second + (1.0 - BETA_SECOND) * grad * grad
    corrected = moment / (1.0 - BETA_FIRST**STEP)
    scale_two = jnp.sqrt(second / (1.0 - BETA_SECOND**STEP))
    return (
        moment,
        second,
        weight - rate * (corrected / (scale_two + ADAM_EPSILON) + decay * weight),
    )


def payload_kernel(n_line, loss_ref, count_ref, *refs):
    zero, three, four, enc, dec = refs[n_line : n_line + 5]
    out_ref, down_ref, up_ref = refs[-3:]
    total = tree_sum([r[...].astype(F32) for r in refs[:n_line]])
    squares = jnp.sum(jnp.sum(total * total, 1, keepdims=True), 0, keepdims=True)
    rows, small = down_ref.shape[1:]
    half = rows // 2
    for k in range(2):
        top, middle, end = k * rows, k * rows + half, (k + 1) * rows
        down_ref[k, :half, :] = total[top:middle, :small]
        down_ref[k, half:, :] = total[top:middle, small:]
        up_ref[k] = total[middle:end]
    rows = [zero, (enc, 0), (enc, 2), three, four, (dec, 0), (dec, 2)]
    for at in range(2):
        for i, row in enumerate(rows):
            ref, first = row if isinstance(row, tuple) else (row, 0)
            out_ref[7 * at + i : 7 * at + i + 1, :] = ref[first + at : first + at + 1, :]
    lane = lax.broadcasted_iota(jnp.int32, (1, out_ref.shape[1]), 1)
    scalars = jnp.where(lane == 2, squares, 0.0)
    scalars = jnp.where(lane == 1, count_ref[...], scalars)
    out_ref[14:15, :] = jnp.where(lane == 0, loss_ref[...], scalars)
    out_ref[15:16, :] = jnp.zeros((1, out_ref.shape[1]), F32)


def payload(loss, count, line, sums, small):
    depth, width = line[0].shape
    rows = depth // 2
    given = [loss.reshape(1, 1), count.reshape(1, 1)] + line + sums
    vmem = pl.BlockSpec(memory_space=pltpu.VMEM)
    return pl.pallas_call(
        lambda *refs: payload_kernel(len(line), *refs),
        out_shape=[
            jax.ShapeDtypeStruct((16, width), F32),
            jax.ShapeDtypeStruct((2, rows, small), F32),
            jax.ShapeDtypeStruct((2, rows // 2, width), F32),
        ],
        in_specs=[vmem] * len(given),
        out_specs=[vmem] * 3,
        cost_estimate=pl.CostEstimate(flops=MIB, bytes_accessed=MIB, transcendentals=0),
    )(*given)


def step_kernel(summed_ref, *refs):
    grads, states, outs = refs[:2], refs[2:8], refs[8:]
    norm_grads = summed_ref[0:14, :]
    loss, count = summed_ref[14:15, 0:1], summed_ref[14:15, 1:2]
    squares = summed_ref[14:15, 2:3] + jnp.sum(
        jnp.sum(norm_grads * norm_grads, 1, keepdims=True), 0, keepdims=True
    )
    norm = jnp.sqrt(squares) / count
    factor = jnp.minimum(1.0, CLIP_NORM / norm) / count
    for ref, value in zip(outs, (loss, count, norm, factor)):
        ref[...] = value
    for i in range(2):
        moment, second, weight = states[3 * i : 3 * i + 3]
        for k in range(2):
            new = adamw(
                grads[i][k] * factor, moment[k], second[k], weight[k], RATE_ADAPTER, DECAY_ADAPTER
            )
            for j in range(3):
                outs[4 + 3 * i + j][k] = new[j]


def optimizer_step(summed, grads, states):
    vmem = pl.BlockSpec(memory_space=pltpu.VMEM)
    given = [summed] + grads + states
    outs = [jax.ShapeDtypeStruct((1, 1), F32)] * 4
    outs += [jax.ShapeDtypeStruct(states[i - i % 3].shape, F32) for i in range(6)]
    results = pl.pallas_call(
        step_kernel,
        out_shape=outs,
        in_specs=[vmem] * len(given),
        out_specs=[vmem] * len(outs),
        cost_estimate=pl.CostEstimate(flops=MIB, bytes_accessed=2 * MIB, transcendentals=0),
    )(*given)
    return [r.reshape(()) for r in results[:4]] + list(results[4:])


def scores_of(left, right):
    return lax.dot_general(left, right, (((1,), (1,)), ((), ())), preferred_element_type=F32)


def head_parts(values):
    side = lax.broadcasted_iota(jnp.int32, values.shape, 1) // HEAD_DIM
    count = values.shape[1] // HEAD_DIM
    return [jnp.where(side == h, values, jnp.zeros((), values.dtype)) for h in range(count)]


def head_join(parts):
    side = lax.broadcasted_iota(jnp.int32, (parts[0].shape[0], 128), 1) // HEAD_DIM
    joined = jnp.broadcast_to(parts[0], side.shape)
    for h in range(1, len(parts)):
        joined = jnp.where(side == h, parts[h], joined)
    return joined


def attend_kernel(limit_ref, spot_ref, q_ref, k_ref, v_ref, *rest):
    context_ref, total_ref = rest[-2:]
    queries = head_parts(q_ref[...] * jnp.asarray(0.125, LOW))
    key, value = k_ref[...], v_ref[...]
    allowed = spot_ref[...] < limit_ref[...]
    raw = [scores_of(query, key) for query in queries]
    contexts, totals = [], []
    for scores in raw:
        scores = jnp.where(allowed, scores, MASKED_SCORE)
        highest = jnp.max(scores, -1, keepdims=True)
        exponent = jnp.exp(scores - highest)
        summed = jnp.sum(exponent, -1, keepdims=True)
        contexts.append(jnp.dot(exponent.astype(LOW), value, preferred_element_type=F32) / summed)
        totals.append(highest + jnp.log(summed))
    context_ref[...] = head_join(contexts).astype(LOW)
    total_ref[...] = head_join(totals)


def attend_specs(rows, length, key_at, value_at, count):
    block = pl.BlockSpec((rows, 128), lambda p, j: (j, p))
    return [
        pl.BlockSpec((rows, 1), lambda p, j: (j, 0)),
        pl.BlockSpec((1, length), lambda p, j: (0, 0)),
        block,
        pl.BlockSpec((length, 128), lambda p, j: (0, key_at + p)),
        pl.BlockSpec((length, 128), lambda p, j: (0, value_at + p)),
    ] + [block] * count


def query_rows(length):
    return 512 if length <= 1024 else 256


def attend(query, keys, key_at, value_at, limit, spots, after=()):
    length = query.shape[0]
    width = keys.shape[1] // (2 if key_at == 0 else 3)
    pairs = width // 128
    rows = query_rows(length)
    block = pl.BlockSpec((rows, 128), lambda p, j: (j, p))
    return pl.pallas_call(
        attend_kernel,
        grid=(pairs, length // rows),
        out_shape=[
            jax.ShapeDtypeStruct((length, width), LOW),
            jax.ShapeDtypeStruct((length, width), F32),
        ],
        in_specs=attend_specs(rows, length, key_at, value_at, 0)
        + [pl.BlockSpec(memory_space=pl.ANY)] * len(after),
        out_specs=[block, block],
        compiler_params=pltpu.CompilerParams(vmem_limit_bytes=56 * MIB),
        cost_estimate=pl.CostEstimate(
            flops=8 * length * length * width,
            bytes_accessed=8 * length * width,
            transcendentals=length * length * width // HEAD_DIM,
        ),
    )(limit, spots, query, keys, keys, *after)


def attend_back_step(limit_ref, spot_ref, q_ref, k_ref, v_ref, grad_ref, total_ref, out_ref, dk_sum, dv_sum):
    pair, step = pl.program_id(0), pl.program_id(1)
    pairs, steps = pl.num_programs(0), pl.num_programs(1)
    rows = q_ref.shape[0]

    @pl.when(step == 0)
    def _():
        dk_sum[...] = jnp.zeros_like(dk_sum)
        dv_sum[...] = jnp.zeros_like(dv_sum)

    queries = head_parts(q_ref[...] * jnp.asarray(0.125, LOW))
    grads = head_parts(grad_ref[...])
    key, value, totals = k_ref[...], v_ref[...], total_ref[...]
    allowed = spot_ref[...] < limit_ref[...]
    raw = [scores_of(query, key) for query in queries]
    grad_softs = [scores_of(grad, value) for grad in grads]
    grad_scores, soft_lows = [], []
    for h, (scores, grad_soft) in enumerate(zip(raw, grad_softs)):
        scores = jnp.where(allowed, scores, MASKED_SCORE)
        soft = jnp.exp(scores - totals[:, h * HEAD_DIM : h * HEAD_DIM + 1])
        weighted = jnp.sum(soft * grad_soft, -1, keepdims=True)
        grad_scores.append((soft * (grad_soft - weighted)).astype(LOW))
        soft_lows.append(soft.astype(LOW))
    dk_sum[...] += inner_rows(jnp.concatenate(grad_scores, 0), jnp.concatenate(queries, 0))
    dv_sum[...] += inner_rows(jnp.concatenate(soft_lows, 0), jnp.concatenate(grads, 0))
    grad_query = head_join([jnp.dot(g, key, preferred_element_type=F32) for g in grad_scores])
    column = pl.multiple_of(pair * 128, 128)
    out_ref[pl.ds(pl.multiple_of(step * rows, rows), rows), pl.ds(column, 128)] = (
        grad_query * 0.125
    ).astype(LOW)

    @pl.when(step == steps - 1)
    def _():
        out_ref[:, pl.ds(pl.multiple_of((pairs + pair) * 128, 128), 128)] = dk_sum[...].astype(LOW)
        out_ref[:, pl.ds(pl.multiple_of((2 * pairs + pair) * 128, 128), 128)] = dv_sum[...].astype(
            LOW
        )


def attend_back_kernel(*refs):
    attend_back_step(*refs[:7], *refs[-3:])


def attend_sums_kernel(*refs):
    hat_ref, weight_ref, own_hat_ref, own_grad_ref = refs[7:11]
    sums_ref, out_ref, dk_sum, dv_sum, hats, weights, sem = refs[-7:]
    pair, step = pl.program_id(0), pl.program_id(1)
    copies = [
        pltpu.make_async_copy(hat_ref, hats, sem.at[0]),
        pltpu.make_async_copy(weight_ref, weights, sem.at[1]),
    ]

    @pl.when((pair == 0) & (step == 0))
    def _():
        for copy in copies:
            copy.start()

    attend_back_step(*refs[:7], out_ref, dk_sum, dv_sum)

    @pl.when((pair == pl.num_programs(0) - 1) & (step == pl.num_programs(1) - 1))
    def _():
        for copy in copies:
            copy.wait()
        weight = weights[...]
        length = out_ref.shape[0]
        coming = scores_of(out_ref[:PART, :], weight)
        own = own_grad_ref[...]
        gain = jnp.sum(own * own_hat_ref[...], 0, keepdims=True)
        shift = jnp.sum(own, 0, keepdims=True)
        for start in range(0, length, PART):
            now = coming
            if start + PART < length:
                coming = scores_of(out_ref[start + PART : start + 2 * PART, :], weight)
            gain += jnp.sum(now * hats[start : start + PART, :].astype(F32), 0, keepdims=True)
            shift += jnp.sum(now, 0, keepdims=True)
        sums_ref[0:1, :] = gain
        sums_ref[1:2, :] = shift


def attend_back(
    query, keys, key_at, value_at, limit, spots, grads, totals, sum_with=None, after=()
):
    length, width = grads.shape
    pairs = width // 128
    rows = query_rows(length)
    hbm = pl.BlockSpec(memory_space=pl.ANY)
    scratch = [pltpu.VMEM((length, 128), F32), pltpu.VMEM((length, 128), F32)]
    extra = () if sum_with is None else tuple(sum_with)
    if sum_with is None:
        kernel = attend_back_kernel
        out = jax.ShapeDtypeStruct((length, 3 * width), LOW)
    else:
        kernel = attend_sums_kernel
        out = jax.ShapeDtypeStruct((2, extra[0].shape[1]), F32)
        scratch = (
            [pltpu.VMEM((length, 3 * width), LOW)]
            + scratch
            + [pltpu.VMEM(v.shape, LOW) for v in extra[:2]]
            + [pltpu.SemaphoreType.DMA((2,))]
        )
    return pl.pallas_call(
        kernel,
        grid=(pairs, length // rows),
        out_shape=out,
        in_specs=attend_specs(rows, length, key_at, value_at, 2)
        + [hbm] * len(extra[:2])
        + [pl.BlockSpec(v.shape, lambda p, j: (0, 0)) for v in extra[2:]]
        + [hbm] * len(after),
        out_specs=pl.BlockSpec(out.shape, lambda p, j: (0, 0)),
        scratch_shapes=scratch,
        compiler_params=pltpu.CompilerParams(vmem_limit_bytes=60 * MIB),
        cost_estimate=pl.CostEstimate(
            flops=20 * length * length * width,
            bytes_accessed=16 * length * width,
            transcendentals=length * length * width // HEAD_DIM,
        ),
    )(limit, spots, query, keys, keys, grads, totals, *extra, *after)


def gelu_both(values):
    below = 0.5 * (1.0 + lax.erf(values * 0.7071067811865476))
    bell = jnp.exp(values * values * -0.5) * 0.3989422804014327
    return values * below, below + values * bell


def pack_feed(expand, reduce, down, up):
    rows, width = expand.shape[0], reduce.shape[1]
    parts = [expand[:, q * width : (q + 1) * width] for q in range(4)]
    return jnp.concatenate(
        parts + [reduce, jnp.concatenate([down[: rows // 2], down[rows // 2 :]], 1), up], 0
    )


def gather_feed(expand, reduce, down, up):
    everyone = ("seq", "enc")
    if expand.shape[0] % 32 == 0:
        return lax.all_gather(pack_feed(expand, reduce, down, up), everyone)
    whole = [lax.all_gather(v, everyone, axis=0, tiled=True) for v in (expand, reduce, down, up)]
    return pack_feed(*whole)[None]


def flat(block):
    return block.reshape(block.shape[0] * block.shape[1], block.shape[2])


def adapter_parts(block):
    count, rows, width = block.shape
    half = rows // 2
    down = jnp.stack([block[:, :half, : width // 2], block[:, :half, width // 2 :]], 1)
    return down.reshape(count * rows, width // 2), flat(block[:, half:])


def feed_scratch(packed):
    count, depth, width = packed.shape
    rows = depth // 9
    spread = max(count // 4, 1)
    return (
        [pltpu.VMEM((count, rows, width), LOW) for _ in range(4)]
        + [pltpu.VMEM((spread, width // spread, width), LOW) for _ in range(4)]
        + [pltpu.VMEM((count, rows, width), LOW), pltpu.VMEM((width, width), LOW)]
        + [pltpu.SemaphoreType.DMA((10,))]
    )


def feed_copies(packed_ref, out_ref, scratch):
    *rooms, sem = scratch
    count, depth, width = packed_ref.shape
    rows = depth // 9
    places = [packed_ref.at[:, pl.ds(q * rows, rows), :] for q in range(4)]
    for q in range(4):
        if count >= 4:
            spread = count // 4
            places.append(packed_ref.at[pl.ds(q * spread, spread), pl.ds(4 * rows, 4 * rows), :])
        else:
            places.append(packed_ref.at[:, pl.ds(4 * rows + q * width, width), :])
    places += [packed_ref.at[:, pl.ds(8 * rows, rows), :], out_ref]
    copies = [
        pltpu.make_async_copy(place, room, sem.at[i])
        for i, (place, room) in enumerate(zip(places, rooms))
    ]
    return copies[:4], copies[4:8], copies[8], copies[9]


def norm_stats(values):
    middle = jnp.mean(values, -1, keepdims=True)
    centred = values - middle
    scale = lax.rsqrt(jnp.mean(centred * centred, -1, keepdims=True) + EPSILON)
    return centred * scale, scale


def norm_back(grad, values, gain):
    hat, scale = norm_stats(values)
    scaled = grad * gain
    inner = scaled - jnp.mean(scaled, -1, keepdims=True)
    inner = inner - hat * jnp.mean(scaled * hat, -1, keepdims=True)
    return (
        inner * scale,
        jnp.sum(grad * hat, 0, keepdims=True),
        jnp.sum(grad, 0, keepdims=True),
    )


PART = 256


def branch_kernel(first, n_parts, *refs):
    parts, refs = refs[:n_parts], refs[n_parts:]
    res_ref, norm_ref, packed_ref, proj_ref = refs[:4]
    va_ref, x_ref, slope_ref, act_ref, bend_ref, vb_ref, low_ref = refs[4:11]
    total, slopes, slope_sem = refs[11:14]
    scratch = refs[14:]
    expands, reduces, small, proj = feed_copies(packed_ref, proj_ref, scratch)
    width = res_ref.shape[1]
    for copy in [proj] + [c for pair in zip(expands, reduces) for c in pair] + [small]:
        copy.start()
    proj.wait()
    context = jnp.concatenate([p[...] for p in parts], 1)
    va = res_ref[...] + jnp.dot(context, scratch[9][...], preferred_element_type=F32)
    va_ref[...] = va
    hat, _ = norm_stats(va)
    after = hat * norm_ref[first : first + 1, :] + norm_ref[7 + first : 8 + first, :]
    x = after.astype(LOW)
    x_ref[...] = x
    total[...] = after
    sends = []
    for q in range(4):
        expands[q].wait()
        expand = flat(scratch[q][...])
        pre = jnp.dot(x, expand[:, :PART], preferred_element_type=F32)
        acts = []
        for start in range(0, width, PART):
            now = pre
            if start + PART < width:
                pre = jnp.dot(
                    x, expand[:, start + PART : start + 2 * PART], preferred_element_type=F32
                )
            act, slope = gelu_both(now)
            slopes[q, :, start : start + PART] = slope
            acts.append(act.astype(LOW))
        sends.append(
            pltpu.make_async_copy(
                slopes.at[q], slope_ref.at[:, pl.ds(q * width, width)], slope_sem.at[q]
            )
        )
        sends[q].start()
        reduces[q].wait()
        total[...] += jnp.dot(
            jnp.concatenate(acts, 1), flat(scratch[4 + q][...]), preferred_element_type=F32
        )
    small.wait()
    down, up = adapter_parts(scratch[8][...])
    act, slope = gelu_both(jnp.dot(x, down, preferred_element_type=F32))
    act = act.astype(LOW)
    act_ref[...] = act
    bend_ref[...] = slope
    vb = total[...] + ADAPTER_SCALE * jnp.dot(act, up, preferred_element_type=F32)
    vb_ref[...] = vb
    hat, _ = norm_stats(vb)
    low_ref[...] = (
        hat * norm_ref[first + 1 : first + 2, :] + norm_ref[8 + first : 9 + first, :]
    ).astype(LOW)
    for send in sends:
        send.wait()


def branch(parts, residual, norms, first, packed, proj):
    rows, width = residual.shape
    hidden, small = 4 * width, width // 2
    vmem = pl.BlockSpec(memory_space=pltpu.VMEM)
    hbm = pl.BlockSpec(memory_space=pl.ANY)
    va, x, slope, act, bend, vb, low = pl.pallas_call(
        lambda *refs: branch_kernel(first, len(parts), *refs),
        out_shape=[
            jax.ShapeDtypeStruct((rows, width), F32),
            jax.ShapeDtypeStruct((rows, width), LOW),
            jax.ShapeDtypeStruct((rows, hidden), F32),
            jax.ShapeDtypeStruct((rows, small), LOW),
            jax.ShapeDtypeStruct((rows, small), F32),
            jax.ShapeDtypeStruct((rows, width), F32),
            jax.ShapeDtypeStruct((rows, width), LOW),
        ],
        in_specs=[vmem] * (len(parts) + 2) + [hbm, hbm],
        out_specs=[vmem, vmem, hbm, vmem, vmem, vmem, vmem],
        scratch_shapes=[
            pltpu.VMEM((rows, width), F32),
            pltpu.VMEM((4, rows, width), F32),
            pltpu.SemaphoreType.DMA((4,)),
        ]
        + feed_scratch(packed),
        compiler_params=pltpu.CompilerParams(vmem_limit_bytes=56 * MIB),
        cost_estimate=pl.CostEstimate(
            flops=4 * rows * width * (hidden + small) + 2 * rows * width * width,
            bytes_accessed=4 * width * (hidden + small) + 4 * rows * hidden,
            transcendentals=2 * rows * hidden,
        ),
    )(*parts, residual, norms, packed, proj)
    return low, (va, x, slope, act, bend, vb)


def branch_back_kernel(first, n_parts, *refs):
    n_given, refs = (refs[0], refs[1:])
    given, refs = refs[:n_given], refs[n_given:]
    vb_ref, va_ref, norm_ref, bend_ref, slope_ref, packed_ref, proj_ref = refs[:7]
    dva_ref, sums_ref, dpre_ref, ga_ref = refs[7:11]
    spread_refs, refs = refs[11 : 11 + n_parts], refs[11 + n_parts :]
    total, slopes, slope_sem = refs[:3]
    scratch = refs[3:]
    expands, reduces, small, proj = feed_copies(packed_ref, proj_ref, scratch)
    width = va_ref.shape[1]
    gets = [
        pltpu.make_async_copy(
            slope_ref.at[:, pl.ds(q * width, width)], slopes.at[q], slope_sem.at[q]
        )
        for q in range(4)
    ]
    for copy in [small] + [c for three in zip(reduces, gets, expands) for c in three] + [proj]:
        copy.start()
    if n_given == 2:
        grad = given[0][...].astype(F32) + given[1][...].astype(F32)
    else:
        mean, total_own, other, total_other, label, valid = [r[...] for r in given]
        grad = merge_means((mean, total_own), (other, total_other))[0]
        grad = (grad - label.astype(F32)) * valid
    grad_out, gain, shift = norm_back(grad, vb_ref[...], norm_ref[first + 1 : first + 2, :])
    sums_ref[2:3, :] = gain
    sums_ref[3:4, :] = shift
    g = grad_out.astype(LOW)
    ga = (ADAPTER_SCALE * grad_out).astype(LOW)
    ga_ref[...] = ga
    small.wait()
    down, up = adapter_parts(scratch[8][...])
    pre = (dense_back(ga, up) * bend_ref[...]).astype(LOW)
    dpre_ref[...] = pre
    total[...] = grad_out + dense_back(pre, down)
    for q in range(4):
        reduces[q].wait()
        reduce = flat(scratch[4 + q][...])
        gets[q].wait()
        grad = dense_back(g, reduce[:PART])
        pres = []
        for start in range(0, width, PART):
            now = grad
            if start + PART < width:
                grad = dense_back(g, reduce[start + PART : start + 2 * PART])
            pres.append((now * slopes[q, :, start : start + PART]).astype(LOW))
        expands[q].wait()
        total[...] += dense_back(jnp.concatenate(pres, 1), flat(scratch[q][...]))
    dva, gain, shift = norm_back(total[...], va_ref[...], norm_ref[first : first + 1, :])
    sums_ref[0:1, :] = gain
    sums_ref[1:2, :] = shift
    dva_ref[...] = dva
    proj.wait()
    spread = dense_back(dva.astype(LOW), scratch[9][...]).astype(LOW)
    share = width // n_parts
    for j in range(n_parts):
        spread_refs[j][...] = spread[:, j * share : (j + 1) * share]


def branch_back(given, kept, norms, first, packed, proj, n_parts):
    va, x, slope, act, bend, vb = kept
    rows, width = va.shape
    hidden, small = 4 * width, width // 2
    vmem = pl.BlockSpec(memory_space=pltpu.VMEM)
    hbm = pl.BlockSpec(memory_space=pl.ANY)
    dva, sums, dpre, ga, *spread = pl.pallas_call(
        lambda *refs: branch_back_kernel(first, n_parts, len(given), *refs),
        out_shape=[
            jax.ShapeDtypeStruct((rows, width), F32),
            jax.ShapeDtypeStruct((4, width), F32),
            jax.ShapeDtypeStruct((rows, small), LOW),
            jax.ShapeDtypeStruct((rows, width), LOW),
        ]
        + [jax.ShapeDtypeStruct((rows, width // n_parts), LOW)] * n_parts,
        in_specs=[vmem] * (4 + len(given)) + [hbm] * 3,
        out_specs=[vmem] * (4 + n_parts),
        scratch_shapes=[
            pltpu.VMEM((rows, width), F32),
            pltpu.VMEM((4, rows, width), F32),
            pltpu.SemaphoreType.DMA((4,)),
        ]
        + feed_scratch(packed),
        compiler_params=pltpu.CompilerParams(vmem_limit_bytes=56 * MIB),
        cost_estimate=pl.CostEstimate(
            flops=4 * rows * width * (hidden + small) + 2 * rows * width * width,
            bytes_accessed=4 * width * (hidden + small) + 4 * rows * hidden,
            transcendentals=0,
        ),
    )(*given, vb, va, norms, bend, slope, packed, proj)
    return dva, spread, sums, (x, dpre, act, ga)


def middle_back_kernel(first, n_parts, *refs):
    res_ref, own_ref, far_ref, va_ref, norm_ref, proj_ref = refs[:6]
    dva_ref, sums_ref = refs[6:8]
    grad = res_ref[...] + own_ref[...].astype(F32) + far_ref[...].astype(F32)
    dva, gain, shift = norm_back(grad, va_ref[...], norm_ref[first : first + 1, :])
    dva_ref[...] = dva
    sums_ref[0:1, :] = gain
    sums_ref[1:2, :] = shift
    spread = dense_back(dva.astype(LOW), proj_ref[...]).astype(LOW)
    share = spread.shape[1] // n_parts
    for j in range(n_parts):
        refs[8 + j][...] = spread[:, j * share : (j + 1) * share]


def middle_back(residual, own, far, va, norms, first, proj, n_parts):
    rows, width = va.shape
    vmem = pl.BlockSpec(memory_space=pltpu.VMEM)
    dva, sums, *spread = pl.pallas_call(
        lambda *refs: middle_back_kernel(first, n_parts, *refs),
        out_shape=[
            jax.ShapeDtypeStruct((rows, width), F32),
            jax.ShapeDtypeStruct((2, width), F32),
        ]
        + [jax.ShapeDtypeStruct((rows, width // n_parts), LOW)] * n_parts,
        in_specs=[vmem] * 6,
        out_specs=[vmem] * (2 + n_parts),
        compiler_params=pltpu.CompilerParams(vmem_limit_bytes=32 * MIB),
        cost_estimate=pl.CostEstimate(
            flops=2 * rows * width * width, bytes_accessed=8 * MIB, transcendentals=0
        ),
    )(residual, own, far, va, norms, proj)
    return dva, spread, sums


def adapter_grad_kernel(core_ref, *refs):
    keep_ref, send_ref, down, up = refs[-4:]
    core = core_ref[0]
    pairs, depth, width = keep_ref.shape
    rows = depth // 2
    half, small = rows // 2, width // 2
    for k in range(2):
        x_ref, dpre_ref, act_ref, ga_ref = refs[4 * k : 4 * k + 4]
        down[...] = inner_rows(x_ref[...], dpre_ref[...])
        up[...] = inner_rows(act_ref[...], ga_ref[...])
        top, middle, end = k * rows, k * rows + half, (k + 1) * rows
        for ref, side in ((keep_ref, core), (send_ref, 1 - core)):
            for pair in range(pairs):
                device = 2 * pair + side
                at = pl.multiple_of(device * rows, rows)
                ref[pair, top:middle, :small] = down[pl.ds(at, half), :].astype(ref.dtype)
                ref[pair, top:middle, small:] = down[pl.ds(at + half, half), :].astype(ref.dtype)
                ref[pair, middle:end, :] = up[
                    pl.ds(pl.multiple_of(device * half, half), half), :
                ].astype(ref.dtype)


def adapter_grads(given, core):
    width, small = given[0][0].shape[1], given[0][1].shape[1]
    n_all = lax.axis_size("seq") * lax.axis_size("enc")
    rows = width // n_all
    if rows % 16:
        layers = []
        for x, dpre, act, ga in given:
            down, up = inner_rows(x, dpre), inner_rows(act, ga)
            folded = down.reshape(n_all, 2, rows // 2, small).transpose(0, 2, 1, 3)
            layers += [folded.reshape(n_all, rows // 2, width), up.reshape(n_all, rows // 2, width)]
        both = jnp.concatenate(layers, 1).reshape(n_all // 2, 2, 2 * rows, width)
        first = core == 0
        keep, send = jnp.where(first, both[:, 0], both[:, 1]), jnp.where(first, both[:, 1], both[:, 0])
        return keep, send.astype(LOW)
    shape = (n_all // 2, 2 * rows, width)
    vmem = pl.BlockSpec(memory_space=pltpu.VMEM)
    return pl.pallas_call(
        adapter_grad_kernel,
        out_shape=[jax.ShapeDtypeStruct(shape, F32), jax.ShapeDtypeStruct(shape, LOW)],
        in_specs=[pl.BlockSpec(memory_space=pltpu.SMEM)] + [vmem] * 8,
        out_specs=[vmem] * 2,
        scratch_shapes=[pltpu.VMEM((width, small), F32), pltpu.VMEM((small, width), F32)],
        compiler_params=pltpu.CompilerParams(vmem_limit_bytes=40 * MIB),
        cost_estimate=pl.CostEstimate(
            flops=8 * given[0][0].shape[0] * width * small,
            bytes_accessed=16 * MIB,
            transcendentals=0,
        ),
    )(core.reshape(1).astype(jnp.int32), *given[0], *given[1])


def head_kernel(n_blocks, *refs):
    o_refs, e_ref = refs[:n_blocks], refs[n_blocks]
    g_refs, lse_refs = refs[n_blocks + 1 : 2 * n_blocks + 1], refs[2 * n_blocks + 1 : -3]
    acc, peak, mass = refs[-3:]
    step = pl.program_id(0)
    rows = o_refs[0].shape[0]
    part = 2 * rows

    @pl.when(step == 0)
    def _():
        acc[...] = jnp.zeros_like(acc)
        peak[...] = jnp.full_like(peak, -1e30)
        mass[...] = jnp.zeros_like(mass)

    table = e_ref[...]
    spans = [pl.ds(start, part) for start in range(0, n_blocks * rows, part)]

    def logits_of(h):
        both = jnp.concatenate([o_refs[2 * h][...], o_refs[2 * h + 1][...]], 0)
        return scores_of(both, table)

    before = [peak[at, :1] for at in spans]
    held = [mass[at, :] for at in spans]
    coming = logits_of(0)
    highest, summed = [], []
    for h, at in enumerate(spans):
        logits = coming
        if h + 1 < len(spans):
            coming = logits_of(h + 1)
        highest.append(jnp.maximum(before[h], jnp.max(logits, -1, keepdims=True)))
        exponent = jnp.exp(logits - highest[h])
        fade = jnp.exp(before[h] - highest[h])
        summed.append(held[h] * fade + jnp.sum(exponent, -1, keepdims=True))
        acc[at, :] = acc[at, :] * fade + jnp.dot(
            exponent.astype(LOW), table, preferred_element_type=F32
        )
    for h, at in enumerate(spans):
        mass[at, :] = summed[h]
        peak[at, :] = jnp.broadcast_to(highest[h], (part, 128))

    @pl.when(step == pl.num_programs(0) - 1)
    def _():
        for j in range(n_blocks):
            at = pl.ds(j * rows, rows)
            g_refs[j][...] = (acc[at, :] / mass[at, :1]).astype(LOW)
            lse_refs[j][...] = peak[at, :1] + jnp.log(mass[at, :1])


def head(blocks, table):
    rows, width = blocks[0].shape
    count = len(blocks)
    entries = table.shape[0]
    tile = next(t for t in (1280, 1024, 640, 512, 256, 128) if entries % t == 0)
    block = pl.BlockSpec((rows, width), lambda j: (0, 0))
    results = pl.pallas_call(
        lambda *refs: head_kernel(count, *refs),
        grid=(entries // tile,),
        out_shape=[jax.ShapeDtypeStruct((rows, width), LOW)] * count
        + [jax.ShapeDtypeStruct((rows, 1), F32)] * count,
        in_specs=[block] * count + [pl.BlockSpec((tile, width), lambda j: (j, 0))],
        out_specs=[block] * count + [pl.BlockSpec((rows, 1), lambda j: (0, 0))] * count,
        scratch_shapes=[
            pltpu.VMEM((count * rows, width), F32),
            pltpu.VMEM((count * rows, 128), F32),
            pltpu.VMEM((count * rows, 128), F32),
        ],
        compiler_params=pltpu.CompilerParams(vmem_limit_bytes=60 * MIB),
        cost_estimate=pl.CostEstimate(
            flops=4 * count * rows * width * entries,
            bytes_accessed=2 * width * entries,
            transcendentals=count * rows * entries,
        ),
    )(*blocks, table)
    return list(results[:count]), list(results[count:])


def adapters_plane(held, seq, enc):
    n_seq, n_enc = lax.axis_size("seq"), lax.axis_size("enc")
    near = n_seq // 4
    rows, width = held.shape[1:]
    held = held.reshape(4, near, n_enc // 2, rows, width)

    def block(s_off, e_off):
        start = (0, (seq & (near - 1)) ^ s_off, (enc >> 1) ^ (e_off >> 1), 0, 0)
        return lax.dynamic_slice(held, start, (4, 1, 1, rows, width))[:, 0, 0]

    return [block(0, 0)] + [flip_both(block(s, e).astype(LOW), s, e) for s, e in plane_offsets()[1:]]


def adapters_line(parts, seq):
    held = tree_sum([p.astype(F32) for p in parts])
    slow = seq // (lax.axis_size("seq") // 4)
    parts = [lax.dynamic_index_in_dim(held, slow ^ k, 0, keepdims=False) for k in range(4)]
    return parts[:1] + [
        flip(p.astype(LOW), "seq", o) for p, o in zip(parts[1:], line_offsets()[1:])
    ]


def sum_everywhere(values):
    values = values + flip(values, "enc", 1)
    values = tree_sum([values] + [flip_both(values, s, e) for s, e in plane_offsets()[1:]])
    return tree_sum([values] + [flip(values, "seq", o) for o in line_offsets()[1:]])


def shards(
    source_ids,
    target_ids,
    labels,
    lengths,
    embedding,
    positions,
    attention_in,
    attention_out,
    feed_in,
    feed_out,
    adapter_down,
    adapter_up,
    norm_params,
    down_moment,
    down_second,
    up_moment,
    up_second,
    norm_moment,
    norm_second,
):
    n_seq, n_enc = lax.axis_size("seq"), lax.axis_size("enc")
    n_all = n_seq * n_enc
    seq, enc = lax.axis_index("seq"), lax.axis_index("enc")
    core = enc & 1
    own_rows = source_ids.shape[1]
    width = embedding.shape[1]
    entries = embedding.shape[0]
    length = own_rows * n_enc
    share = width // n_enc
    source_length, target_length = lengths[0, 0], lengths[0, 1]

    blocks = jnp.arange(n_enc) ^ enc
    spots = (blocks[:, None] * own_rows + jnp.arange(own_rows)[None, :]).reshape(length)
    spots = spots.astype(jnp.int32)
    source_limit = jnp.broadcast_to(source_length, (length, 1)).astype(jnp.int32)
    causal_limit = jnp.minimum(spots + 1, target_length)[:, None].astype(jnp.int32)
    spots = spots[None, :]
    in_strip = share // 128

    def gather_rows(rows_low):
        return jnp.concatenate(gather_enc(rows_low), 0)

    def lookup(ids):
        inside = (ids >= 0) & (ids < entries)
        found = jnp.take(embedding, jnp.clip(ids, 0, entries - 1), axis=0)
        return jnp.where(inside[:, :, None], found, jnp.zeros((), LOW))

    def rows_of(found):
        return scatter_enc([found[j] for j in range(n_enc)])

    def own_parts(context):
        return swap_blocks([context[j * own_rows : (j + 1) * own_rows] for j in range(n_enc)])

    def all_heads(spread):
        return jnp.concatenate(swap_blocks(spread), 0)

    def row_blocks(partial):
        return [partial[j * own_rows : (j + 1) * own_rows] for j in range(n_enc)]

    down_low, up_low = adapter_down.astype(LOW), adapter_up.astype(LOW)
    feeds = [gather_feed(feed_in[k], feed_out[k], down_low[k], up_low[k]) for k in range(2)]

    gains = norm_params.astype(LOW).astype(F32)
    ids = jnp.concatenate([source_ids, target_ids, labels], 0).astype(F32)
    small_own = jnp.concatenate([ids.reshape(1, -1), gains.reshape(1, -1)], 1)
    small_all = unxor([v[0] for v in jnp.split(lax.all_gather(small_own, "enc"), n_enc)], enc)
    small_all = jnp.concatenate(small_all, 0)
    all_ids = small_all[:, : 3 * own_rows].astype(jnp.int32).reshape(n_enc, 3, own_rows)
    all_ids = all_ids - enc * entries
    gains = small_all[:, 3 * own_rows :].astype(LOW)[None]

    triple = attention_in.reshape(3, -1, 3, n_enc, share).transpose(3, 1, 0, 2, 4)
    shard_rows = triple.shape[1]
    strip_rows, pair_rows = n_enc * shard_rows, 2 * shard_rows
    triple = triple.reshape(n_enc, shard_rows, 9 * share)
    strip = lax.all_to_all(triple, "enc", 0, 0, tiled=True).reshape(strip_rows, 9 * share)
    strip, late = strip[:, : 6 * share], strip[:, 6 * share :]
    half = width // 2
    packed = jnp.concatenate(
        [attention_out[k][:, h * half : (h + 1) * half] for h in range(2) for k in range(3)], 1
    )
    pair_out = pair_split(packed, core)

    ids = [all_ids[:, k] for k in range(3)]

    slow = slow_flips(strip)
    for mask in bits("seq"):
        gains = jnp.concatenate([gains, flip(gains, "seq", mask)], 0)
    found = [lookup(ids[0]), lookup(ids[1]), lookup(ids[2])]
    pair_out, *slow = gate([pair_out] + slow)
    order_seq, order_enc = jnp.arange(n_seq) ^ seq, jnp.arange(n_enc) ^ enc
    gains = jnp.take(jnp.take(gains, order_seq, axis=0), order_enc, axis=1)
    gains = gains.reshape(n_all, 14, width // n_all).transpose(1, 0, 2)
    norms = gains.reshape(2, 7, width).astype(F32)

    strip_offsets, strips = near_flips(jnp.stack([strip] + slow))
    source_rows, target_rows = rows_of(found[0]), rows_of(found[1])
    slow = slow_flips(pair_out)
    late, *slow = gate([late] + slow)

    in_enc, in_dec = assemble_strips(strip_offsets, strips, 2, seq)
    encoder_in, encoder_hat = norm_start(source_rows + positions[0].astype(F32), norms, 0)
    decoder_in, decoder_hat = norm_start(target_rows + positions[1].astype(F32), norms, 3)
    encoder_all = gather_rows(encoder_in.astype(LOW))
    decoder_all = gather_rows(decoder_in.astype(LOW))
    stacked = jnp.stack([pair_out] + slow)
    singles = plane_start(stacked)

    triple_encoder = dense(encoder_all, in_enc).astype(LOW)
    enc_args = (triple_encoder, triple_encoder, in_strip, 2 * in_strip, source_limit, spots)
    context_enc, total_encoder = attend(*enc_args)
    context_enc, *singles = gate([context_enc] + singles)
    own, other, mine = plane_finish(stacked, singles, core)
    partners = [flip(v, "enc", 1) for v in mine]
    slow = slow_flips(late)
    triple_decoder = dense(decoder_all, in_dec).astype(LOW)
    dec_args = (triple_decoder, triple_decoder, in_strip, 2 * in_strip, causal_limit, spots)
    context_dec, total_decoder = attend(*dec_args)

    def out_layout(pair, side):
        row = pair * pair_rows
        block = (row // share) ^ enc
        return [
            (0, k * half, pair_rows, half, k, block * share + row % share, side * half)
            for k in range(3)
        ]

    attend_out = assemble_matrix(
        own, other, mine, partners, out_layout, [(width, width)] * 3, seq, enc
    )
    late_offsets, strips = near_flips(jnp.stack([late] + slow))
    attended = dense(jnp.concatenate(own_parts(context_dec), 1), attend_out[1])
    causal_in = decoder_in + attended
    after_causal = norm_start(causal_in, norms, 4)[0]
    in_cross = assemble_strips(late_offsets, strips, 1, seq)[0]
    attend_in = [in_enc, in_dec, in_cross]
    causal_all = gather_rows(after_causal.astype(LOW))
    norm_rows = norms.reshape(14, width)
    encoded_low, kept_enc = branch(
        own_parts(context_enc), encoder_in, norm_rows, 1, feeds[0], attend_out[0]
    )
    query_cross = dense(causal_all, in_cross[:, :share]).astype(LOW)

    encoded_all, found[2] = gate([gather_rows(encoded_low), found[2]])
    label_rows, label_came = scatter_two([found[2][j] for j in range(n_enc)])
    pairs_cross = dense(encoded_all, in_cross[:, share:]).astype(LOW)
    cross_args = (query_cross, pairs_cross, 0, in_strip, source_limit, spots)
    context, total_cross = attend(*cross_args)
    decoded_low, kept_dec = branch(
        own_parts(context), after_causal, norm_rows, 5, feeds[1], attend_out[2]
    )

    decoded_low, label_came = gate([decoded_low, label_came])

    *decoded_all, encoder_low, decoder_low = gate(
        gather_enc(decoded_low) + [encoder_hat.astype(LOW), decoder_hat.astype(LOW)]
    )
    pulled, totals = head(decoded_all, embedding)
    hats = gather_across(encoder_low) + gather_across(decoder_low)
    results = gate(pulled + totals + hats)
    pulled, totals, hats = results[:n_enc], results[n_enc : 2 * n_enc], results[2 * n_enc :]
    label_rows = (label_rows.astype(F32) + label_came.astype(F32)).astype(LOW)
    row_spots = enc * own_rows + jnp.arange(own_rows)
    valid = (row_spots < target_length).astype(F32)[:, None]
    picked = jnp.sum(decoded_low.astype(F32) * label_rows.astype(F32), -1, keepdims=True)
    own_mean, far_mean = merge_enc(pulled, totals)
    half_hats = len(hats) // 2
    hats = gather_pair(hats[:half_hats]) + gather_pair(hats[half_hats:])
    far, *hats = gate([far_mean[0]] + hats)
    encoder_hats, decoder_hats = jnp.concatenate(hats[:n_enc], 0), jnp.concatenate(hats[n_enc:], 0)
    highest = jnp.maximum(own_mean[1], far_mean[1])
    log_total = highest + jnp.log(
        jnp.exp(own_mean[1] - highest) + jnp.exp(far_mean[1] - highest)
    )
    loss_own = jnp.sum((log_total - picked) * valid)

    grad_res, spread, sums_dec, given_dec = branch_back(
        [own_mean[0], own_mean[1], far, far_mean[1], label_rows, valid],
        kept_dec,
        norm_rows,
        5,
        feeds[1],
        attend_out[2],
        n_enc,
    )
    grads = attend_back(*cross_args, all_heads(spread), total_cross)
    own_encoded, far_encoded = scatter_two(
        row_blocks(dense_back(grads[:, share:], attend_in[2][:, share:]))
    )
    own_causal, far_causal = scatter_two(
        row_blocks(dense_back(grads[:, :share], attend_in[2][:, :share]))
    )
    grad_enc, spread, sums_enc, given_enc = branch_back(
        [own_encoded, far_encoded], kept_enc, norm_rows, 1, feeds[0], attend_out[0], n_enc
    )
    spread = swap_blocks(spread)
    x, dpre, act, ga = given_enc
    spread[1], dpre, far_causal = gate([spread[1], dpre, far_causal])
    keep, send = adapter_grads([(x, dpre, act, ga), given_dec], core)
    held = keep + flip(send, "enc", 1).astype(F32)
    grad_dec, spread_dec, sums_four = middle_back(
        grad_res, own_causal, far_causal, causal_in, norm_rows, 4, attend_out[1], n_enc
    )
    sums_zero = attend_back(
        *enc_args,
        jnp.concatenate(spread, 0),
        total_encoder,
        sum_with=(encoder_hats, in_enc, encoder_hat, grad_enc),
        after=[held, grad_dec],
    )
    parts = adapters_plane(held, seq, enc)
    sums_zero, *parts[1:] = gate([sums_zero] + parts[1:])
    parts = adapters_line(parts, seq)
    sums_three = attend_back(
        *dec_args,
        all_heads(spread_dec),
        total_decoder,
        sum_with=(decoder_hats, in_dec, decoder_hat, grad_dec),
        after=[sums_zero],
    )
    sums_three, *parts[1:] = gate([sums_three] + parts[1:])

    count_own = jnp.clip(target_length - enc * own_rows, 0, own_rows).astype(F32)
    summed, grad_down, grad_up = payload(
        loss_own,
        count_own,
        parts,
        [sums_zero, sums_three, sums_four, sums_enc, sums_dec],
        adapter_down.shape[2],
    )
    summed = sum_everywhere(summed)
    per = width // n_all
    own = lax.dynamic_slice_in_dim(summed, (seq * n_enc + enc) * per, per, 1)[:14]
    loss_sum, token_total, grad_norm, factor, *adapters = optimizer_step(
        summed,
        [grad_down, grad_up],
        [down_moment, down_second, adapter_down, up_moment, up_second, adapter_up],
    )
    new_norms = adamw(
        own.reshape(2, 7, per) * factor, norm_moment, norm_second, norm_params, RATE_NORMS, 0.0
    )
    return (loss_sum, token_total, grad_norm, *adapters, *new_norms)


def solution(mesh):
    everywhere = P(None, ("seq", "enc"), None)
    columns = P(None, None, ("seq", "enc"))
    return jax.shard_map(
        shards,
        mesh=mesh,
        in_specs=(
            P("seq", "enc"),
            P("seq", "enc"),
            P("seq", "enc"),
            P("seq", None),
            P("enc", None),
            P(None, "enc", None),
            everywhere,
            everywhere,
            everywhere,
            everywhere,
            everywhere,
            everywhere,
            columns,
            everywhere,
            everywhere,
            everywhere,
            everywhere,
            columns,
            columns,
        ),
        out_specs=(
            P(),
            P(),
            P(),
            everywhere,
            everywhere,
            everywhere,
            everywhere,
            everywhere,
            everywhere,
            columns,
            columns,
            columns,
        ),
        check_vma=False,
    )
```

```python
import jax
import jax.numpy as jnp
from jax import lax
from jax.experimental import pallas as pl
from jax.experimental.pallas import tpu as pltpu
from jax.sharding import PartitionSpec as P

HEAD_DIM = 64
STEP = 10

EPSILON = 1e-05
ADAPTER_SCALE = 4.0
CLIP_NORM = 0.25
RATE_ADAPTER = 0.05
RATE_NORMS = 0.5
BETA_FIRST = 0.9
BETA_SECOND = 0.999
ADAM_EPSILON = 1e-08
DECAY_ADAPTER = 0.01
MASKED_SCORE = -1000000000.0

LOW = jnp.bfloat16
F32 = jnp.float32
MIB = 1024 * 1024


def flip(value, axis, mask):
    count = lax.axis_size(axis)
    return lax.ppermute(value, axis, [(i, i ^ mask) for i in range(count)])


def bits(axis):
    count = lax.axis_size(axis)
    return [1 << i for i in range(count.bit_length() - 1)]


def unxor(blocks, me):
    blocks = list(blocks)
    mask = 1
    while mask < len(blocks):
        bit = (me & mask) != 0
        blocks = [jnp.where(bit, blocks[i ^ mask], blocks[i]) for i in range(len(blocks))]
        mask *= 2
    return blocks


def gather_across(value):
    found = {0: value}
    for mask in bits("enc")[1:]:
        found.update({j | mask: flip(v, "enc", mask) for j, v in list(found.items())})
    return [found[j] for j in sorted(found)]


def gather_pair(blocks):
    return [v for block in blocks for v in (block, flip(block, "enc", 1))]


def gather_enc(value):
    return gather_pair(gather_across(value))


def scatter_two(blocks):
    held = dict(enumerate(blocks))
    for mask in bits("enc"):
        away = [j for j in held if j & mask]
        sent = [flip(held[j].astype(LOW), "enc", mask) for j in away]
        for j, part in zip(away, sent):
            if len(held) == 2:
                return held[j ^ mask], part
            held[j ^ mask] = held[j ^ mask].astype(F32) + part.astype(F32)
            del held[j]


def scatter_enc(blocks):
    own, came = scatter_two(blocks)
    return own.astype(F32) + came.astype(F32)


def merge_means(first, second):
    (mean, total), (other, other_total) = first, second
    highest = jnp.maximum(total, other_total)
    own, far = jnp.exp(total - highest), jnp.exp(other_total - highest)
    both = own + far
    return (mean.astype(F32) * own + other.astype(F32) * far) / both, highest + jnp.log(both)


def merge_enc(blocks, totals, beside):
    held = {j: (b, t) for j, (b, t) in enumerate(zip(blocks, totals))}
    for mask in bits("enc"):
        away = [j for j in held if j & mask]
        means = [held[j][0].astype(LOW) for j in away]
        if len(held) == 2:
            means[0], *beside = gate([means[0]] + beside)
        sent = [(flip(m, "enc", mask), flip(held[j][1], "enc", mask)) for j, m in zip(away, means)]
        for j, came in zip(away, sent):
            if len(held) == 2:
                return held[j ^ mask], came, beside
            held[j ^ mask] = merge_means(held[j ^ mask], came)
            del held[j]


def swap_blocks(blocks):
    return [blocks[0]] + [flip(blocks[j], "enc", j) for j in range(1, len(blocks))]


def pair_split(shard, core):
    half = shard.shape[1] // 2
    first = core == 0
    low, high = shard[:, :half], shard[:, half:]
    keep = jnp.where(first, low, high)
    came = flip(jnp.where(first, high, low), "enc", 1)
    return jnp.concatenate([jnp.where(first, keep, came), jnp.where(first, came, keep)], 0)


def gate(arrays):
    def kernel(*refs):
        pass

    results = pl.pallas_call(
        kernel,
        out_shape=[jax.ShapeDtypeStruct(v.shape, v.dtype) for v in arrays],
        in_specs=[pl.BlockSpec(memory_space=pl.ANY)] * len(arrays),
        out_specs=[pl.BlockSpec(memory_space=pl.ANY)] * len(arrays),
        input_output_aliases={i: i for i in range(len(arrays))},
        compiler_params=pltpu.CompilerParams(vmem_limit_bytes=60 * MIB),
        cost_estimate=pl.CostEstimate(flops=0, bytes_accessed=0, transcendentals=0),
    )(*arrays)
    return list(results)


def flip_both(value, seq_mask, enc_mask):
    n_enc = lax.axis_size("enc")
    perm = []
    for i in range(lax.axis_size("seq") * n_enc):
        s, e = divmod(i, n_enc)
        perm.append((i, (s ^ seq_mask) * n_enc + (e ^ enc_mask)))
    return lax.ppermute(value, ("seq", "enc"), perm)


def tree_sum(values):
    values = list(values)
    while len(values) > 1:
        values = [values[i] + values[i + 1] for i in range(0, len(values), 2)]
    return values[0]


def plane_offsets():
    near = lax.axis_size("seq") // 4
    return [(s, e) for e in range(0, lax.axis_size("enc"), 2) for s in range(near)]


def line_offsets():
    return [k * (lax.axis_size("seq") // 4) for k in range(4)]


def mixed_flip(value, for_even, for_odd):
    n_enc = lax.axis_size("enc")
    perm = []
    for i in range(lax.axis_size("seq") * n_enc):
        s, e = divmod(i, n_enc)
        axis, mask = for_odd if e & 1 else for_even
        perm.append((i, (s ^ mask) * n_enc + e if axis == "seq" else s * n_enc + (e ^ mask)))
    return lax.ppermute(value, ("seq", "enc"), perm)


def near_bits():
    return [("seq", mask) for mask in bits("seq") if mask < lax.axis_size("seq") // 4]


def across_bits():
    return [("enc", mask) for mask in bits("enc")[1:]]


def moved(offset, step):
    return (offset[0] ^ step[1], offset[1]) if step[0] == "seq" else (offset[0], offset[1] ^ step[1])


def slow_flips(value):
    return [flip(value, "seq", o) for o in line_offsets()[1:]]


def slow_flips_both(first, second):
    if first.shape[1] != second.shape[1]:
        return slow_flips(first), slow_flips(second)
    return slow_flips(jnp.concatenate([first, second], 0)), None


def plane_steps():
    return list(zip(near_bits() + across_bits(), across_bits() + near_bits()))


def plane_start(stacked):
    return [mixed_flip(stacked, *step) for step in plane_steps()]


def plane_finish(stacked, singles, core):
    found = [((0, 0), (0, 0), stacked)]
    for step, single in zip(plane_steps(), singles):
        fresh = [(moved((0, 0), step[0]), moved((0, 0), step[1]), single)]
        fresh += [
            (moved(o, step[0]), moved(p, step[1]), mixed_flip(v, *step)) for o, p, v in found[1:]
        ]
        found += fresh
    own = [tuple(jnp.where(core == 0, i, k) for i, k in zip(o, p)) for o, p, _ in found]
    other = [tuple(jnp.where(core == 0, k, i) for i, k in zip(o, p)) for o, p, _ in found]
    return own, other, [v for _, _, v in found]


def near_flips(stacked):
    found = [(0, stacked)]
    for _, mask in near_bits():
        found += [(o ^ mask, flip(v, "seq", mask)) for o, v in found]
    return [o for o, _ in found], [v for _, v in found]


def assemble(sources, pieces, places, outs):
    count = len(pieces)
    n_src, n_out = len(sources), len(outs)

    def kernel(*refs):
        table = refs[0]
        given = refs[1 : 1 + n_src]
        results = refs[1 + n_src : 1 + n_src + n_out]
        stage = refs[1 + n_src + n_out : 1 + n_src + n_out + count]
        sem_in, sem_out = refs[-2:]
        copies_in, copies_out = [], []
        for i, (src, block, row, column, rows, columns, out) in enumerate(pieces):
            copies_in.append(
                pltpu.make_async_copy(
                    given[src].at[block, pl.ds(row, rows), pl.ds(column, columns)],
                    stage[i],
                    sem_in.at[i],
                )
            )
            to_row = pl.multiple_of(table[2 * i], rows)
            to_column = pl.multiple_of(table[2 * i + 1], columns)
            copies_out.append(
                pltpu.make_async_copy(
                    stage[i],
                    results[out].at[pl.ds(to_row, rows), pl.ds(to_column, columns)],
                    sem_out.at[i],
                )
            )
        for copy in copies_in:
            copy.start()
        for i in range(count):
            copies_in[i].wait()
            copies_out[i].start()
        for copy in copies_out:
            copy.wait()

    size = sum(p[4] * p[5] * 2 for p in pieces)
    return pl.pallas_call(
        kernel,
        out_shape=[jax.ShapeDtypeStruct(shape, LOW) for shape in outs],
        in_specs=[pl.BlockSpec(memory_space=pltpu.SMEM)]
        + [pl.BlockSpec(memory_space=pl.ANY)] * n_src,
        out_specs=[pl.BlockSpec(memory_space=pl.ANY)] * n_out,
        scratch_shapes=[pltpu.VMEM((p[4], p[5]), LOW) for p in pieces]
        + [pltpu.SemaphoreType.DMA((count,)), pltpu.SemaphoreType.DMA((count,))],
        compiler_params=pltpu.CompilerParams(vmem_limit_bytes=size + 8 * MIB),
        cost_estimate=pl.CostEstimate(flops=0, bytes_accessed=2 * size, transcendentals=0),
    )(places, *sources)


def place_table(places):
    return jnp.stack([jnp.asarray(p, jnp.int32) for p in places])


def assemble_matrix(own, other, mine, partners, layout, outs, seq, enc):
    n_enc = lax.axis_size("enc")
    core = enc & 1
    sources, pieces, places = [], [], []
    for offsets, half, buffers in ((own, core, mine), (other, 1 - core, partners)):
        for (s_off, e_off), v in zip(offsets, buffers):
            for n, o in enumerate(line_offsets()):
                device = (seq ^ s_off ^ o) * n_enc + (enc ^ e_off)
                for row, column, rows, columns, out, to_row, to_column in layout(device >> 1, half):
                    pieces.append((len(sources), n, row, column, rows, columns, out))
                    places += [to_row, to_column]
            sources.append(v)
    return assemble(sources, pieces, place_table(places), outs)


def assemble_strips(offsets, buffers, count, seq):
    rows, width = buffers[0].shape[1], buffers[0].shape[2] // count
    pieces, places = [], []
    for i, s_off in enumerate(offsets):
        for n, o in enumerate(line_offsets()):
            for k in range(count):
                pieces.append((i, n, 0, k * width, rows, width, k))
                places += [(seq ^ s_off ^ o) * rows, 0]
    total = rows * lax.axis_size("seq")
    return assemble(buffers, pieces, place_table(places), [(total, width)] * count)


def dense(left, right):
    return jnp.dot(left, right, preferred_element_type=F32)


def dense_back(left, right):
    return lax.dot_general(left, right, (((1,), (1,)), ((), ())), preferred_element_type=F32)


def inner_rows(left, right):
    return lax.dot_general(left, right, (((0,), (0,)), ((), ())), preferred_element_type=F32)


def layer_norm(values, gain, shift):
    middle = jnp.mean(values, -1, keepdims=True)
    centred = values - middle
    variance = jnp.mean(centred * centred, -1, keepdims=True)
    return centred * lax.rsqrt(variance + EPSILON) * gain + shift


def norm_start(values, norms, index):
    middle = jnp.mean(values, -1, keepdims=True)
    centred = values - middle
    hat = centred * lax.rsqrt(jnp.mean(centred * centred, -1, keepdims=True) + EPSILON)
    return hat * norms[0, index] + norms[1, index], hat


def adamw(grad, moment, second, weight, rate, decay):
    moment = BETA_FIRST * moment + (1.0 - BETA_FIRST) * grad
    second = BETA_SECOND * second + (1.0 - BETA_SECOND) * grad * grad
    corrected = moment / (1.0 - BETA_FIRST**STEP)
    scale_two = jnp.sqrt(second / (1.0 - BETA_SECOND**STEP))
    return (
        moment,
        second,
        weight - rate * (corrected / (scale_two + ADAM_EPSILON) + decay * weight),
    )


def payload_kernel(n_line, loss_ref, count_ref, *refs):
    zero, three, four, enc, dec = refs[n_line : n_line + 5]
    out_ref, down_ref, up_ref = refs[-3:]
    total = tree_sum([r[...].astype(F32) for r in refs[:n_line]])
    squares = jnp.sum(jnp.sum(total * total, 1, keepdims=True), 0, keepdims=True)
    rows, small = down_ref.shape[1:]
    half = rows // 2
    for k in range(2):
        top, middle, end = k * rows, k * rows + half, (k + 1) * rows
        down_ref[k, :half, :] = total[top:middle, :small]
        down_ref[k, half:, :] = total[top:middle, small:]
        up_ref[k] = total[middle:end]
    rows = [zero, (enc, 0), (enc, 2), three, four, (dec, 0), (dec, 2)]
    for at in range(2):
        for i, row in enumerate(rows):
            ref, first = row if isinstance(row, tuple) else (row, 0)
            out_ref[7 * at + i : 7 * at + i + 1, :] = ref[first + at : first + at + 1, :]
    lane = lax.broadcasted_iota(jnp.int32, (1, out_ref.shape[1]), 1)
    scalars = jnp.where(lane == 2, squares, 0.0)
    scalars = jnp.where(lane == 1, count_ref[...], scalars)
    out_ref[14:15, :] = jnp.where(lane == 0, loss_ref[...], scalars)
    out_ref[15:16, :] = jnp.zeros((1, out_ref.shape[1]), F32)


def payload(loss, count, line, sums, small):
    depth, width = line[0].shape
    rows = depth // 2
    given = [loss.reshape(1, 1), count.reshape(1, 1)] + line + sums
    vmem = pl.BlockSpec(memory_space=pltpu.VMEM)
    return pl.pallas_call(
        lambda *refs: payload_kernel(len(line), *refs),
        out_shape=[
            jax.ShapeDtypeStruct((16, width), F32),
            jax.ShapeDtypeStruct((2, rows, small), F32),
            jax.ShapeDtypeStruct((2, rows // 2, width), F32),
        ],
        in_specs=[vmem] * len(given),
        out_specs=[vmem] * 3,
        cost_estimate=pl.CostEstimate(flops=MIB, bytes_accessed=MIB, transcendentals=0),
    )(*given)


def step_kernel(summed_ref, *refs):
    grads, states, outs = refs[:2], refs[2:8], refs[8:]
    norm_grads = summed_ref[0:14, :]
    loss, count = summed_ref[14:15, 0:1], summed_ref[14:15, 1:2]
    squares = summed_ref[14:15, 2:3] + jnp.sum(
        jnp.sum(norm_grads * norm_grads, 1, keepdims=True), 0, keepdims=True
    )
    norm = jnp.sqrt(squares) / count
    factor = jnp.minimum(1.0, CLIP_NORM / norm) / count
    for ref, value in zip(outs, (loss, count, norm, factor)):
        ref[...] = value
    for i in range(2):
        moment, second, weight = states[3 * i : 3 * i + 3]
        for k in range(2):
            new = adamw(
                grads[i][k] * factor, moment[k], second[k], weight[k], RATE_ADAPTER, DECAY_ADAPTER
            )
            for j in range(3):
                outs[4 + 3 * i + j][k] = new[j]


def optimizer_step(summed, grads, states):
    vmem = pl.BlockSpec(memory_space=pltpu.VMEM)
    given = [summed] + grads + states
    outs = [jax.ShapeDtypeStruct((1, 1), F32)] * 4
    outs += [jax.ShapeDtypeStruct(states[i - i % 3].shape, F32) for i in range(6)]
    results = pl.pallas_call(
        step_kernel,
        out_shape=outs,
        in_specs=[vmem] * len(given),
        out_specs=[vmem] * len(outs),
        cost_estimate=pl.CostEstimate(flops=MIB, bytes_accessed=2 * MIB, transcendentals=0),
    )(*given)
    return [r.reshape(()) for r in results[:4]] + list(results[4:])


def scores_of(left, right):
    return lax.dot_general(left, right, (((1,), (1,)), ((), ())), preferred_element_type=F32)


def head_parts(values):
    side = lax.broadcasted_iota(jnp.int32, values.shape, 1) // HEAD_DIM
    count = values.shape[1] // HEAD_DIM
    return [jnp.where(side == h, values, jnp.zeros((), values.dtype)) for h in range(count)]


def head_join(parts):
    side = lax.broadcasted_iota(jnp.int32, (parts[0].shape[0], 128), 1) // HEAD_DIM
    joined = jnp.broadcast_to(parts[0], side.shape)
    for h in range(1, len(parts)):
        joined = jnp.where(side == h, parts[h], joined)
    return joined


def attend_kernel(limit_ref, spot_ref, q_ref, k_ref, v_ref, *rest):
    context_ref, total_ref = rest[-2:]
    queries = head_parts(q_ref[...] * jnp.asarray(0.125, LOW))
    key, value = k_ref[...], v_ref[...]
    allowed = spot_ref[...] < limit_ref[...]
    raw = [scores_of(query, key) for query in queries]
    contexts, totals = [], []
    for scores in raw:
        scores = jnp.where(allowed, scores, MASKED_SCORE)
        highest = jnp.max(scores, -1, keepdims=True)
        exponent = jnp.exp(scores - highest)
        summed = jnp.sum(exponent, -1, keepdims=True)
        contexts.append(jnp.dot(exponent.astype(LOW), value, preferred_element_type=F32) / summed)
        totals.append(highest + jnp.log(summed))
    context_ref[...] = head_join(contexts).astype(LOW)
    total_ref[...] = head_join(totals)


def attend_specs(rows, length, key_at, value_at, count):
    block = pl.BlockSpec((rows, 128), lambda p, j: (j, p))
    return [
        pl.BlockSpec((rows, 1), lambda p, j: (j, 0)),
        pl.BlockSpec((1, length), lambda p, j: (0, 0)),
        block,
        pl.BlockSpec((length, 128), lambda p, j: (0, key_at + p)),
        pl.BlockSpec((length, 128), lambda p, j: (0, value_at + p)),
    ] + [block] * count


def query_rows(length):
    return 512 if length <= 1024 else 256


def attend(query, keys, key_at, value_at, limit, spots, after=()):
    length = query.shape[0]
    width = keys.shape[1] // (2 if key_at == 0 else 3)
    pairs = width // 128
    rows = query_rows(length)
    block = pl.BlockSpec((rows, 128), lambda p, j: (j, p))
    return pl.pallas_call(
        attend_kernel,
        grid=(pairs, length // rows),
        out_shape=[
            jax.ShapeDtypeStruct((length, width), LOW),
            jax.ShapeDtypeStruct((length, width), F32),
        ],
        in_specs=attend_specs(rows, length, key_at, value_at, 0)
        + [pl.BlockSpec(memory_space=pl.ANY)] * len(after),
        out_specs=[block, block],
        compiler_params=pltpu.CompilerParams(vmem_limit_bytes=56 * MIB),
        cost_estimate=pl.CostEstimate(
            flops=8 * length * length * width,
            bytes_accessed=8 * length * width,
            transcendentals=length * length * width // HEAD_DIM,
        ),
    )(limit, spots, query, keys, keys, *after)


def attend_back_step(limit_ref, spot_ref, q_ref, k_ref, v_ref, grad_ref, total_ref, out_ref, dk_sum, dv_sum):
    pair, step = pl.program_id(0), pl.program_id(1)
    pairs, steps = pl.num_programs(0), pl.num_programs(1)
    rows = q_ref.shape[0]

    @pl.when(step == 0)
    def _():
        dk_sum[...] = jnp.zeros_like(dk_sum)
        dv_sum[...] = jnp.zeros_like(dv_sum)

    queries = head_parts(q_ref[...] * jnp.asarray(0.125, LOW))
    grads = head_parts(grad_ref[...])
    key, value, totals = k_ref[...], v_ref[...], total_ref[...]
    allowed = spot_ref[...] < limit_ref[...]
    raw = [scores_of(query, key) for query in queries]
    grad_softs = [scores_of(grad, value) for grad in grads]
    grad_scores, soft_lows = [], []
    for h, (scores, grad_soft) in enumerate(zip(raw, grad_softs)):
        scores = jnp.where(allowed, scores, MASKED_SCORE)
        soft = jnp.exp(scores - totals[:, h * HEAD_DIM : h * HEAD_DIM + 1])
        weighted = jnp.sum(soft * grad_soft, -1, keepdims=True)
        grad_scores.append((soft * (grad_soft - weighted)).astype(LOW))
        soft_lows.append(soft.astype(LOW))
    dk_sum[...] += inner_rows(jnp.concatenate(grad_scores, 0), jnp.concatenate(queries, 0))
    dv_sum[...] += inner_rows(jnp.concatenate(soft_lows, 0), jnp.concatenate(grads, 0))
    grad_query = head_join([jnp.dot(g, key, preferred_element_type=F32) for g in grad_scores])
    column = pl.multiple_of(pair * 128, 128)
    out_ref[pl.ds(pl.multiple_of(step * rows, rows), rows), pl.ds(column, 128)] = (
        grad_query * 0.125
    ).astype(LOW)

    @pl.when(step == steps - 1)
    def _():
        out_ref[:, pl.ds(pl.multiple_of((pairs + pair) * 128, 128), 128)] = dk_sum[...].astype(LOW)
        out_ref[:, pl.ds(pl.multiple_of((2 * pairs + pair) * 128, 128), 128)] = dv_sum[...].astype(
            LOW
        )


def attend_back_kernel(*refs):
    attend_back_step(*refs[:7], *refs[-3:])


def attend_sums_kernel(n_blocks, *refs):
    *hat_refs, weight_ref, own_hat_ref, own_grad_ref = refs[7 : 10 + n_blocks]
    sums_ref, out_ref, dk_sum, dv_sum, hats, weights, sem = refs[-7:]
    rows = hat_refs[0].shape[0]
    pair, step = pl.program_id(0), pl.program_id(1)
    copies = [
        pltpu.make_async_copy(ref, hats.at[pl.ds(j * rows, rows), :], sem.at[j])
        for j, ref in enumerate(hat_refs)
    ] + [pltpu.make_async_copy(weight_ref, weights, sem.at[n_blocks])]

    @pl.when((pair == 0) & (step == 0))
    def _():
        for copy in copies:
            copy.start()

    attend_back_step(*refs[:7], out_ref, dk_sum, dv_sum)

    @pl.when((pair == pl.num_programs(0) - 1) & (step == pl.num_programs(1) - 1))
    def _():
        for copy in copies:
            copy.wait()
        weight = weights[...]
        length = out_ref.shape[0]
        coming = scores_of(out_ref[:PART, :], weight)
        own = own_grad_ref[...]
        gain = jnp.sum(own * own_hat_ref[...], 0, keepdims=True)
        shift = jnp.sum(own, 0, keepdims=True)
        for start in range(0, length, PART):
            now = coming
            if start + PART < length:
                coming = scores_of(out_ref[start + PART : start + 2 * PART, :], weight)
            gain += jnp.sum(now * hats[start : start + PART, :].astype(F32), 0, keepdims=True)
            shift += jnp.sum(now, 0, keepdims=True)
        sums_ref[0:1, :] = gain
        sums_ref[1:2, :] = shift


def attend_back(
    query, keys, key_at, value_at, limit, spots, grads, totals, sum_with=None, after=()
):
    length, width = grads.shape
    pairs = width // 128
    rows = query_rows(length)
    hbm = pl.BlockSpec(memory_space=pl.ANY)
    scratch = [pltpu.VMEM((length, 128), F32), pltpu.VMEM((length, 128), F32)]
    extra = () if sum_with is None else tuple(sum_with[0]) + tuple(sum_with[1:])
    n_blocks = len(extra) - 3
    if sum_with is None:
        kernel = attend_back_kernel
        out = jax.ShapeDtypeStruct((length, 3 * width), LOW)
    else:

        def kernel(*refs):
            attend_sums_kernel(n_blocks, *refs)

        out = jax.ShapeDtypeStruct((2, extra[0].shape[1]), F32)
        scratch = (
            [pltpu.VMEM((length, 3 * width), LOW)]
            + scratch
            + [pltpu.VMEM((length, extra[0].shape[1]), LOW), pltpu.VMEM(extra[n_blocks].shape, LOW)]
            + [pltpu.SemaphoreType.DMA((n_blocks + 1,))]
        )
    return pl.pallas_call(
        kernel,
        grid=(pairs, length // rows),
        out_shape=out,
        in_specs=attend_specs(rows, length, key_at, value_at, 2)
        + [hbm] * len(extra[:-2])
        + [pl.BlockSpec(v.shape, lambda p, j: (0, 0)) for v in extra[-2:]]
        + [hbm] * len(after),
        out_specs=pl.BlockSpec(out.shape, lambda p, j: (0, 0)),
        scratch_shapes=scratch,
        compiler_params=pltpu.CompilerParams(vmem_limit_bytes=60 * MIB),
        cost_estimate=pl.CostEstimate(
            flops=20 * length * length * width,
            bytes_accessed=16 * length * width,
            transcendentals=length * length * width // HEAD_DIM,
        ),
    )(limit, spots, query, keys, keys, grads, totals, *extra, *after)


def gelu_both(values):
    below = 0.5 * (1.0 + lax.erf(values * 0.7071067811865476))
    bell = jnp.exp(values * values * -0.5) * 0.3989422804014327
    return values * below, below + values * bell


def pack_feed(expand, reduce, down, up):
    rows, width = expand.shape[0], reduce.shape[1]
    parts = [expand[:, q * width : (q + 1) * width] for q in range(4)]
    return jnp.concatenate(
        parts + [reduce, jnp.concatenate([down[: rows // 2], down[rows // 2 :]], 1), up], 0
    )


def gather_feed(expand, reduce, down, up):
    everyone = ("seq", "enc")
    if expand.shape[0] % 32 == 0:
        return lax.all_gather(pack_feed(expand, reduce, down, up), everyone)
    whole = [lax.all_gather(v, everyone, axis=0, tiled=True) for v in (expand, reduce, down, up)]
    return pack_feed(*whole)[None]


def flat(block):
    return block.reshape(block.shape[0] * block.shape[1], block.shape[2])


def adapter_parts(block):
    count, rows, width = block.shape
    half = rows // 2
    down = jnp.stack([block[:, :half, : width // 2], block[:, :half, width // 2 :]], 1)
    return down.reshape(count * rows, width // 2), flat(block[:, half:])


def feed_scratch(packed):
    count, depth, width = packed.shape
    rows = depth // 9
    spread = max(count // 4, 1)
    return (
        [pltpu.VMEM((count, rows, width), LOW) for _ in range(4)]
        + [pltpu.VMEM((spread, width // spread, width), LOW) for _ in range(4)]
        + [pltpu.VMEM((count, rows, width), LOW), pltpu.VMEM((width, width), LOW)]
        + [pltpu.SemaphoreType.DMA((10,))]
    )


def feed_copies(packed_ref, out_ref, scratch):
    *rooms, sem = scratch
    count, depth, width = packed_ref.shape
    rows = depth // 9
    places = [packed_ref.at[:, pl.ds(q * rows, rows), :] for q in range(4)]
    for q in range(4):
        if count >= 4:
            spread = count // 4
            places.append(packed_ref.at[pl.ds(q * spread, spread), pl.ds(4 * rows, 4 * rows), :])
        else:
            places.append(packed_ref.at[:, pl.ds(4 * rows + q * width, width), :])
    places += [packed_ref.at[:, pl.ds(8 * rows, rows), :], out_ref]
    copies = [
        pltpu.make_async_copy(place, room, sem.at[i])
        for i, (place, room) in enumerate(zip(places, rooms))
    ]
    return copies[:4], copies[4:8], copies[8], copies[9]


def norm_stats(values):
    middle = jnp.mean(values, -1, keepdims=True)
    centred = values - middle
    scale = lax.rsqrt(jnp.mean(centred * centred, -1, keepdims=True) + EPSILON)
    return centred * scale, scale


def norm_back(grad, values, gain):
    hat, scale = norm_stats(values)
    scaled = grad * gain
    inner = scaled - jnp.mean(scaled, -1, keepdims=True)
    inner = inner - hat * jnp.mean(scaled * hat, -1, keepdims=True)
    return (
        inner * scale,
        jnp.sum(grad * hat, 0, keepdims=True),
        jnp.sum(grad, 0, keepdims=True),
    )


PART = 256


def branch_kernel(first, n_parts, *refs):
    parts, refs = refs[:n_parts], refs[n_parts:]
    res_ref, norm_ref, packed_ref, proj_ref = refs[:4]
    va_ref, x_ref, slope_ref, act_ref, bend_ref, vb_ref, low_ref = refs[4:11]
    total, slopes, slope_sem = refs[11:14]
    scratch = refs[14:]
    expands, reduces, small, proj = feed_copies(packed_ref, proj_ref, scratch)
    width = res_ref.shape[1]
    for copy in [proj] + [c for pair in zip(expands, reduces) for c in pair] + [small]:
        copy.start()
    proj.wait()
    context = jnp.concatenate([p[...] for p in parts], 1)
    va = res_ref[...] + jnp.dot(context, scratch[9][...], preferred_element_type=F32)
    va_ref[...] = va
    hat, _ = norm_stats(va)
    after = hat * norm_ref[first : first + 1, :] + norm_ref[7 + first : 8 + first, :]
    x = after.astype(LOW)
    x_ref[...] = x
    total[...] = after
    sends = []
    for q in range(4):
        expands[q].wait()
        expand = flat(scratch[q][...])
        pre = jnp.dot(x, expand[:, :PART], preferred_element_type=F32)
        acts = []
        for start in range(0, width, PART):
            now = pre
            if start + PART < width:
                pre = jnp.dot(
                    x, expand[:, start + PART : start + 2 * PART], preferred_element_type=F32
                )
            act, slope = gelu_both(now)
            slopes[q, :, start : start + PART] = slope
            acts.append(act.astype(LOW))
        sends.append(
            pltpu.make_async_copy(
                slopes.at[q], slope_ref.at[:, pl.ds(q * width, width)], slope_sem.at[q]
            )
        )
        sends[q].start()
        reduces[q].wait()
        total[...] += jnp.dot(
            jnp.concatenate(acts, 1), flat(scratch[4 + q][...]), preferred_element_type=F32
        )
    small.wait()
    down, up = adapter_parts(scratch[8][...])
    act, slope = gelu_both(jnp.dot(x, down, preferred_element_type=F32))
    act = act.astype(LOW)
    act_ref[...] = act
    bend_ref[...] = slope
    vb = total[...] + ADAPTER_SCALE * jnp.dot(act, up, preferred_element_type=F32)
    vb_ref[...] = vb
    hat, _ = norm_stats(vb)
    low_ref[...] = (
        hat * norm_ref[first + 1 : first + 2, :] + norm_ref[8 + first : 9 + first, :]
    ).astype(LOW)
    for send in sends:
        send.wait()


def branch(parts, residual, norms, first, packed, proj):
    rows, width = residual.shape
    hidden, small = 4 * width, width // 2
    vmem = pl.BlockSpec(memory_space=pltpu.VMEM)
    hbm = pl.BlockSpec(memory_space=pl.ANY)
    va, x, slope, act, bend, vb, low = pl.pallas_call(
        lambda *refs: branch_kernel(first, len(parts), *refs),
        out_shape=[
            jax.ShapeDtypeStruct((rows, width), F32),
            jax.ShapeDtypeStruct((rows, width), LOW),
            jax.ShapeDtypeStruct((rows, hidden), F32),
            jax.ShapeDtypeStruct((rows, small), LOW),
            jax.ShapeDtypeStruct((rows, small), F32),
            jax.ShapeDtypeStruct((rows, width), F32),
            jax.ShapeDtypeStruct((rows, width), LOW),
        ],
        in_specs=[vmem] * (len(parts) + 2) + [hbm, hbm],
        out_specs=[vmem, vmem, hbm, vmem, vmem, vmem, vmem],
        scratch_shapes=[
            pltpu.VMEM((rows, width), F32),
            pltpu.VMEM((4, rows, width), F32),
            pltpu.SemaphoreType.DMA((4,)),
        ]
        + feed_scratch(packed),
        compiler_params=pltpu.CompilerParams(vmem_limit_bytes=56 * MIB),
        cost_estimate=pl.CostEstimate(
            flops=4 * rows * width * (hidden + small) + 2 * rows * width * width,
            bytes_accessed=4 * width * (hidden + small) + 4 * rows * hidden,
            transcendentals=2 * rows * hidden,
        ),
    )(*parts, residual, norms, packed, proj)
    return low, (va, x, slope, act, bend, vb)


def branch_back_kernel(first, n_parts, *refs):
    n_given, refs = (refs[0], refs[1:])
    given, refs = refs[:n_given], refs[n_given:]
    vb_ref, va_ref, norm_ref, bend_ref, slope_ref, packed_ref, proj_ref = refs[:7]
    dva_ref, sums_ref, dpre_ref, ga_ref = refs[7:11]
    spread_refs, refs = refs[11 : 11 + n_parts], refs[11 + n_parts :]
    total, slopes, slope_sem = refs[:3]
    scratch = refs[3:]
    expands, reduces, small, proj = feed_copies(packed_ref, proj_ref, scratch)
    width = va_ref.shape[1]
    gets = [
        pltpu.make_async_copy(
            slope_ref.at[:, pl.ds(q * width, width)], slopes.at[q], slope_sem.at[q]
        )
        for q in range(4)
    ]
    for copy in [small] + [c for three in zip(reduces, gets, expands) for c in three] + [proj]:
        copy.start()
    if n_given == 2:
        grad = given[0][...].astype(F32) + given[1][...].astype(F32)
    else:
        mean, total_own, other, total_other, label, valid = [r[...] for r in given]
        grad = merge_means((mean, total_own), (other, total_other))[0]
        grad = (grad - label.astype(F32)) * valid
    grad_out, gain, shift = norm_back(grad, vb_ref[...], norm_ref[first + 1 : first + 2, :])
    sums_ref[2:3, :] = gain
    sums_ref[3:4, :] = shift
    g = grad_out.astype(LOW)
    ga = (ADAPTER_SCALE * grad_out).astype(LOW)
    ga_ref[...] = ga
    small.wait()
    down, up = adapter_parts(scratch[8][...])
    pre = (dense_back(ga, up) * bend_ref[...]).astype(LOW)
    dpre_ref[...] = pre
    total[...] = grad_out + dense_back(pre, down)
    for q in range(4):
        reduces[q].wait()
        reduce = flat(scratch[4 + q][...])
        gets[q].wait()
        grad = dense_back(g, reduce[:PART])
        pres = []
        for start in range(0, width, PART):
            now = grad
            if start + PART < width:
                grad = dense_back(g, reduce[start + PART : start + 2 * PART])
            pres.append((now * slopes[q, :, start : start + PART]).astype(LOW))
        expands[q].wait()
        total[...] += dense_back(jnp.concatenate(pres, 1), flat(scratch[q][...]))
    dva, gain, shift = norm_back(total[...], va_ref[...], norm_ref[first : first + 1, :])
    sums_ref[0:1, :] = gain
    sums_ref[1:2, :] = shift
    dva_ref[...] = dva
    proj.wait()
    spread = dense_back(dva.astype(LOW), scratch[9][...]).astype(LOW)
    share = width // n_parts
    for j in range(n_parts):
        spread_refs[j][...] = spread[:, j * share : (j + 1) * share]


def branch_back(given, kept, norms, first, packed, proj, n_parts):
    va, x, slope, act, bend, vb = kept
    rows, width = va.shape
    hidden, small = 4 * width, width // 2
    vmem = pl.BlockSpec(memory_space=pltpu.VMEM)
    hbm = pl.BlockSpec(memory_space=pl.ANY)
    dva, sums, dpre, ga, *spread = pl.pallas_call(
        lambda *refs: branch_back_kernel(first, n_parts, len(given), *refs),
        out_shape=[
            jax.ShapeDtypeStruct((rows, width), F32),
            jax.ShapeDtypeStruct((4, width), F32),
            jax.ShapeDtypeStruct((rows, small), LOW),
            jax.ShapeDtypeStruct((rows, width), LOW),
        ]
        + [jax.ShapeDtypeStruct((rows, width // n_parts), LOW)] * n_parts,
        in_specs=[vmem] * (4 + len(given)) + [hbm] * 3,
        out_specs=[vmem] * (4 + n_parts),
        scratch_shapes=[
            pltpu.VMEM((rows, width), F32),
            pltpu.VMEM((4, rows, width), F32),
            pltpu.SemaphoreType.DMA((4,)),
        ]
        + feed_scratch(packed),
        compiler_params=pltpu.CompilerParams(vmem_limit_bytes=56 * MIB),
        cost_estimate=pl.CostEstimate(
            flops=4 * rows * width * (hidden + small) + 2 * rows * width * width,
            bytes_accessed=4 * width * (hidden + small) + 4 * rows * hidden,
            transcendentals=0,
        ),
    )(*given, vb, va, norms, bend, slope, packed, proj)
    return dva, spread, sums, (x, dpre, act, ga)


def middle_back_kernel(first, n_parts, *refs):
    res_ref, own_ref, far_ref, va_ref, norm_ref, proj_ref = refs[:6]
    dva_ref, sums_ref = refs[6:8]
    grad = res_ref[...] + own_ref[...].astype(F32) + far_ref[...].astype(F32)
    dva, gain, shift = norm_back(grad, va_ref[...], norm_ref[first : first + 1, :])
    dva_ref[...] = dva
    sums_ref[0:1, :] = gain
    sums_ref[1:2, :] = shift
    spread = dense_back(dva.astype(LOW), proj_ref[...]).astype(LOW)
    share = spread.shape[1] // n_parts
    for j in range(n_parts):
        refs[8 + j][...] = spread[:, j * share : (j + 1) * share]


def middle_back(residual, own, far, va, norms, first, proj, n_parts):
    rows, width = va.shape
    vmem = pl.BlockSpec(memory_space=pltpu.VMEM)
    dva, sums, *spread = pl.pallas_call(
        lambda *refs: middle_back_kernel(first, n_parts, *refs),
        out_shape=[
            jax.ShapeDtypeStruct((rows, width), F32),
            jax.ShapeDtypeStruct((2, width), F32),
        ]
        + [jax.ShapeDtypeStruct((rows, width // n_parts), LOW)] * n_parts,
        in_specs=[vmem] * 6,
        out_specs=[vmem] * (2 + n_parts),
        compiler_params=pltpu.CompilerParams(vmem_limit_bytes=32 * MIB),
        cost_estimate=pl.CostEstimate(
            flops=0, bytes_accessed=0, transcendentals=0
        ),
    )(residual, own, far, va, norms, proj)
    return dva, spread, sums


def adapter_grad_kernel(core_ref, *refs):
    given, refs = refs[:8], refs[8:]
    keep_ref, send_ref = refs[:2]
    rooms, (down, up, keep, send, sem, sem_out) = refs[2:10], refs[10:]
    copies = [pltpu.make_async_copy(g, r, sem.at[i]) for i, (g, r) in enumerate(zip(given, rooms))]
    for copy in copies:
        copy.start()
    core = core_ref[0]
    pairs, depth, width = keep.shape
    rows = depth // 2
    half, small = rows // 2, width // 2
    for k in range(2):
        for copy in copies[4 * k : 4 * k + 4]:
            copy.wait()
        x, dpre, act, ga = rooms[4 * k : 4 * k + 4]
        down[...] = inner_rows(x[...], dpre[...])
        up[...] = inner_rows(act[...], ga[...])
        top, middle, end = k * rows, k * rows + half, (k + 1) * rows
        for ref, side in ((send, 1 - core), (keep, core)):
            for pair in range(pairs):
                device = 2 * pair + side
                at = pl.multiple_of(device * rows, rows)
                ref[pair, top:middle, :small] = down[pl.ds(at, half), :].astype(LOW)
                ref[pair, top:middle, small:] = down[pl.ds(at + half, half), :].astype(LOW)
                ref[pair, middle:end, :] = up[
                    pl.ds(pl.multiple_of(device * half, half), half), :
                ].astype(LOW)
    outs = [
        pltpu.make_async_copy(send, send_ref, sem_out.at[0]),
        pltpu.make_async_copy(keep, keep_ref, sem_out.at[1]),
    ]
    for copy in outs:
        copy.start()
    for copy in outs:
        copy.wait()


def adapter_grads(given, core):
    width, small = given[0][0].shape[1], given[0][1].shape[1]
    n_all = lax.axis_size("seq") * lax.axis_size("enc")
    rows = width // n_all
    if rows % 16:
        layers = []
        for x, dpre, act, ga in given:
            down, up = inner_rows(x, dpre), inner_rows(act, ga)
            folded = down.reshape(n_all, 2, rows // 2, small).transpose(0, 2, 1, 3)
            layers += [folded.reshape(n_all, rows // 2, width), up.reshape(n_all, rows // 2, width)]
        both = jnp.concatenate(layers, 1).reshape(n_all // 2, 2, 2 * rows, width)
        first = core == 0
        keep, send = jnp.where(first, both[:, 0], both[:, 1]), jnp.where(first, both[:, 1], both[:, 0])
        return keep.astype(LOW), send.astype(LOW)
    shape = (n_all // 2, 2 * rows, width)
    hbm = pl.BlockSpec(memory_space=pl.ANY)
    loads = list(given[0]) + list(given[1])
    return pl.pallas_call(
        adapter_grad_kernel,
        out_shape=[jax.ShapeDtypeStruct(shape, LOW)] * 2,
        in_specs=[pl.BlockSpec(memory_space=pltpu.SMEM)] + [hbm] * 8,
        out_specs=[hbm] * 2,
        scratch_shapes=[pltpu.VMEM(v.shape, LOW) for v in loads]
        + [pltpu.VMEM((width, small), F32), pltpu.VMEM((small, width), F32)]
        + [pltpu.VMEM(shape, LOW), pltpu.VMEM(shape, LOW)]
        + [pltpu.SemaphoreType.DMA((8,)), pltpu.SemaphoreType.DMA((2,))],
        compiler_params=pltpu.CompilerParams(vmem_limit_bytes=60 * MIB),
        cost_estimate=pl.CostEstimate(flops=0, bytes_accessed=0, transcendentals=0),
    )(core.reshape(1).astype(jnp.int32), *loads)


def head_kernel(n_blocks, *refs):
    o_refs, e_ref = refs[:n_blocks], refs[n_blocks]
    g_refs, lse_refs = refs[n_blocks + 1 : 2 * n_blocks + 1], refs[2 * n_blocks + 1 : -3]
    acc, peak, mass = refs[-3:]
    step = pl.program_id(0)
    rows = o_refs[0].shape[0]
    part = 2 * rows

    @pl.when(step == 0)
    def _():
        acc[...] = jnp.zeros_like(acc)
        peak[...] = jnp.full_like(peak, -1e30)
        mass[...] = jnp.zeros_like(mass)

    table = e_ref[...]
    spans = [pl.ds(start, part) for start in range(0, n_blocks * rows, part)]

    def logits_of(h):
        both = jnp.concatenate([o_refs[2 * h][...], o_refs[2 * h + 1][...]], 0)
        return scores_of(both, table)

    before = [peak[at, :1] for at in spans]
    held = [mass[at, :] for at in spans]
    coming = logits_of(0)
    highest, summed = [], []
    for h, at in enumerate(spans):
        logits = coming
        if h + 1 < len(spans):
            coming = logits_of(h + 1)
        highest.append(jnp.maximum(before[h], jnp.max(logits, -1, keepdims=True)))
        exponent = jnp.exp(logits - highest[h])
        fade = jnp.exp(before[h] - highest[h])
        summed.append(held[h] * fade + jnp.sum(exponent, -1, keepdims=True))
        acc[at, :] = acc[at, :] * fade + jnp.dot(
            exponent.astype(LOW), table, preferred_element_type=F32
        )
    for h, at in enumerate(spans):
        mass[at, :] = summed[h]
        peak[at, :] = jnp.broadcast_to(highest[h], (part, 128))

    @pl.when(step == pl.num_programs(0) - 1)
    def _():
        for j in range(n_blocks):
            at = pl.ds(j * rows, rows)
            g_refs[j][...] = (acc[at, :] / mass[at, :1]).astype(LOW)
            lse_refs[j][...] = peak[at, :1] + jnp.log(mass[at, :1])


def head(blocks, table):
    rows, width = blocks[0].shape
    count = len(blocks)
    entries = table.shape[0]
    tile = next(t for t in (1280, 1024, 640, 512, 256, 128) if entries % t == 0)
    block = pl.BlockSpec((rows, width), lambda j: (0, 0))
    results = pl.pallas_call(
        lambda *refs: head_kernel(count, *refs),
        grid=(entries // tile,),
        out_shape=[jax.ShapeDtypeStruct((rows, width), LOW)] * count
        + [jax.ShapeDtypeStruct((rows, 1), F32)] * count,
        in_specs=[block] * count + [pl.BlockSpec((tile, width), lambda j: (j, 0))],
        out_specs=[block] * count + [pl.BlockSpec((rows, 1), lambda j: (0, 0))] * count,
        scratch_shapes=[
            pltpu.VMEM((count * rows, width), F32),
            pltpu.VMEM((count * rows, 128), F32),
            pltpu.VMEM((count * rows, 128), F32),
        ],
        compiler_params=pltpu.CompilerParams(vmem_limit_bytes=60 * MIB),
        cost_estimate=pl.CostEstimate(
            flops=4 * count * rows * width * entries,
            bytes_accessed=2 * width * entries,
            transcendentals=count * rows * entries,
        ),
    )(*blocks, table)
    return list(results[:count]), list(results[count:])


def adapters_plane(keep, came, seq, enc):
    n_seq, n_enc = lax.axis_size("seq"), lax.axis_size("enc")
    near = n_seq // 4
    rows, width = keep.shape[1:]

    def block(s_off, e_off):
        start = (0, (seq & (near - 1)) ^ s_off, (enc >> 1) ^ (e_off >> 1), 0, 0)
        parts = [v.reshape(4, near, n_enc // 2, rows, width) for v in (keep, came)]
        parts = [lax.dynamic_slice(v, start, (4, 1, 1, rows, width))[:, 0, 0] for v in parts]
        return parts[0].astype(F32) + parts[1].astype(F32)

    return [block(0, 0)] + [flip_both(block(s, e).astype(LOW), s, e) for s, e in plane_offsets()[1:]]


def adapters_line(parts, seq):
    held = tree_sum([p.astype(F32) for p in parts])
    slow = seq // (lax.axis_size("seq") // 4)
    parts = [lax.dynamic_index_in_dim(held, slow ^ k, 0, keepdims=False) for k in range(4)]
    return parts[:1] + [
        flip(p.astype(LOW), "seq", o) for p, o in zip(parts[1:], line_offsets()[1:])
    ]


def sum_everywhere(values):
    values = values + flip(values, "enc", 1)
    values = tree_sum([values] + [flip_both(values, s, e) for s, e in plane_offsets()[1:]])
    return tree_sum([values] + [flip(values, "seq", o) for o in line_offsets()[1:]])


def shards(
    source_ids,
    target_ids,
    labels,
    lengths,
    embedding,
    positions,
    attention_in,
    attention_out,
    feed_in,
    feed_out,
    adapter_down,
    adapter_up,
    norm_params,
    down_moment,
    down_second,
    up_moment,
    up_second,
    norm_moment,
    norm_second,
):
    n_seq, n_enc = lax.axis_size("seq"), lax.axis_size("enc")
    n_all = n_seq * n_enc
    seq, enc = lax.axis_index("seq"), lax.axis_index("enc")
    core = enc & 1
    own_rows = source_ids.shape[1]
    width = embedding.shape[1]
    entries = embedding.shape[0]
    length = own_rows * n_enc
    share = width // n_enc
    source_length, target_length = lengths[0, 0], lengths[0, 1]

    blocks = jnp.arange(n_enc) ^ enc
    spots = (blocks[:, None] * own_rows + jnp.arange(own_rows)[None, :]).reshape(length)
    spots = spots.astype(jnp.int32)
    source_limit = jnp.broadcast_to(source_length, (length, 1)).astype(jnp.int32)
    causal_limit = jnp.minimum(spots + 1, target_length)[:, None].astype(jnp.int32)
    spots = spots[None, :]
    in_strip = share // 128

    def gather_rows(rows_low):
        return jnp.concatenate(gather_enc(rows_low), 0)

    def lookup(ids):
        inside = (ids >= 0) & (ids < entries)
        found = jnp.take(embedding, jnp.clip(ids, 0, entries - 1), axis=0)
        return jnp.where(inside[:, :, None], found, jnp.zeros((), LOW))

    def rows_of(found):
        return scatter_enc([found[j] for j in range(n_enc)])

    def own_parts(context):
        return swap_blocks([context[j * own_rows : (j + 1) * own_rows] for j in range(n_enc)])

    def all_heads(spread):
        return jnp.concatenate(swap_blocks(spread), 0)

    def row_blocks(partial):
        return [partial[j * own_rows : (j + 1) * own_rows] for j in range(n_enc)]

    down_low, up_low = adapter_down.astype(LOW), adapter_up.astype(LOW)
    feeds = [gather_feed(feed_in[k], feed_out[k], down_low[k], up_low[k]) for k in range(2)]

    gains = norm_params.astype(LOW).astype(F32)
    ids = jnp.concatenate([source_ids, target_ids, labels], 0).astype(F32)
    small_own = jnp.concatenate([ids.reshape(1, -1), gains.reshape(1, -1)], 1)
    small_all = unxor([v[0] for v in jnp.split(lax.all_gather(small_own, "enc"), n_enc)], enc)
    small_all = jnp.concatenate(small_all, 0)
    all_ids = small_all[:, : 3 * own_rows].astype(jnp.int32).reshape(n_enc, 3, own_rows)
    all_ids = all_ids - enc * entries
    gains = small_all[:, 3 * own_rows :].astype(LOW)[None]

    triple = attention_in.reshape(3, -1, 3, n_enc, share).transpose(3, 1, 0, 2, 4)
    shard_rows = triple.shape[1]
    strip_rows, pair_rows = n_enc * shard_rows, 2 * shard_rows
    triple = triple.reshape(n_enc, shard_rows, 9 * share)
    strip = lax.all_to_all(triple, "enc", 0, 0, tiled=True).reshape(strip_rows, 9 * share)
    strip, late = strip[:, : 6 * share], strip[:, 6 * share :]
    half = width // 2
    packed = jnp.concatenate(
        [attention_out[k][:, h * half : (h + 1) * half] for h in range(2) for k in range(3)], 1
    )
    pair_out = pair_split(packed, core)

    ids = [all_ids[:, k] for k in range(3)]
    strip, pair_out, *ids = gate([strip, pair_out] + ids)

    slow, slow_out = slow_flips_both(strip, pair_out)
    for mask in bits("seq"):
        gains = jnp.concatenate([gains, flip(gains, "seq", mask)], 0)
    arrived = gate([lookup(v) for v in ids] + slow + (slow_out or []))
    found, slow, slow_out = arrived[:3], arrived[3:6], arrived[6:]
    if not slow_out:
        slow_out = [v[strip_rows:] for v in slow]
        slow = [v[:strip_rows] for v in slow]
    order_seq, order_enc = jnp.arange(n_seq) ^ seq, jnp.arange(n_enc) ^ enc
    gains = jnp.take(jnp.take(gains, order_seq, axis=0), order_enc, axis=1)
    gains = gains.reshape(n_all, 14, width // n_all).transpose(1, 0, 2)
    norms = gains.reshape(2, 7, width).astype(F32)

    strip_offsets, strips = near_flips(jnp.stack([strip] + slow))
    source_rows, target_rows = rows_of(found[0]), rows_of(found[1])

    in_enc, in_dec = assemble_strips(strip_offsets, strips, 2, seq)
    encoder_in, encoder_hat = norm_start(source_rows + positions[0].astype(F32), norms, 0)
    decoder_in, decoder_hat = norm_start(target_rows + positions[1].astype(F32), norms, 3)
    across = gather_across(encoder_in.astype(LOW))
    decoder_low, *across[1:] = gate([decoder_in.astype(LOW)] + across[1:])
    encoder_all = jnp.concatenate(gather_pair(across), 0)
    decoder_all = gather_rows(decoder_low)
    stacked = jnp.stack([pair_out] + slow_out)
    singles = plane_start(stacked)

    triple_encoder = dense(encoder_all, in_enc).astype(LOW)
    enc_args = (triple_encoder, triple_encoder, in_strip, 2 * in_strip, source_limit, spots)
    context_enc, total_encoder = attend(*enc_args)
    slow = slow_flips(late)
    context_enc, *arrived = gate([context_enc] + slow + singles)
    slow, singles = arrived[:3], arrived[3:]
    own, other, mine = plane_finish(stacked, singles, core)
    partners = [flip(v, "enc", 1) for v in mine]
    triple_decoder = dense(decoder_all, in_dec).astype(LOW)
    dec_args = (triple_decoder, triple_decoder, in_strip, 2 * in_strip, causal_limit, spots)
    context_dec, total_decoder = attend(*dec_args, after=[context_enc])

    def out_layout(pair, side):
        row = pair * pair_rows
        block = (row // share) ^ enc
        return [
            (0, k * half, pair_rows, half, k, block * share + row % share, side * half)
            for k in range(3)
        ]

    attend_out = assemble_matrix(
        own, other, mine, partners, out_layout, [(width, width)] * 3, seq, enc
    )
    late_offsets, strips = near_flips(jnp.stack([late] + slow))
    attended = dense(jnp.concatenate(own_parts(context_dec), 1), attend_out[1])
    causal_in = decoder_in + attended
    after_causal = norm_start(causal_in, norms, 4)[0]
    in_cross = assemble_strips(late_offsets, strips, 1, seq)[0]
    attend_in = [in_enc, in_dec, in_cross]
    causal_all = gather_rows(after_causal.astype(LOW))
    norm_rows = norms.reshape(14, width)
    encoded_low, kept_enc = branch(
        own_parts(context_enc), encoder_in, norm_rows, 1, feeds[0], attend_out[0]
    )
    query_cross = dense(causal_all, in_cross[:, :share]).astype(LOW)

    encoded_all = gather_rows(encoded_low)
    pairs_cross = dense(encoded_all, in_cross[:, share:]).astype(LOW)
    cross_args = (query_cross, pairs_cross, 0, in_strip, source_limit, spots)
    context, total_cross = attend(*cross_args)
    context, found_label = gate([context, found[2]])
    label_rows, label_came = scatter_two([found_label[j] for j in range(n_enc)])
    decoded_low, kept_dec = branch(
        own_parts(context), after_causal, norm_rows, 5, feeds[1], attend_out[2]
    )

    decoded_low, label_came = gate([decoded_low, label_came])

    *decoded_all, encoder_low, decoder_low = gate(
        gather_enc(decoded_low) + [encoder_hat.astype(LOW), decoder_hat.astype(LOW)]
    )
    pulled, totals = head(decoded_all, embedding)
    hats = gather_across(encoder_low) + gather_across(decoder_low)
    *results, decoded_low, label_came = gate(
        pulled + totals + hats + [decoded_all[0], label_came]
    )
    pulled, totals, hats = results[:n_enc], results[n_enc : 2 * n_enc], results[2 * n_enc :]
    label_rows = (label_rows.astype(F32) + label_came.astype(F32)).astype(LOW)
    row_spots = enc * own_rows + jnp.arange(own_rows)
    valid = (row_spots < target_length).astype(F32)[:, None]
    picked = jnp.sum(decoded_low.astype(F32) * label_rows.astype(F32), -1, keepdims=True)
    own_mean, far_mean, hats = merge_enc(pulled, totals, hats)
    half_hats = len(hats) // 2
    hats = gather_pair(hats[:half_hats]) + gather_pair(hats[half_hats:])
    far, *hats = gate([far_mean[0]] + hats)
    encoder_hats, decoder_hats = hats[:n_enc], hats[n_enc:]
    highest = jnp.maximum(own_mean[1], far_mean[1])
    log_total = highest + jnp.log(
        jnp.exp(own_mean[1] - highest) + jnp.exp(far_mean[1] - highest)
    )
    loss_own = jnp.sum((log_total - picked) * valid)

    grad_res, spread, sums_dec, given_dec = branch_back(
        [own_mean[0], own_mean[1], far, far_mean[1], label_rows, valid],
        kept_dec,
        norm_rows,
        5,
        feeds[1],
        attend_out[2],
        n_enc,
    )
    grads = attend_back(*cross_args, all_heads(spread), total_cross)
    own_encoded, far_encoded = scatter_two(
        row_blocks(dense_back(grads[:, share:], attend_in[2][:, share:]))
    )
    own_causal, far_causal = scatter_two(
        row_blocks(dense_back(grads[:, :share], attend_in[2][:, :share]))
    )
    grad_enc, spread, sums_enc, given_enc = branch_back(
        [own_encoded, far_encoded], kept_enc, norm_rows, 1, feeds[0], attend_out[0], n_enc
    )
    spread = swap_blocks(spread)
    x, dpre, act, ga = given_enc
    dpre, far_causal = gate([dpre, far_causal])
    keep, send = adapter_grads([(x, dpre, act, ga), given_dec], core)
    came = flip(send, "enc", 1)
    grad_dec, spread_dec, sums_four = middle_back(
        grad_res, own_causal, far_causal, causal_in, norm_rows, 4, attend_out[1], n_enc
    )
    sums_zero = attend_back(
        *enc_args,
        jnp.concatenate(spread, 0),
        total_encoder,
        sum_with=(encoder_hats, in_enc, encoder_hat, grad_enc),
        after=[grad_dec],
    )
    parts = adapters_plane(keep, came, seq, enc)
    sums_zero, *parts[1:] = gate([sums_zero] + parts[1:])
    parts = adapters_line(parts, seq)
    sums_three = attend_back(
        *dec_args,
        all_heads(spread_dec),
        total_decoder,
        sum_with=(decoder_hats, in_dec, decoder_hat, grad_dec),
        after=[sums_zero],
    )
    sums_three, *parts[1:] = gate([sums_three] + parts[1:])

    count_own = jnp.clip(target_length - enc * own_rows, 0, own_rows).astype(F32)
    summed, grad_down, grad_up = payload(
        loss_own,
        count_own,
        parts,
        [sums_zero, sums_three, sums_four, sums_enc, sums_dec],
        adapter_down.shape[2],
    )
    summed = sum_everywhere(summed)
    per = width // n_all
    own = lax.dynamic_slice_in_dim(summed, (seq * n_enc + enc) * per, per, 1)[:14]
    loss_sum, token_total, grad_norm, factor, *adapters = optimizer_step(
        summed,
        [grad_down, grad_up],
        [down_moment, down_second, adapter_down, up_moment, up_second, adapter_up],
    )
    new_norms = adamw(
        own.reshape(2, 7, per) * factor, norm_moment, norm_second, norm_params, RATE_NORMS, 0.0
    )
    return (loss_sum, token_total, grad_norm, *adapters, *new_norms)


def solution(mesh):
    everywhere = P(None, ("seq", "enc"), None)
    columns = P(None, None, ("seq", "enc"))
    return jax.shard_map(
        shards,
        mesh=mesh,
        in_specs=(
            P("seq", "enc"),
            P("seq", "enc"),
            P("seq", "enc"),
            P("seq", None),
            P("enc", None),
            P(None, "enc", None),
            everywhere,
            everywhere,
            everywhere,
            everywhere,
            everywhere,
            everywhere,
            columns,
            everywhere,
            everywhere,
            everywhere,
            everywhere,
            columns,
            columns,
        ),
        out_specs=(
            P(),
            P(),
            P(),
            everywhere,
            everywhere,
            everywhere,
            everywhere,
            everywhere,
            everywhere,
            columns,
            columns,
            columns,
        ),
        check_vma=False,
    )
```

```python
import jax
import jax.numpy as jnp
from jax import lax
from jax.experimental import pallas as pl
from jax.experimental.pallas import tpu as pltpu
from jax.sharding import PartitionSpec as P

HEAD_DIM = 64
STEP = 10

EPSILON = 1e-05
ADAPTER_SCALE = 4.0
CLIP_NORM = 0.25
RATE_ADAPTER = 0.05
RATE_NORMS = 0.5
BETA_FIRST = 0.9
BETA_SECOND = 0.999
ADAM_EPSILON = 1e-08
DECAY_ADAPTER = 0.01
MASKED_SCORE = -1000000000.0

LOW = jnp.bfloat16
F32 = jnp.float32
MIB = 1024 * 1024


def flip(value, axis, mask):
    count = lax.axis_size(axis)
    return lax.ppermute(value, axis, [(i, i ^ mask) for i in range(count)])


def bits(axis):
    count = lax.axis_size(axis)
    return [1 << i for i in range(count.bit_length() - 1)]


def unxor(blocks, me):
    blocks = list(blocks)
    mask = 1
    while mask < len(blocks):
        bit = (me & mask) != 0
        blocks = [jnp.where(bit, blocks[i ^ mask], blocks[i]) for i in range(len(blocks))]
        mask *= 2
    return blocks


def gather_across(value):
    found = {0: value}
    for mask in bits("enc")[1:]:
        found.update({j | mask: flip(v, "enc", mask) for j, v in list(found.items())})
    return [found[j] for j in sorted(found)]


def gather_pair(blocks):
    return [v for block in blocks for v in (block, flip(block, "enc", 1))]


def gather_enc(value):
    return gather_pair(gather_across(value))


def scatter_two(blocks):
    held = dict(enumerate(blocks))
    for mask in bits("enc"):
        away = [j for j in held if j & mask]
        sent = [flip(held[j].astype(LOW), "enc", mask) for j in away]
        for j, part in zip(away, sent):
            if len(held) == 2:
                return held[j ^ mask], part
            held[j ^ mask] = held[j ^ mask].astype(F32) + part.astype(F32)
            del held[j]


def scatter_enc(blocks):
    own, came = scatter_two(blocks)
    return own.astype(F32) + came.astype(F32)


def merge_means(first, second):
    (mean, total), (other, other_total) = first, second
    highest = jnp.maximum(total, other_total)
    own, far = jnp.exp(total - highest), jnp.exp(other_total - highest)
    both = own + far
    return (mean.astype(F32) * own + other.astype(F32) * far) / both, highest + jnp.log(both)


def merge_enc(blocks, totals, beside):
    held = {j: (b, t) for j, (b, t) in enumerate(zip(blocks, totals))}
    for mask in bits("enc"):
        away = [j for j in held if j & mask]
        means = [held[j][0].astype(LOW) for j in away]
        if len(held) == 2:
            means[0], *beside = gate([means[0]] + beside)
        sent = [(flip(m, "enc", mask), flip(held[j][1], "enc", mask)) for j, m in zip(away, means)]
        for j, came in zip(away, sent):
            if len(held) == 2:
                return held[j ^ mask], came, beside
            held[j ^ mask] = merge_means(held[j ^ mask], came)
            del held[j]


def swap_blocks(blocks):
    return [blocks[0]] + [flip(blocks[j], "enc", j) for j in range(1, len(blocks))]


def pair_split(shard, core):
    half = shard.shape[1] // 2
    first = core == 0
    low, high = shard[:, :half], shard[:, half:]
    keep = jnp.where(first, low, high)
    came = flip(jnp.where(first, high, low), "enc", 1)
    return jnp.concatenate([jnp.where(first, keep, came), jnp.where(first, came, keep)], 0)


def gate(arrays):
    def kernel(*refs):
        pass

    results = pl.pallas_call(
        kernel,
        out_shape=[jax.ShapeDtypeStruct(v.shape, v.dtype) for v in arrays],
        in_specs=[pl.BlockSpec(memory_space=pl.ANY)] * len(arrays),
        out_specs=[pl.BlockSpec(memory_space=pl.ANY)] * len(arrays),
        input_output_aliases={i: i for i in range(len(arrays))},
        compiler_params=pltpu.CompilerParams(vmem_limit_bytes=60 * MIB),
        cost_estimate=pl.CostEstimate(flops=0, bytes_accessed=0, transcendentals=0),
    )(*arrays)
    return list(results)


def flip_both(value, seq_mask, enc_mask):
    n_enc = lax.axis_size("enc")
    perm = []
    for i in range(lax.axis_size("seq") * n_enc):
        s, e = divmod(i, n_enc)
        perm.append((i, (s ^ seq_mask) * n_enc + (e ^ enc_mask)))
    return lax.ppermute(value, ("seq", "enc"), perm)


def tree_sum(values):
    values = list(values)
    while len(values) > 1:
        values = [values[i] + values[i + 1] for i in range(0, len(values), 2)]
    return values[0]


def plane_offsets():
    near = lax.axis_size("seq") // 4
    return [(s, e) for e in range(0, lax.axis_size("enc"), 2) for s in range(near)]


def line_offsets():
    return [k * (lax.axis_size("seq") // 4) for k in range(4)]


def mixed_flip(value, for_even, for_odd):
    n_enc = lax.axis_size("enc")
    perm = []
    for i in range(lax.axis_size("seq") * n_enc):
        s, e = divmod(i, n_enc)
        axis, mask = for_odd if e & 1 else for_even
        perm.append((i, (s ^ mask) * n_enc + e if axis == "seq" else s * n_enc + (e ^ mask)))
    return lax.ppermute(value, ("seq", "enc"), perm)


def near_bits():
    return [("seq", mask) for mask in bits("seq") if mask < lax.axis_size("seq") // 4]


def across_bits():
    return [("enc", mask) for mask in bits("enc")[1:]]


def moved(offset, step):
    return (offset[0] ^ step[1], offset[1]) if step[0] == "seq" else (offset[0], offset[1] ^ step[1])


def slow_flips(value):
    return [flip(value, "seq", o) for o in line_offsets()[1:]]


def slow_flips_both(first, second):
    if first.shape[1] != second.shape[1]:
        return slow_flips(first), slow_flips(second)
    return slow_flips(jnp.concatenate([first, second], 0)), None


def plane_steps():
    return list(zip(near_bits() + across_bits(), across_bits() + near_bits()))


def plane_start(stacked):
    return [mixed_flip(stacked, *step) for step in plane_steps()]


def plane_finish(stacked, singles, core):
    found = [((0, 0), (0, 0), stacked)]
    for step, single in zip(plane_steps(), singles):
        fresh = [(moved((0, 0), step[0]), moved((0, 0), step[1]), single)]
        fresh += [
            (moved(o, step[0]), moved(p, step[1]), mixed_flip(v, *step)) for o, p, v in found[1:]
        ]
        found += fresh
    own = [tuple(jnp.where(core == 0, i, k) for i, k in zip(o, p)) for o, p, _ in found]
    other = [tuple(jnp.where(core == 0, k, i) for i, k in zip(o, p)) for o, p, _ in found]
    return own, other, [v for _, _, v in found]


def near_flips(stacked):
    found = [(0, stacked)]
    for _, mask in near_bits():
        found += [(o ^ mask, flip(v, "seq", mask)) for o, v in found]
    return [o for o, _ in found], [v for _, v in found]


def assemble(sources, pieces, places, outs):
    count = len(pieces)
    n_src, n_out = len(sources), len(outs)

    def kernel(*refs):
        table = refs[0]
        given = refs[1 : 1 + n_src]
        results = refs[1 + n_src : 1 + n_src + n_out]
        stage = refs[1 + n_src + n_out : 1 + n_src + n_out + count]
        sem_in, sem_out = refs[-2:]
        copies_in, copies_out = [], []
        for i, (src, block, row, column, rows, columns, out) in enumerate(pieces):
            copies_in.append(
                pltpu.make_async_copy(
                    given[src].at[block, pl.ds(row, rows), pl.ds(column, columns)],
                    stage[i],
                    sem_in.at[i],
                )
            )
            to_row = pl.multiple_of(table[2 * i], rows)
            to_column = pl.multiple_of(table[2 * i + 1], columns)
            copies_out.append(
                pltpu.make_async_copy(
                    stage[i],
                    results[out].at[pl.ds(to_row, rows), pl.ds(to_column, columns)],
                    sem_out.at[i],
                )
            )
        for copy in copies_in:
            copy.start()
        for i in range(count):
            copies_in[i].wait()
            copies_out[i].start()
        for copy in copies_out:
            copy.wait()

    size = sum(p[4] * p[5] * 2 for p in pieces)
    return pl.pallas_call(
        kernel,
        out_shape=[jax.ShapeDtypeStruct(shape, LOW) for shape in outs],
        in_specs=[pl.BlockSpec(memory_space=pltpu.SMEM)]
        + [pl.BlockSpec(memory_space=pl.ANY)] * n_src,
        out_specs=[pl.BlockSpec(memory_space=pl.ANY)] * n_out,
        scratch_shapes=[pltpu.VMEM((p[4], p[5]), LOW) for p in pieces]
        + [pltpu.SemaphoreType.DMA((count,)), pltpu.SemaphoreType.DMA((count,))],
        compiler_params=pltpu.CompilerParams(vmem_limit_bytes=size + 8 * MIB),
        cost_estimate=pl.CostEstimate(flops=0, bytes_accessed=2 * size, transcendentals=0),
    )(places, *sources)


def place_table(places):
    return jnp.stack([jnp.asarray(p, jnp.int32) for p in places])


def assemble_matrix(own, other, mine, partners, layout, outs, seq, enc):
    n_enc = lax.axis_size("enc")
    core = enc & 1
    sources, pieces, places = [], [], []
    for offsets, half, buffers in ((own, core, mine), (other, 1 - core, partners)):
        for (s_off, e_off), v in zip(offsets, buffers):
            for n, o in enumerate(line_offsets()):
                device = (seq ^ s_off ^ o) * n_enc + (enc ^ e_off)
                for row, column, rows, columns, out, to_row, to_column in layout(device >> 1, half):
                    pieces.append((len(sources), n, row, column, rows, columns, out))
                    places += [to_row, to_column]
            sources.append(v)
    return assemble(sources, pieces, place_table(places), outs)


def assemble_strips(offsets, buffers, count, seq):
    rows, width = buffers[0].shape[1], buffers[0].shape[2] // count
    pieces, places = [], []
    for i, s_off in enumerate(offsets):
        for n, o in enumerate(line_offsets()):
            for k in range(count):
                pieces.append((i, n, 0, k * width, rows, width, k))
                places += [(seq ^ s_off ^ o) * rows, 0]
    total = rows * lax.axis_size("seq")
    return assemble(buffers, pieces, place_table(places), [(total, width)] * count)


def dense(left, right):
    return jnp.dot(left, right, preferred_element_type=F32)


def dense_back(left, right):
    return lax.dot_general(left, right, (((1,), (1,)), ((), ())), preferred_element_type=F32)


def inner_rows(left, right):
    return lax.dot_general(left, right, (((0,), (0,)), ((), ())), preferred_element_type=F32)


def layer_norm(values, gain, shift):
    middle = jnp.mean(values, -1, keepdims=True)
    centred = values - middle
    variance = jnp.mean(centred * centred, -1, keepdims=True)
    return centred * lax.rsqrt(variance + EPSILON) * gain + shift


def norm_start(values, norms, index):
    middle = jnp.mean(values, -1, keepdims=True)
    centred = values - middle
    hat = centred * lax.rsqrt(jnp.mean(centred * centred, -1, keepdims=True) + EPSILON)
    return hat * norms[0, index] + norms[1, index], hat


def adamw(grad, moment, second, weight, rate, decay):
    moment = BETA_FIRST * moment + (1.0 - BETA_FIRST) * grad
    second = BETA_SECOND * second + (1.0 - BETA_SECOND) * grad * grad
    corrected = moment / (1.0 - BETA_FIRST**STEP)
    scale_two = jnp.sqrt(second / (1.0 - BETA_SECOND**STEP))
    return (
        moment,
        second,
        weight - rate * (corrected / (scale_two + ADAM_EPSILON) + decay * weight),
    )


def payload_kernel(n_line, loss_ref, count_ref, *refs):
    zero, three, four, enc, dec = refs[n_line : n_line + 5]
    out_ref, down_ref, up_ref = refs[-3:]
    total = tree_sum([r[...].astype(F32) for r in refs[:n_line]])
    squares = jnp.sum(jnp.sum(total * total, 1, keepdims=True), 0, keepdims=True)
    rows, small = down_ref.shape[1:]
    half = rows // 2
    for k in range(2):
        top, middle, end = k * rows, k * rows + half, (k + 1) * rows
        down_ref[k, :half, :] = total[top:middle, :small]
        down_ref[k, half:, :] = total[top:middle, small:]
        up_ref[k] = total[middle:end]
    rows = [zero, (enc, 0), (enc, 2), three, four, (dec, 0), (dec, 2)]
    for at in range(2):
        for i, row in enumerate(rows):
            ref, first = row if isinstance(row, tuple) else (row, 0)
            out_ref[7 * at + i : 7 * at + i + 1, :] = ref[first + at : first + at + 1, :]
    lane = lax.broadcasted_iota(jnp.int32, (1, out_ref.shape[1]), 1)
    scalars = jnp.where(lane == 2, squares, 0.0)
    scalars = jnp.where(lane == 1, count_ref[...], scalars)
    out_ref[14:15, :] = jnp.where(lane == 0, loss_ref[...], scalars)
    out_ref[15:16, :] = jnp.zeros((1, out_ref.shape[1]), F32)


def payload(loss, count, line, sums, small):
    depth, width = line[0].shape
    rows = depth // 2
    given = [loss.reshape(1, 1), count.reshape(1, 1)] + line + sums
    vmem = pl.BlockSpec(memory_space=pltpu.VMEM)
    return pl.pallas_call(
        lambda *refs: payload_kernel(len(line), *refs),
        out_shape=[
            jax.ShapeDtypeStruct((16, width), F32),
            jax.ShapeDtypeStruct((2, rows, small), F32),
            jax.ShapeDtypeStruct((2, rows // 2, width), F32),
        ],
        in_specs=[vmem] * len(given),
        out_specs=[vmem] * 3,
        cost_estimate=pl.CostEstimate(flops=MIB, bytes_accessed=MIB, transcendentals=0),
    )(*given)


def step_kernel(summed_ref, *refs):
    grads, states, outs = refs[:2], refs[2:8], refs[8:]
    norm_grads = summed_ref[0:14, :]
    loss, count = summed_ref[14:15, 0:1], summed_ref[14:15, 1:2]
    squares = summed_ref[14:15, 2:3] + jnp.sum(
        jnp.sum(norm_grads * norm_grads, 1, keepdims=True), 0, keepdims=True
    )
    norm = jnp.sqrt(squares) / count
    factor = jnp.minimum(1.0, CLIP_NORM / norm) / count
    for ref, value in zip(outs, (loss, count, norm, factor)):
        ref[...] = value
    for i in range(2):
        moment, second, weight = states[3 * i : 3 * i + 3]
        for k in range(2):
            new = adamw(
                grads[i][k] * factor, moment[k], second[k], weight[k], RATE_ADAPTER, DECAY_ADAPTER
            )
            for j in range(3):
                outs[4 + 3 * i + j][k] = new[j]


def optimizer_step(summed, grads, states):
    vmem = pl.BlockSpec(memory_space=pltpu.VMEM)
    given = [summed] + grads + states
    outs = [jax.ShapeDtypeStruct((1, 1), F32)] * 4
    outs += [jax.ShapeDtypeStruct(states[i - i % 3].shape, F32) for i in range(6)]
    results = pl.pallas_call(
        step_kernel,
        out_shape=outs,
        in_specs=[vmem] * len(given),
        out_specs=[vmem] * len(outs),
        cost_estimate=pl.CostEstimate(flops=MIB, bytes_accessed=2 * MIB, transcendentals=0),
    )(*given)
    return [r.reshape(()) for r in results[:4]] + list(results[4:])


def scores_of(left, right):
    return lax.dot_general(left, right, (((1,), (1,)), ((), ())), preferred_element_type=F32)


def head_parts(values):
    side = lax.broadcasted_iota(jnp.int32, values.shape, 1) // HEAD_DIM
    count = values.shape[1] // HEAD_DIM
    return [jnp.where(side == h, values, jnp.zeros((), values.dtype)) for h in range(count)]


def head_join(parts):
    side = lax.broadcasted_iota(jnp.int32, (parts[0].shape[0], 128), 1) // HEAD_DIM
    joined = jnp.broadcast_to(parts[0], side.shape)
    for h in range(1, len(parts)):
        joined = jnp.where(side == h, parts[h], joined)
    return joined


def attend_kernel(limit_ref, spot_ref, q_ref, k_ref, v_ref, *rest):
    context_ref, total_ref = rest[-2:]
    queries = head_parts(q_ref[...] * jnp.asarray(0.125, LOW))
    key, value = k_ref[...], v_ref[...]
    allowed = spot_ref[...] < limit_ref[...]
    raw = [scores_of(query, key) for query in queries]
    contexts, totals = [], []
    for scores in raw:
        scores = jnp.where(allowed, scores, MASKED_SCORE)
        highest = jnp.max(scores, -1, keepdims=True)
        exponent = jnp.exp(scores - highest)
        summed = jnp.sum(exponent, -1, keepdims=True)
        contexts.append(jnp.dot(exponent.astype(LOW), value, preferred_element_type=F32) / summed)
        totals.append(highest + jnp.log(summed))
    context_ref[...] = head_join(contexts).astype(LOW)
    total_ref[...] = head_join(totals)


def attend_specs(rows, length, key_at, value_at, count):
    block = pl.BlockSpec((rows, 128), lambda p, j: (j, p))
    return [
        pl.BlockSpec((rows, 1), lambda p, j: (j, 0)),
        pl.BlockSpec((1, length), lambda p, j: (0, 0)),
        block,
        pl.BlockSpec((length, 128), lambda p, j: (0, key_at + p)),
        pl.BlockSpec((length, 128), lambda p, j: (0, value_at + p)),
    ] + [block] * count


def query_rows(length):
    return 512 if length <= 1024 else 256


def attend(query, keys, key_at, value_at, limit, spots, after=()):
    length = query.shape[0]
    width = keys.shape[1] // (2 if key_at == 0 else 3)
    pairs = width // 128
    rows = query_rows(length)
    block = pl.BlockSpec((rows, 128), lambda p, j: (j, p))
    return pl.pallas_call(
        attend_kernel,
        grid=(pairs, length // rows),
        out_shape=[
            jax.ShapeDtypeStruct((length, width), LOW),
            jax.ShapeDtypeStruct((length, width), F32),
        ],
        in_specs=attend_specs(rows, length, key_at, value_at, 0)
        + [pl.BlockSpec(memory_space=pl.ANY)] * len(after),
        out_specs=[block, block],
        compiler_params=pltpu.CompilerParams(vmem_limit_bytes=56 * MIB),
        cost_estimate=pl.CostEstimate(
            flops=8 * length * length * width,
            bytes_accessed=8 * length * width,
            transcendentals=length * length * width // HEAD_DIM,
        ),
    )(limit, spots, query, keys, keys, *after)


def attend_back_part(refs, start, count):
    limit_ref, spot_ref, q_ref, k_ref, v_ref, grad_ref, total_ref, out_ref, dk_sum, dv_sum = refs
    pair, step = pl.program_id(0), pl.program_id(1)
    rows = q_ref.shape[0]
    at = pl.ds(start, count)
    queries = head_parts(q_ref[...] * jnp.asarray(0.125, LOW))
    grads = head_parts(grad_ref[...])
    key, value, totals = k_ref[at, :], v_ref[at, :], total_ref[...]
    allowed = spot_ref[:, at] < limit_ref[...]
    raw = [scores_of(query, key) for query in queries]
    grad_softs = [scores_of(grad, value) for grad in grads]
    grad_scores, soft_lows = [], []
    for h, (scores, grad_soft) in enumerate(zip(raw, grad_softs)):
        scores = jnp.where(allowed, scores, MASKED_SCORE)
        soft = jnp.exp(scores - totals[:, h * HEAD_DIM : h * HEAD_DIM + 1])
        weighted = jnp.sum(soft * grad_soft, -1, keepdims=True)
        grad_scores.append((soft * (grad_soft - weighted)).astype(LOW))
        soft_lows.append(soft.astype(LOW))
    dk_sum[at, :] += inner_rows(jnp.concatenate(grad_scores, 0), jnp.concatenate(queries, 0))
    dv_sum[at, :] += inner_rows(jnp.concatenate(soft_lows, 0), jnp.concatenate(grads, 0))
    grad_query = head_join([jnp.dot(g, key, preferred_element_type=F32) for g in grad_scores])
    column = pl.multiple_of(pair * 128, 128)
    out_ref[pl.ds(pl.multiple_of(step * rows, rows), rows), pl.ds(column, 128)] = (
        grad_query * 0.125
    ).astype(LOW)


def attend_back_step(refs, half=None):
    out_ref, dk_sum, dv_sum = refs[-3:]
    pair, step = pl.program_id(0), pl.program_id(1)
    pairs, steps = pl.num_programs(0), pl.num_programs(1)
    rows, length = refs[2].shape[0], refs[3].shape[0]

    @pl.when(step == 0)
    def _():
        dk_sum[...] = jnp.zeros_like(dk_sum)
        dv_sum[...] = jnp.zeros_like(dv_sum)

    if half is None:
        attend_back_part(refs, 0, length)
    else:

        @pl.when(step == half)
        def _():
            attend_back_part(refs, pl.multiple_of(half * rows, rows), rows)

        @pl.when(step != half)
        def _():
            attend_back_part(refs, 0, length)

    @pl.when(step == steps - 1)
    def _():
        out_ref[:, pl.ds(pl.multiple_of((pairs + pair) * 128, 128), 128)] = dk_sum[...].astype(LOW)
        out_ref[:, pl.ds(pl.multiple_of((2 * pairs + pair) * 128, 128), 128)] = dv_sum[...].astype(
            LOW
        )


def attend_back_kernel(*refs):
    attend_back_step(refs[:7] + refs[-3:])


def attend_sums_kernel(n_blocks, causal, *refs):
    half = refs[0][0] if causal else None
    refs = refs[1:] if causal else refs
    *hat_refs, weight_ref, own_hat_ref, own_grad_ref = refs[7 : 10 + n_blocks]
    sums_ref, out_ref, dk_sum, dv_sum, hats, weights, sem = refs[-7:]
    rows = hat_refs[0].shape[0]
    pair, step = pl.program_id(0), pl.program_id(1)
    copies = [
        pltpu.make_async_copy(ref, hats.at[pl.ds(j * rows, rows), :], sem.at[j])
        for j, ref in enumerate(hat_refs)
    ] + [pltpu.make_async_copy(weight_ref, weights, sem.at[n_blocks])]

    @pl.when((pair == 0) & (step == 0))
    def _():
        for copy in copies:
            copy.start()

    attend_back_step(refs[:7] + (out_ref, dk_sum, dv_sum), half)

    @pl.when((pair == pl.num_programs(0) - 1) & (step == pl.num_programs(1) - 1))
    def _():
        for copy in copies:
            copy.wait()
        weight = weights[...]
        length = out_ref.shape[0]
        coming = scores_of(out_ref[:PART, :], weight)
        own = own_grad_ref[...]
        gain = jnp.sum(own * own_hat_ref[...], 0, keepdims=True)
        shift = jnp.sum(own, 0, keepdims=True)
        for start in range(0, length, PART):
            now = coming
            if start + PART < length:
                coming = scores_of(out_ref[start + PART : start + 2 * PART, :], weight)
            gain += jnp.sum(now * hats[start : start + PART, :].astype(F32), 0, keepdims=True)
            shift += jnp.sum(now, 0, keepdims=True)
        sums_ref[0:1, :] = gain
        sums_ref[1:2, :] = shift


def attend_back(
    query, keys, key_at, value_at, limit, spots, grads, totals, sum_with=None, after=(), half=None
):
    length, width = grads.shape
    pairs = width // 128
    rows = query_rows(length)
    hbm = pl.BlockSpec(memory_space=pl.ANY)
    scratch = [pltpu.VMEM((length, 128), F32), pltpu.VMEM((length, 128), F32)]
    extra = () if sum_with is None else tuple(sum_with[0]) + tuple(sum_with[1:])
    n_blocks = len(extra) - 3
    causal = half is not None and 2 * rows == length
    chosen = [half.reshape(1).astype(jnp.int32)] if causal else []
    if sum_with is None:
        kernel = attend_back_kernel
        out = jax.ShapeDtypeStruct((length, 3 * width), LOW)
    else:

        def kernel(*refs):
            attend_sums_kernel(n_blocks, causal, *refs)

        out = jax.ShapeDtypeStruct((2, extra[0].shape[1]), F32)
        scratch = (
            [pltpu.VMEM((length, 3 * width), LOW)]
            + scratch
            + [pltpu.VMEM((length, extra[0].shape[1]), LOW), pltpu.VMEM(extra[n_blocks].shape, LOW)]
            + [pltpu.SemaphoreType.DMA((n_blocks + 1,))]
        )
    return pl.pallas_call(
        kernel,
        grid=(pairs, length // rows),
        out_shape=out,
        in_specs=[pl.BlockSpec(memory_space=pltpu.SMEM)] * len(chosen)
        + attend_specs(rows, length, key_at, value_at, 2)
        + [hbm] * len(extra[:-2])
        + [pl.BlockSpec(v.shape, lambda p, j: (0, 0)) for v in extra[-2:]]
        + [hbm] * len(after),
        out_specs=pl.BlockSpec(out.shape, lambda p, j: (0, 0)),
        scratch_shapes=scratch,
        compiler_params=pltpu.CompilerParams(vmem_limit_bytes=60 * MIB),
        cost_estimate=pl.CostEstimate(
            flops=20 * length * length * width,
            bytes_accessed=16 * length * width,
            transcendentals=length * length * width // HEAD_DIM,
        ),
    )(*chosen, limit, spots, query, keys, keys, grads, totals, *extra, *after)


def gelu_both(values):
    below = 0.5 * (1.0 + lax.erf(values * 0.7071067811865476))
    bell = jnp.exp(values * values * -0.5) * 0.3989422804014327
    return values * below, below + values * bell


def pack_feed(expand, reduce, down, up):
    rows, width = expand.shape[0], reduce.shape[1]
    parts = [expand[:, q * width : (q + 1) * width] for q in range(4)]
    return jnp.concatenate(
        parts + [reduce, jnp.concatenate([down[: rows // 2], down[rows // 2 :]], 1), up], 0
    )


def gather_feed(expand, reduce, down, up):
    everyone = ("seq", "enc")
    if expand.shape[0] % 32 == 0:
        return lax.all_gather(pack_feed(expand, reduce, down, up), everyone)
    whole = [lax.all_gather(v, everyone, axis=0, tiled=True) for v in (expand, reduce, down, up)]
    return pack_feed(*whole)[None]


def flat(block):
    return block.reshape(block.shape[0] * block.shape[1], block.shape[2])


def adapter_parts(block):
    count, rows, width = block.shape
    half = rows // 2
    down = jnp.stack([block[:, :half, : width // 2], block[:, :half, width // 2 :]], 1)
    return down.reshape(count * rows, width // 2), flat(block[:, half:])


def feed_scratch(packed):
    count, depth, width = packed.shape
    rows = depth // 9
    spread = max(count // 4, 1)
    return (
        [pltpu.VMEM((count, rows, width), LOW) for _ in range(4)]
        + [pltpu.VMEM((spread, width // spread, width), LOW) for _ in range(4)]
        + [pltpu.VMEM((count, rows, width), LOW), pltpu.VMEM((width, width), LOW)]
        + [pltpu.SemaphoreType.DMA((10,))]
    )


def feed_copies(packed_ref, out_ref, scratch):
    *rooms, sem = scratch
    count, depth, width = packed_ref.shape
    rows = depth // 9
    places = [packed_ref.at[:, pl.ds(q * rows, rows), :] for q in range(4)]
    for q in range(4):
        if count >= 4:
            spread = count // 4
            places.append(packed_ref.at[pl.ds(q * spread, spread), pl.ds(4 * rows, 4 * rows), :])
        else:
            places.append(packed_ref.at[:, pl.ds(4 * rows + q * width, width), :])
    places += [packed_ref.at[:, pl.ds(8 * rows, rows), :], out_ref]
    copies = [
        pltpu.make_async_copy(place, room, sem.at[i])
        for i, (place, room) in enumerate(zip(places, rooms))
    ]
    return copies[:4], copies[4:8], copies[8], copies[9]


def norm_stats(values):
    middle = jnp.mean(values, -1, keepdims=True)
    centred = values - middle
    scale = lax.rsqrt(jnp.mean(centred * centred, -1, keepdims=True) + EPSILON)
    return centred * scale, scale


def norm_back(grad, values, gain):
    hat, scale = norm_stats(values)
    scaled = grad * gain
    inner = scaled - jnp.mean(scaled, -1, keepdims=True)
    inner = inner - hat * jnp.mean(scaled * hat, -1, keepdims=True)
    return (
        inner * scale,
        jnp.sum(grad * hat, 0, keepdims=True),
        jnp.sum(grad, 0, keepdims=True),
    )


PART = 256


def branch_kernel(first, n_parts, *refs):
    parts, refs = refs[:n_parts], refs[n_parts:]
    res_ref, norm_ref, packed_ref, proj_ref = refs[:4]
    va_ref, x_ref, slope_ref, act_ref, bend_ref, vb_ref, low_ref = refs[4:11]
    total, slopes, slope_sem = refs[11:14]
    scratch = refs[14:]
    expands, reduces, small, proj = feed_copies(packed_ref, proj_ref, scratch)
    width = res_ref.shape[1]
    for copy in [proj] + [c for pair in zip(expands, reduces) for c in pair] + [small]:
        copy.start()
    proj.wait()
    context = jnp.concatenate([p[...] for p in parts], 1)
    va = res_ref[...] + jnp.dot(context, scratch[9][...], preferred_element_type=F32)
    va_ref[...] = va
    hat, _ = norm_stats(va)
    after = hat * norm_ref[first : first + 1, :] + norm_ref[7 + first : 8 + first, :]
    x = after.astype(LOW)
    x_ref[...] = x
    total[...] = after
    sends = []
    for q in range(4):
        expands[q].wait()
        expand = flat(scratch[q][...])
        pre = jnp.dot(x, expand[:, :PART], preferred_element_type=F32)
        acts = []
        for start in range(0, width, PART):
            now = pre
            if start + PART < width:
                pre = jnp.dot(
                    x, expand[:, start + PART : start + 2 * PART], preferred_element_type=F32
                )
            act, slope = gelu_both(now)
            slopes[q, :, start : start + PART] = slope
            acts.append(act.astype(LOW))
        sends.append(
            pltpu.make_async_copy(
                slopes.at[q], slope_ref.at[:, pl.ds(q * width, width)], slope_sem.at[q]
            )
        )
        sends[q].start()
        reduces[q].wait()
        total[...] += jnp.dot(
            jnp.concatenate(acts, 1), flat(scratch[4 + q][...]), preferred_element_type=F32
        )
    small.wait()
    down, up = adapter_parts(scratch[8][...])
    act, slope = gelu_both(jnp.dot(x, down, preferred_element_type=F32))
    act = act.astype(LOW)
    act_ref[...] = act
    bend_ref[...] = slope
    vb = total[...] + ADAPTER_SCALE * jnp.dot(act, up, preferred_element_type=F32)
    vb_ref[...] = vb
    hat, _ = norm_stats(vb)
    low_ref[...] = (
        hat * norm_ref[first + 1 : first + 2, :] + norm_ref[8 + first : 9 + first, :]
    ).astype(LOW)
    for send in sends:
        send.wait()


def branch(parts, residual, norms, first, packed, proj):
    rows, width = residual.shape
    hidden, small = 4 * width, width // 2
    vmem = pl.BlockSpec(memory_space=pltpu.VMEM)
    hbm = pl.BlockSpec(memory_space=pl.ANY)
    va, x, slope, act, bend, vb, low = pl.pallas_call(
        lambda *refs: branch_kernel(first, len(parts), *refs),
        out_shape=[
            jax.ShapeDtypeStruct((rows, width), F32),
            jax.ShapeDtypeStruct((rows, width), LOW),
            jax.ShapeDtypeStruct((rows, hidden), F32),
            jax.ShapeDtypeStruct((rows, small), LOW),
            jax.ShapeDtypeStruct((rows, small), F32),
            jax.ShapeDtypeStruct((rows, width), F32),
            jax.ShapeDtypeStruct((rows, width), LOW),
        ],
        in_specs=[vmem] * (len(parts) + 2) + [hbm, hbm],
        out_specs=[vmem, vmem, hbm, vmem, vmem, vmem, vmem],
        scratch_shapes=[
            pltpu.VMEM((rows, width), F32),
            pltpu.VMEM((4, rows, width), F32),
            pltpu.SemaphoreType.DMA((4,)),
        ]
        + feed_scratch(packed),
        compiler_params=pltpu.CompilerParams(vmem_limit_bytes=56 * MIB),
        cost_estimate=pl.CostEstimate(
            flops=4 * rows * width * (hidden + small) + 2 * rows * width * width,
            bytes_accessed=4 * width * (hidden + small) + 4 * rows * hidden,
            transcendentals=2 * rows * hidden,
        ),
    )(*parts, residual, norms, packed, proj)
    return low, (va, x, slope, act, bend, vb)


def branch_back_kernel(first, n_parts, *refs):
    n_given, refs = (refs[0], refs[1:])
    given, refs = refs[:n_given], refs[n_given:]
    vb_ref, va_ref, norm_ref, bend_ref, slope_ref, packed_ref, proj_ref = refs[:7]
    dva_ref, sums_ref, dpre_ref, ga_ref = refs[7:11]
    spread_refs, refs = refs[11 : 11 + n_parts], refs[11 + n_parts :]
    total, slopes, slope_sem = refs[:3]
    scratch = refs[3:]
    expands, reduces, small, proj = feed_copies(packed_ref, proj_ref, scratch)
    width = va_ref.shape[1]
    gets = [
        pltpu.make_async_copy(
            slope_ref.at[:, pl.ds(q * width, width)], slopes.at[q], slope_sem.at[q]
        )
        for q in range(4)
    ]
    for copy in [small] + [c for three in zip(reduces, gets, expands) for c in three] + [proj]:
        copy.start()
    if n_given == 2:
        grad = given[0][...].astype(F32) + given[1][...].astype(F32)
    else:
        mean, total_own, other, total_other, label, valid = [r[...] for r in given]
        grad = merge_means((mean, total_own), (other, total_other))[0]
        grad = (grad - label.astype(F32)) * valid
    grad_out, gain, shift = norm_back(grad, vb_ref[...], norm_ref[first + 1 : first + 2, :])
    sums_ref[2:3, :] = gain
    sums_ref[3:4, :] = shift
    g = grad_out.astype(LOW)
    ga = (ADAPTER_SCALE * grad_out).astype(LOW)
    ga_ref[...] = ga
    small.wait()
    down, up = adapter_parts(scratch[8][...])
    pre = (dense_back(ga, up) * bend_ref[...]).astype(LOW)
    dpre_ref[...] = pre
    total[...] = grad_out + dense_back(pre, down)
    for q in range(4):
        reduces[q].wait()
        reduce = flat(scratch[4 + q][...])
        gets[q].wait()
        grad = dense_back(g, reduce[:PART])
        pres = []
        for start in range(0, width, PART):
            now = grad
            if start + PART < width:
                grad = dense_back(g, reduce[start + PART : start + 2 * PART])
            pres.append((now * slopes[q, :, start : start + PART]).astype(LOW))
        expands[q].wait()
        total[...] += dense_back(jnp.concatenate(pres, 1), flat(scratch[q][...]))
    dva, gain, shift = norm_back(total[...], va_ref[...], norm_ref[first : first + 1, :])
    sums_ref[0:1, :] = gain
    sums_ref[1:2, :] = shift
    dva_ref[...] = dva
    proj.wait()
    spread = dense_back(dva.astype(LOW), scratch[9][...]).astype(LOW)
    share = width // n_parts
    for j in range(n_parts):
        spread_refs[j][...] = spread[:, j * share : (j + 1) * share]


def branch_back(given, kept, norms, first, packed, proj, n_parts):
    va, x, slope, act, bend, vb = kept
    rows, width = va.shape
    hidden, small = 4 * width, width // 2
    vmem = pl.BlockSpec(memory_space=pltpu.VMEM)
    hbm = pl.BlockSpec(memory_space=pl.ANY)
    dva, sums, dpre, ga, *spread = pl.pallas_call(
        lambda *refs: branch_back_kernel(first, n_parts, len(given), *refs),
        out_shape=[
            jax.ShapeDtypeStruct((rows, width), F32),
            jax.ShapeDtypeStruct((4, width), F32),
            jax.ShapeDtypeStruct((rows, small), LOW),
            jax.ShapeDtypeStruct((rows, width), LOW),
        ]
        + [jax.ShapeDtypeStruct((rows, width // n_parts), LOW)] * n_parts,
        in_specs=[vmem] * (4 + len(given)) + [hbm] * 3,
        out_specs=[vmem] * (4 + n_parts),
        scratch_shapes=[
            pltpu.VMEM((rows, width), F32),
            pltpu.VMEM((4, rows, width), F32),
            pltpu.SemaphoreType.DMA((4,)),
        ]
        + feed_scratch(packed),
        compiler_params=pltpu.CompilerParams(vmem_limit_bytes=56 * MIB),
        cost_estimate=pl.CostEstimate(
            flops=4 * rows * width * (hidden + small) + 2 * rows * width * width,
            bytes_accessed=4 * width * (hidden + small) + 4 * rows * hidden,
            transcendentals=0,
        ),
    )(*given, vb, va, norms, bend, slope, packed, proj)
    return dva, spread, sums, (x, dpre, act, ga)


def middle_back_kernel(first, n_parts, *refs):
    res_ref, own_ref, far_ref, va_ref, norm_ref, proj_ref = refs[:6]
    dva_ref, sums_ref = refs[6:8]
    grad = res_ref[...] + own_ref[...].astype(F32) + far_ref[...].astype(F32)
    dva, gain, shift = norm_back(grad, va_ref[...], norm_ref[first : first + 1, :])
    dva_ref[...] = dva
    sums_ref[0:1, :] = gain
    sums_ref[1:2, :] = shift
    spread = dense_back(dva.astype(LOW), proj_ref[...]).astype(LOW)
    share = spread.shape[1] // n_parts
    for j in range(n_parts):
        refs[8 + j][...] = spread[:, j * share : (j + 1) * share]


def middle_back(residual, own, far, va, norms, first, proj, n_parts):
    rows, width = va.shape
    vmem = pl.BlockSpec(memory_space=pltpu.VMEM)
    dva, sums, *spread = pl.pallas_call(
        lambda *refs: middle_back_kernel(first, n_parts, *refs),
        out_shape=[
            jax.ShapeDtypeStruct((rows, width), F32),
            jax.ShapeDtypeStruct((2, width), F32),
        ]
        + [jax.ShapeDtypeStruct((rows, width // n_parts), LOW)] * n_parts,
        in_specs=[vmem] * 6,
        out_specs=[vmem] * (2 + n_parts),
        compiler_params=pltpu.CompilerParams(vmem_limit_bytes=32 * MIB),
        cost_estimate=pl.CostEstimate(
            flops=0, bytes_accessed=0, transcendentals=0
        ),
    )(residual, own, far, va, norms, proj)
    return dva, spread, sums


def adapter_grad_kernel(core_ref, *refs):
    given, refs = refs[:8], refs[8:]
    keep_ref, send_ref = refs[:2]
    rooms, (down, up, keep, send, sem, sem_out) = refs[2:10], refs[10:]
    copies = [pltpu.make_async_copy(g, r, sem.at[i]) for i, (g, r) in enumerate(zip(given, rooms))]
    for copy in copies:
        copy.start()
    core = core_ref[0]
    pairs, depth, width = keep.shape
    rows = depth // 2
    half, small = rows // 2, width // 2
    for k in range(2):
        for copy in copies[4 * k : 4 * k + 4]:
            copy.wait()
        x, dpre, act, ga = rooms[4 * k : 4 * k + 4]
        down[...] = inner_rows(x[...], dpre[...])
        up[...] = inner_rows(act[...], ga[...])
        top, middle, end = k * rows, k * rows + half, (k + 1) * rows
        for ref, side in ((send, 1 - core), (keep, core)):
            for pair in range(pairs):
                device = 2 * pair + side
                at = pl.multiple_of(device * rows, rows)
                ref[pair, top:middle, :small] = down[pl.ds(at, half), :].astype(LOW)
                ref[pair, top:middle, small:] = down[pl.ds(at + half, half), :].astype(LOW)
                ref[pair, middle:end, :] = up[
                    pl.ds(pl.multiple_of(device * half, half), half), :
                ].astype(LOW)
    outs = [
        pltpu.make_async_copy(send, send_ref, sem_out.at[0]),
        pltpu.make_async_copy(keep, keep_ref, sem_out.at[1]),
    ]
    for copy in outs:
        copy.start()
    for copy in outs:
        copy.wait()


def adapter_grads(given, core):
    width, small = given[0][0].shape[1], given[0][1].shape[1]
    n_all = lax.axis_size("seq") * lax.axis_size("enc")
    rows = width // n_all
    if rows % 16:
        layers = []
        for x, dpre, act, ga in given:
            down, up = inner_rows(x, dpre), inner_rows(act, ga)
            folded = down.reshape(n_all, 2, rows // 2, small).transpose(0, 2, 1, 3)
            layers += [folded.reshape(n_all, rows // 2, width), up.reshape(n_all, rows // 2, width)]
        both = jnp.concatenate(layers, 1).reshape(n_all // 2, 2, 2 * rows, width)
        first = core == 0
        keep, send = jnp.where(first, both[:, 0], both[:, 1]), jnp.where(first, both[:, 1], both[:, 0])
        return keep.astype(LOW), send.astype(LOW)
    shape = (n_all // 2, 2 * rows, width)
    hbm = pl.BlockSpec(memory_space=pl.ANY)
    loads = list(given[0]) + list(given[1])
    return pl.pallas_call(
        adapter_grad_kernel,
        out_shape=[jax.ShapeDtypeStruct(shape, LOW)] * 2,
        in_specs=[pl.BlockSpec(memory_space=pltpu.SMEM)] + [hbm] * 8,
        out_specs=[hbm] * 2,
        scratch_shapes=[pltpu.VMEM(v.shape, LOW) for v in loads]
        + [pltpu.VMEM((width, small), F32), pltpu.VMEM((small, width), F32)]
        + [pltpu.VMEM(shape, LOW), pltpu.VMEM(shape, LOW)]
        + [pltpu.SemaphoreType.DMA((8,)), pltpu.SemaphoreType.DMA((2,))],
        compiler_params=pltpu.CompilerParams(vmem_limit_bytes=60 * MIB),
        cost_estimate=pl.CostEstimate(flops=0, bytes_accessed=0, transcendentals=0),
    )(core.reshape(1).astype(jnp.int32), *loads)


def head_kernel(n_blocks, *refs):
    o_refs, e_ref = refs[:n_blocks], refs[n_blocks]
    g_refs, lse_refs = refs[n_blocks + 1 : 2 * n_blocks + 1], refs[2 * n_blocks + 1 : -3]
    acc, peak, mass = refs[-3:]
    step = pl.program_id(0)
    rows = o_refs[0].shape[0]
    part = 2 * rows

    @pl.when(step == 0)
    def _():
        acc[...] = jnp.zeros_like(acc)
        peak[...] = jnp.full_like(peak, -1e30)
        mass[...] = jnp.zeros_like(mass)

    table = e_ref[...]
    spans = [pl.ds(start, part) for start in range(0, n_blocks * rows, part)]

    def logits_of(h):
        both = jnp.concatenate([o_refs[2 * h][...], o_refs[2 * h + 1][...]], 0)
        return scores_of(both, table)

    before = [peak[at, :1] for at in spans]
    held = [mass[at, :] for at in spans]
    coming = logits_of(0)
    highest, summed = [], []
    for h, at in enumerate(spans):
        logits = coming
        if h + 1 < len(spans):
            coming = logits_of(h + 1)
        highest.append(jnp.maximum(before[h], jnp.max(logits, -1, keepdims=True)))
        exponent = jnp.exp(logits - highest[h])
        fade = jnp.exp(before[h] - highest[h])
        summed.append(held[h] * fade + jnp.sum(exponent, -1, keepdims=True))
        acc[at, :] = acc[at, :] * fade + jnp.dot(
            exponent.astype(LOW), table, preferred_element_type=F32
        )
    for h, at in enumerate(spans):
        mass[at, :] = summed[h]
        peak[at, :] = jnp.broadcast_to(highest[h], (part, 128))

    @pl.when(step == pl.num_programs(0) - 1)
    def _():
        for j in range(n_blocks):
            at = pl.ds(j * rows, rows)
            g_refs[j][...] = (acc[at, :] / mass[at, :1]).astype(LOW)
            lse_refs[j][...] = peak[at, :1] + jnp.log(mass[at, :1])


def head(blocks, table):
    rows, width = blocks[0].shape
    count = len(blocks)
    entries = table.shape[0]
    tile = next(t for t in (1280, 1024, 640, 512, 256, 128) if entries % t == 0)
    block = pl.BlockSpec((rows, width), lambda j: (0, 0))
    results = pl.pallas_call(
        lambda *refs: head_kernel(count, *refs),
        grid=(entries // tile,),
        out_shape=[jax.ShapeDtypeStruct((rows, width), LOW)] * count
        + [jax.ShapeDtypeStruct((rows, 1), F32)] * count,
        in_specs=[block] * count + [pl.BlockSpec((tile, width), lambda j: (j, 0))],
        out_specs=[block] * count + [pl.BlockSpec((rows, 1), lambda j: (0, 0))] * count,
        scratch_shapes=[
            pltpu.VMEM((count * rows, width), F32),
            pltpu.VMEM((count * rows, 128), F32),
            pltpu.VMEM((count * rows, 128), F32),
        ],
        compiler_params=pltpu.CompilerParams(vmem_limit_bytes=60 * MIB),
        cost_estimate=pl.CostEstimate(
            flops=4 * count * rows * width * entries,
            bytes_accessed=2 * width * entries,
            transcendentals=count * rows * entries,
        ),
    )(*blocks, table)
    return list(results[:count]), list(results[count:])


def adapters_plane(keep, came, seq, enc):
    n_seq, n_enc = lax.axis_size("seq"), lax.axis_size("enc")
    near = n_seq // 4
    rows, width = keep.shape[1:]

    def block(s_off, e_off):
        start = (0, (seq & (near - 1)) ^ s_off, (enc >> 1) ^ (e_off >> 1), 0, 0)
        parts = [v.reshape(4, near, n_enc // 2, rows, width) for v in (keep, came)]
        parts = [lax.dynamic_slice(v, start, (4, 1, 1, rows, width))[:, 0, 0] for v in parts]
        return parts[0].astype(F32) + parts[1].astype(F32)

    return [block(0, 0)] + [flip_both(block(s, e).astype(LOW), s, e) for s, e in plane_offsets()[1:]]


def adapters_line(parts, seq):
    held = tree_sum([p.astype(F32) for p in parts])
    slow = seq // (lax.axis_size("seq") // 4)
    parts = [lax.dynamic_index_in_dim(held, slow ^ k, 0, keepdims=False) for k in range(4)]
    return parts[:1] + [
        flip(p.astype(LOW), "seq", o) for p, o in zip(parts[1:], line_offsets()[1:])
    ]


def sum_everywhere(values):
    values = values + flip(values, "enc", 1)
    values = tree_sum([values] + [flip_both(values, s, e) for s, e in plane_offsets()[1:]])
    return tree_sum([values] + [flip(values, "seq", o) for o in line_offsets()[1:]])


def shards(
    source_ids,
    target_ids,
    labels,
    lengths,
    embedding,
    positions,
    attention_in,
    attention_out,
    feed_in,
    feed_out,
    adapter_down,
    adapter_up,
    norm_params,
    down_moment,
    down_second,
    up_moment,
    up_second,
    norm_moment,
    norm_second,
):
    n_seq, n_enc = lax.axis_size("seq"), lax.axis_size("enc")
    n_all = n_seq * n_enc
    seq, enc = lax.axis_index("seq"), lax.axis_index("enc")
    core = enc & 1
    own_rows = source_ids.shape[1]
    width = embedding.shape[1]
    entries = embedding.shape[0]
    length = own_rows * n_enc
    share = width // n_enc
    source_length, target_length = lengths[0, 0], lengths[0, 1]

    blocks = jnp.arange(n_enc) ^ enc
    spots = (blocks[:, None] * own_rows + jnp.arange(own_rows)[None, :]).reshape(length)
    spots = spots.astype(jnp.int32)
    source_limit = jnp.broadcast_to(source_length, (length, 1)).astype(jnp.int32)
    causal_limit = jnp.minimum(spots + 1, target_length)[:, None].astype(jnp.int32)
    spots = spots[None, :]
    in_strip = share // 128

    def gather_rows(rows_low):
        return jnp.concatenate(gather_enc(rows_low), 0)

    def lookup(ids):
        inside = (ids >= 0) & (ids < entries)
        found = jnp.take(embedding, jnp.clip(ids, 0, entries - 1), axis=0)
        return jnp.where(inside[:, :, None], found, jnp.zeros((), LOW))

    def rows_of(found):
        return scatter_enc([found[j] for j in range(n_enc)])

    def own_parts(context):
        return swap_blocks([context[j * own_rows : (j + 1) * own_rows] for j in range(n_enc)])

    def all_heads(spread):
        return jnp.concatenate(swap_blocks(spread), 0)

    def row_blocks(partial):
        return [partial[j * own_rows : (j + 1) * own_rows] for j in range(n_enc)]

    down_low, up_low = adapter_down.astype(LOW), adapter_up.astype(LOW)
    feeds = [gather_feed(feed_in[k], feed_out[k], down_low[k], up_low[k]) for k in range(2)]

    gains = norm_params.astype(LOW).astype(F32)
    ids = jnp.concatenate([source_ids, target_ids, labels], 0).astype(F32)
    small_own = jnp.concatenate([ids.reshape(1, -1), gains.reshape(1, -1)], 1)
    small_all = unxor([v[0] for v in jnp.split(lax.all_gather(small_own, "enc"), n_enc)], enc)
    small_all = jnp.concatenate(small_all, 0)
    all_ids = small_all[:, : 3 * own_rows].astype(jnp.int32).reshape(n_enc, 3, own_rows)
    all_ids = all_ids - enc * entries
    gains = small_all[:, 3 * own_rows :].astype(LOW)[None]

    triple = attention_in.reshape(3, -1, 3, n_enc, share).transpose(3, 1, 0, 2, 4)
    shard_rows = triple.shape[1]
    strip_rows, pair_rows = n_enc * shard_rows, 2 * shard_rows
    triple = triple.reshape(n_enc, shard_rows, 9 * share)
    strip = lax.all_to_all(triple, "enc", 0, 0, tiled=True).reshape(strip_rows, 9 * share)
    strip, late = strip[:, : 6 * share], strip[:, 6 * share :]
    half = width // 2
    packed = jnp.concatenate(
        [attention_out[k][:, h * half : (h + 1) * half] for h in range(2) for k in range(3)], 1
    )
    pair_out = pair_split(packed, core)

    ids = [all_ids[:, k] for k in range(3)]
    strip, pair_out, *ids = gate([strip, pair_out] + ids)

    slow, slow_out = slow_flips_both(strip, pair_out)
    for mask in bits("seq"):
        gains = jnp.concatenate([gains, flip(gains, "seq", mask)], 0)
    arrived = gate([lookup(v) for v in ids] + slow + (slow_out or []))
    found, slow, slow_out = arrived[:3], arrived[3:6], arrived[6:]
    if not slow_out:
        slow_out = [v[strip_rows:] for v in slow]
        slow = [v[:strip_rows] for v in slow]
    order_seq, order_enc = jnp.arange(n_seq) ^ seq, jnp.arange(n_enc) ^ enc
    gains = jnp.take(jnp.take(gains, order_seq, axis=0), order_enc, axis=1)
    gains = gains.reshape(n_all, 14, width // n_all).transpose(1, 0, 2)
    norms = gains.reshape(2, 7, width).astype(F32)

    strip_offsets, strips = near_flips(jnp.stack([strip] + slow))
    source_rows, target_rows = rows_of(found[0]), rows_of(found[1])

    in_enc, in_dec = assemble_strips(strip_offsets, strips, 2, seq)
    encoder_in, encoder_hat = norm_start(source_rows + positions[0].astype(F32), norms, 0)
    decoder_in, decoder_hat = norm_start(target_rows + positions[1].astype(F32), norms, 3)
    across = gather_across(encoder_in.astype(LOW))
    decoder_low, *across[1:] = gate([decoder_in.astype(LOW)] + across[1:])
    encoder_all = jnp.concatenate(gather_pair(across), 0)
    decoder_all = gather_rows(decoder_low)
    stacked = jnp.stack([pair_out] + slow_out)
    singles = plane_start(stacked)

    triple_encoder = dense(encoder_all, in_enc).astype(LOW)
    enc_args = (triple_encoder, triple_encoder, in_strip, 2 * in_strip, source_limit, spots)
    context_enc, total_encoder = attend(*enc_args)
    slow = slow_flips(late)
    context_enc, *arrived = gate([context_enc] + slow + singles)
    slow, singles = arrived[:3], arrived[3:]
    own, other, mine = plane_finish(stacked, singles, core)
    partners = [flip(v, "enc", 1) for v in mine]
    triple_decoder = dense(decoder_all, in_dec).astype(LOW)
    dec_args = (triple_decoder, triple_decoder, in_strip, 2 * in_strip, causal_limit, spots)
    context_dec, total_decoder = attend(*dec_args, after=[context_enc])

    def out_layout(pair, side):
        row = pair * pair_rows
        block = (row // share) ^ enc
        return [
            (0, k * half, pair_rows, half, k, block * share + row % share, side * half)
            for k in range(3)
        ]

    attend_out = assemble_matrix(
        own, other, mine, partners, out_layout, [(width, width)] * 3, seq, enc
    )
    late_offsets, strips = near_flips(jnp.stack([late] + slow))
    attended = dense(jnp.concatenate(own_parts(context_dec), 1), attend_out[1])
    causal_in = decoder_in + attended
    after_causal = norm_start(causal_in, norms, 4)[0]
    in_cross = assemble_strips(late_offsets, strips, 1, seq)[0]
    attend_in = [in_enc, in_dec, in_cross]
    causal_all = gather_rows(after_causal.astype(LOW))
    norm_rows = norms.reshape(14, width)
    encoded_low, kept_enc = branch(
        own_parts(context_enc), encoder_in, norm_rows, 1, feeds[0], attend_out[0]
    )
    query_cross = dense(causal_all, in_cross[:, :share]).astype(LOW)

    encoded_all = gather_rows(encoded_low)
    pairs_cross = dense(encoded_all, in_cross[:, share:]).astype(LOW)
    cross_args = (query_cross, pairs_cross, 0, in_strip, source_limit, spots)
    context, total_cross = attend(*cross_args)
    context, found_label = gate([context, found[2]])
    label_rows, label_came = scatter_two([found_label[j] for j in range(n_enc)])
    decoded_low, kept_dec = branch(
        own_parts(context), after_causal, norm_rows, 5, feeds[1], attend_out[2]
    )

    decoded_low, label_came = gate([decoded_low, label_came])

    *decoded_all, encoder_low, decoder_low = gate(
        gather_enc(decoded_low) + [encoder_hat.astype(LOW), decoder_hat.astype(LOW)]
    )
    pulled, totals = head(decoded_all, embedding)
    hats = gather_across(encoder_low) + gather_across(decoder_low)
    *results, decoded_low, label_came = gate(
        pulled + totals + hats + [decoded_all[0], label_came]
    )
    pulled, totals, hats = results[:n_enc], results[n_enc : 2 * n_enc], results[2 * n_enc :]
    label_rows = (label_rows.astype(F32) + label_came.astype(F32)).astype(LOW)
    row_spots = enc * own_rows + jnp.arange(own_rows)
    valid = (row_spots < target_length).astype(F32)[:, None]
    picked = jnp.sum(decoded_low.astype(F32) * label_rows.astype(F32), -1, keepdims=True)
    own_mean, far_mean, hats = merge_enc(pulled, totals, hats)
    half_hats = len(hats) // 2
    hats = gather_pair(hats[:half_hats]) + gather_pair(hats[half_hats:])
    far, *hats = gate([far_mean[0]] + hats)
    encoder_hats, decoder_hats = hats[:n_enc], hats[n_enc:]
    highest = jnp.maximum(own_mean[1], far_mean[1])
    log_total = highest + jnp.log(
        jnp.exp(own_mean[1] - highest) + jnp.exp(far_mean[1] - highest)
    )
    loss_own = jnp.sum((log_total - picked) * valid)

    grad_res, spread, sums_dec, given_dec = branch_back(
        [own_mean[0], own_mean[1], far, far_mean[1], label_rows, valid],
        kept_dec,
        norm_rows,
        5,
        feeds[1],
        attend_out[2],
        n_enc,
    )
    grads = attend_back(*cross_args, all_heads(spread), total_cross)
    own_encoded, far_encoded = scatter_two(
        row_blocks(dense_back(grads[:, share:], attend_in[2][:, share:]))
    )
    own_causal, far_causal = scatter_two(
        row_blocks(dense_back(grads[:, :share], attend_in[2][:, :share]))
    )
    grad_enc, spread, sums_enc, given_enc = branch_back(
        [own_encoded, far_encoded], kept_enc, norm_rows, 1, feeds[0], attend_out[0], n_enc
    )
    spread = swap_blocks(spread)
    x, dpre, act, ga = given_enc
    dpre, far_causal = gate([dpre, far_causal])
    keep, send = adapter_grads([(x, dpre, act, ga), given_dec], core)
    came = flip(send, "enc", 1)
    grad_dec, spread_dec, sums_four = middle_back(
        grad_res, own_causal, far_causal, causal_in, norm_rows, 4, attend_out[1], n_enc
    )
    sums_zero = attend_back(
        *enc_args,
        jnp.concatenate(spread, 0),
        total_encoder,
        sum_with=(encoder_hats, in_enc, encoder_hat, grad_enc),
        after=[grad_dec],
    )
    parts = adapters_plane(keep, came, seq, enc)
    sums_zero, *parts[1:] = gate([sums_zero] + parts[1:])
    parts = adapters_line(parts, seq)
    sums_three = attend_back(
        *dec_args,
        all_heads(spread_dec),
        total_decoder,
        sum_with=(decoder_hats, in_dec, decoder_hat, grad_dec),
        after=[sums_zero],
        half=enc >> 1,
    )
    sums_three, *parts[1:] = gate([sums_three] + parts[1:])

    count_own = jnp.clip(target_length - enc * own_rows, 0, own_rows).astype(F32)
    summed, grad_down, grad_up = payload(
        loss_own,
        count_own,
        parts,
        [sums_zero, sums_three, sums_four, sums_enc, sums_dec],
        adapter_down.shape[2],
    )
    summed = sum_everywhere(summed)
    per = width // n_all
    own = lax.dynamic_slice_in_dim(summed, (seq * n_enc + enc) * per, per, 1)[:14]
    loss_sum, token_total, grad_norm, factor, *adapters = optimizer_step(
        summed,
        [grad_down, grad_up],
        [down_moment, down_second, adapter_down, up_moment, up_second, adapter_up],
    )
    new_norms = adamw(
        own.reshape(2, 7, per) * factor, norm_moment, norm_second, norm_params, RATE_NORMS, 0.0
    )
    return (loss_sum, token_total, grad_norm, *adapters, *new_norms)


def solution(mesh):
    everywhere = P(None, ("seq", "enc"), None)
    columns = P(None, None, ("seq", "enc"))
    return jax.shard_map(
        shards,
        mesh=mesh,
        in_specs=(
            P("seq", "enc"),
            P("seq", "enc"),
            P("seq", "enc"),
            P("seq", None),
            P("enc", None),
            P(None, "enc", None),
            everywhere,
            everywhere,
            everywhere,
            everywhere,
            everywhere,
            everywhere,
            columns,
            everywhere,
            everywhere,
            everywhere,
            everywhere,
            columns,
            columns,
        ),
        out_specs=(
            P(),
            P(),
            P(),
            everywhere,
            everywhere,
            everywhere,
            everywhere,
            everywhere,
            everywhere,
            columns,
            columns,
            columns,
        ),
        check_vma=False,
    )
```

```python
import jax
import jax.numpy as jnp
from jax import lax
from jax.experimental import pallas as pl
from jax.experimental.pallas import tpu as pltpu
from jax.sharding import PartitionSpec as P

HEAD_DIM = 64
STEP = 10

EPSILON = 1e-05
ADAPTER_SCALE = 4.0
CLIP_NORM = 0.25
RATE_ADAPTER = 0.05
RATE_NORMS = 0.5
BETA_FIRST = 0.9
BETA_SECOND = 0.999
ADAM_EPSILON = 1e-08
DECAY_ADAPTER = 0.01
MASKED_SCORE = -1000000000.0

LOW = jnp.bfloat16
F32 = jnp.float32
MIB = 1024 * 1024


def flip(value, axis, mask):
    count = lax.axis_size(axis)
    return lax.ppermute(value, axis, [(i, i ^ mask) for i in range(count)])


def bits(axis):
    count = lax.axis_size(axis)
    return [1 << i for i in range(count.bit_length() - 1)]


def unxor(blocks, me):
    blocks = list(blocks)
    mask = 1
    while mask < len(blocks):
        bit = (me & mask) != 0
        blocks = [jnp.where(bit, blocks[i ^ mask], blocks[i]) for i in range(len(blocks))]
        mask *= 2
    return blocks


def gather_across(value):
    found = {0: value}
    for mask in bits("enc")[1:]:
        found.update({j | mask: flip(v, "enc", mask) for j, v in list(found.items())})
    return [found[j] for j in sorted(found)]


def gather_pair(blocks):
    return [v for block in blocks for v in (block, flip(block, "enc", 1))]


def gather_enc(value):
    return gather_pair(gather_across(value))


def scatter_two(blocks):
    held = dict(enumerate(blocks))
    for mask in bits("enc"):
        away = [j for j in held if j & mask]
        sent = [flip(held[j].astype(LOW), "enc", mask) for j in away]
        for j, part in zip(away, sent):
            if len(held) == 2:
                return held[j ^ mask], part
            held[j ^ mask] = held[j ^ mask].astype(F32) + part.astype(F32)
            del held[j]


def scatter_enc(blocks):
    own, came = scatter_two(blocks)
    return own.astype(F32) + came.astype(F32)


def merge_means(first, second):
    (mean, total), (other, other_total) = first, second
    highest = jnp.maximum(total, other_total)
    own, far = jnp.exp(total - highest), jnp.exp(other_total - highest)
    both = own + far
    return (mean.astype(F32) * own + other.astype(F32) * far) / both, highest + jnp.log(both)


def merge_enc(blocks, totals, beside):
    held = {j: (b, t) for j, (b, t) in enumerate(zip(blocks, totals))}
    for mask in bits("enc"):
        away = [j for j in held if j & mask]
        means = [held[j][0].astype(LOW) for j in away]
        if len(held) == 2:
            means[0], *beside = gate([means[0]] + beside)
        sent = [(flip(m, "enc", mask), flip(held[j][1], "enc", mask)) for j, m in zip(away, means)]
        for j, came in zip(away, sent):
            if len(held) == 2:
                return held[j ^ mask], came, beside
            held[j ^ mask] = merge_means(held[j ^ mask], came)
            del held[j]


def swap_blocks(blocks):
    return [blocks[0]] + [flip(blocks[j], "enc", j) for j in range(1, len(blocks))]


def pair_split(shard, core):
    half = shard.shape[1] // 2
    first = core == 0
    low, high = shard[:, :half], shard[:, half:]
    keep = jnp.where(first, low, high)
    came = flip(jnp.where(first, high, low), "enc", 1)
    return jnp.concatenate([jnp.where(first, keep, came), jnp.where(first, came, keep)], 0)


def gate(arrays):
    def kernel(*refs):
        pass

    results = pl.pallas_call(
        kernel,
        out_shape=[jax.ShapeDtypeStruct(v.shape, v.dtype) for v in arrays],
        in_specs=[pl.BlockSpec(memory_space=pl.ANY)] * len(arrays),
        out_specs=[pl.BlockSpec(memory_space=pl.ANY)] * len(arrays),
        input_output_aliases={i: i for i in range(len(arrays))},
        compiler_params=pltpu.CompilerParams(vmem_limit_bytes=60 * MIB),
        cost_estimate=pl.CostEstimate(flops=0, bytes_accessed=0, transcendentals=0),
    )(*arrays)
    return list(results)


def flip_both(value, seq_mask, enc_mask):
    n_enc = lax.axis_size("enc")
    perm = []
    for i in range(lax.axis_size("seq") * n_enc):
        s, e = divmod(i, n_enc)
        perm.append((i, (s ^ seq_mask) * n_enc + (e ^ enc_mask)))
    return lax.ppermute(value, ("seq", "enc"), perm)


def tree_sum(values):
    values = list(values)
    while len(values) > 1:
        values = [values[i] + values[i + 1] for i in range(0, len(values), 2)]
    return values[0]


def plane_offsets():
    near = lax.axis_size("seq") // 4
    return [(s, e) for e in range(0, lax.axis_size("enc"), 2) for s in range(near)]


def line_offsets():
    return [k * (lax.axis_size("seq") // 4) for k in range(4)]


def mixed_flip(value, for_even, for_odd):
    n_enc = lax.axis_size("enc")
    perm = []
    for i in range(lax.axis_size("seq") * n_enc):
        s, e = divmod(i, n_enc)
        axis, mask = for_odd if e & 1 else for_even
        perm.append((i, (s ^ mask) * n_enc + e if axis == "seq" else s * n_enc + (e ^ mask)))
    return lax.ppermute(value, ("seq", "enc"), perm)


def near_bits():
    return [("seq", mask) for mask in bits("seq") if mask < lax.axis_size("seq") // 4]


def across_bits():
    return [("enc", mask) for mask in bits("enc")[1:]]


def moved(offset, step):
    return (offset[0] ^ step[1], offset[1]) if step[0] == "seq" else (offset[0], offset[1] ^ step[1])


def slow_flips(value):
    return [flip(value, "seq", o) for o in line_offsets()[1:]]


def slow_flips_both(first, second):
    if first.shape[1] != second.shape[1]:
        return slow_flips(first), slow_flips(second)
    return slow_flips(jnp.concatenate([first, second], 0)), None


def plane_steps():
    return list(zip(near_bits() + across_bits(), across_bits() + near_bits()))


def plane_start(stacked):
    return [mixed_flip(stacked, *step) for step in plane_steps()]


def plane_finish(stacked, singles, core):
    found = [((0, 0), (0, 0), stacked)]
    for step, single in zip(plane_steps(), singles):
        fresh = [(moved((0, 0), step[0]), moved((0, 0), step[1]), single)]
        fresh += [
            (moved(o, step[0]), moved(p, step[1]), mixed_flip(v, *step)) for o, p, v in found[1:]
        ]
        found += fresh
    own = [tuple(jnp.where(core == 0, i, k) for i, k in zip(o, p)) for o, p, _ in found]
    other = [tuple(jnp.where(core == 0, k, i) for i, k in zip(o, p)) for o, p, _ in found]
    return own, other, [v for _, _, v in found]


def near_flips(stacked):
    found = [(0, stacked)]
    for _, mask in near_bits():
        found += [(o ^ mask, flip(v, "seq", mask)) for o, v in found]
    return [o for o, _ in found], [v for _, v in found]


def assemble(sources, pieces, places, outs):
    count = len(pieces)
    n_src, n_out = len(sources), len(outs)

    def kernel(*refs):
        table = refs[0]
        given = refs[1 : 1 + n_src]
        results = refs[1 + n_src : 1 + n_src + n_out]
        stage = refs[1 + n_src + n_out : 1 + n_src + n_out + count]
        sem_in, sem_out = refs[-2:]
        copies_in, copies_out = [], []
        for i, (src, block, row, column, rows, columns, out) in enumerate(pieces):
            copies_in.append(
                pltpu.make_async_copy(
                    given[src].at[block, pl.ds(row, rows), pl.ds(column, columns)],
                    stage[i],
                    sem_in.at[i],
                )
            )
            to_row = pl.multiple_of(table[2 * i], rows)
            to_column = pl.multiple_of(table[2 * i + 1], columns)
            copies_out.append(
                pltpu.make_async_copy(
                    stage[i],
                    results[out].at[pl.ds(to_row, rows), pl.ds(to_column, columns)],
                    sem_out.at[i],
                )
            )
        for copy in copies_in:
            copy.start()
        for i in range(count):
            copies_in[i].wait()
            copies_out[i].start()
        for copy in copies_out:
            copy.wait()

    size = sum(p[4] * p[5] * 2 for p in pieces)
    return pl.pallas_call(
        kernel,
        out_shape=[jax.ShapeDtypeStruct(shape, LOW) for shape in outs],
        in_specs=[pl.BlockSpec(memory_space=pltpu.SMEM)]
        + [pl.BlockSpec(memory_space=pl.ANY)] * n_src,
        out_specs=[pl.BlockSpec(memory_space=pl.ANY)] * n_out,
        scratch_shapes=[pltpu.VMEM((p[4], p[5]), LOW) for p in pieces]
        + [pltpu.SemaphoreType.DMA((count,)), pltpu.SemaphoreType.DMA((count,))],
        compiler_params=pltpu.CompilerParams(vmem_limit_bytes=size + 8 * MIB),
        cost_estimate=pl.CostEstimate(flops=0, bytes_accessed=2 * size, transcendentals=0),
    )(places, *sources)


def place_table(places):
    return jnp.stack([jnp.asarray(p, jnp.int32) for p in places])


def assemble_matrix(own, other, mine, partners, layout, outs, seq, enc):
    n_enc = lax.axis_size("enc")
    core = enc & 1
    sources, pieces, places = [], [], []
    for offsets, half, buffers in ((own, core, mine), (other, 1 - core, partners)):
        for (s_off, e_off), v in zip(offsets, buffers):
            for n, o in enumerate(line_offsets()):
                device = (seq ^ s_off ^ o) * n_enc + (enc ^ e_off)
                for row, column, rows, columns, out, to_row, to_column in layout(device >> 1, half):
                    pieces.append((len(sources), n, row, column, rows, columns, out))
                    places += [to_row, to_column]
            sources.append(v)
    return assemble(sources, pieces, place_table(places), outs)


def assemble_strips(offsets, buffers, count, seq):
    rows, width = buffers[0].shape[1], buffers[0].shape[2] // count
    pieces, places = [], []
    for i, s_off in enumerate(offsets):
        for n, o in enumerate(line_offsets()):
            for k in range(count):
                pieces.append((i, n, 0, k * width, rows, width, k))
                places += [(seq ^ s_off ^ o) * rows, 0]
    total = rows * lax.axis_size("seq")
    return assemble(buffers, pieces, place_table(places), [(total, width)] * count)


def dense(left, right):
    return jnp.dot(left, right, preferred_element_type=F32)


def dense_back(left, right):
    return lax.dot_general(left, right, (((1,), (1,)), ((), ())), preferred_element_type=F32)


def inner_rows(left, right):
    return lax.dot_general(left, right, (((0,), (0,)), ((), ())), preferred_element_type=F32)


def layer_norm(values, gain, shift):
    middle = jnp.mean(values, -1, keepdims=True)
    centred = values - middle
    variance = jnp.mean(centred * centred, -1, keepdims=True)
    return centred * lax.rsqrt(variance + EPSILON) * gain + shift


def norm_start(values, norms, index):
    middle = jnp.mean(values, -1, keepdims=True)
    centred = values - middle
    hat = centred * lax.rsqrt(jnp.mean(centred * centred, -1, keepdims=True) + EPSILON)
    return hat * norms[0, index] + norms[1, index], hat


def adamw(grad, moment, second, weight, rate, decay):
    moment = BETA_FIRST * moment + (1.0 - BETA_FIRST) * grad
    second = BETA_SECOND * second + (1.0 - BETA_SECOND) * grad * grad
    corrected = moment / (1.0 - BETA_FIRST**STEP)
    scale_two = jnp.sqrt(second / (1.0 - BETA_SECOND**STEP))
    return (
        moment,
        second,
        weight - rate * (corrected / (scale_two + ADAM_EPSILON) + decay * weight),
    )


def payload_kernel(n_line, loss_ref, count_ref, *refs):
    zero, three, four, enc, dec = refs[n_line : n_line + 5]
    out_ref, down_ref, up_ref = refs[-3:]
    total = tree_sum([r[...].astype(F32) for r in refs[:n_line]])
    squares = jnp.sum(jnp.sum(total * total, 1, keepdims=True), 0, keepdims=True)
    rows, small = down_ref.shape[1:]
    half = rows // 2
    for k in range(2):
        top, middle, end = k * rows, k * rows + half, (k + 1) * rows
        down_ref[k, :half, :] = total[top:middle, :small]
        down_ref[k, half:, :] = total[top:middle, small:]
        up_ref[k] = total[middle:end]
    rows = [zero, (enc, 0), (enc, 2), three, four, (dec, 0), (dec, 2)]
    for at in range(2):
        for i, row in enumerate(rows):
            ref, first = row if isinstance(row, tuple) else (row, 0)
            out_ref[7 * at + i : 7 * at + i + 1, :] = ref[first + at : first + at + 1, :]
    lane = lax.broadcasted_iota(jnp.int32, (1, out_ref.shape[1]), 1)
    scalars = jnp.where(lane == 2, squares, 0.0)
    scalars = jnp.where(lane == 1, count_ref[...], scalars)
    out_ref[14:15, :] = jnp.where(lane == 0, loss_ref[...], scalars)
    out_ref[15:16, :] = jnp.zeros((1, out_ref.shape[1]), F32)


def payload(loss, count, line, sums, small):
    depth, width = line[0].shape
    rows = depth // 2
    given = [loss.reshape(1, 1), count.reshape(1, 1)] + line + sums
    vmem = pl.BlockSpec(memory_space=pltpu.VMEM)
    return pl.pallas_call(
        lambda *refs: payload_kernel(len(line), *refs),
        out_shape=[
            jax.ShapeDtypeStruct((16, width), F32),
            jax.ShapeDtypeStruct((2, rows, small), F32),
            jax.ShapeDtypeStruct((2, rows // 2, width), F32),
        ],
        in_specs=[vmem] * len(given),
        out_specs=[vmem] * 3,
        cost_estimate=pl.CostEstimate(flops=MIB, bytes_accessed=MIB, transcendentals=0),
    )(*given)


def step_kernel(summed_ref, *refs):
    grads, states, outs = refs[:2], refs[2:8], refs[8:]
    norm_grads = summed_ref[0:14, :]
    loss, count = summed_ref[14:15, 0:1], summed_ref[14:15, 1:2]
    squares = summed_ref[14:15, 2:3] + jnp.sum(
        jnp.sum(norm_grads * norm_grads, 1, keepdims=True), 0, keepdims=True
    )
    norm = jnp.sqrt(squares) / count
    factor = jnp.minimum(1.0, CLIP_NORM / norm) / count
    for ref, value in zip(outs, (loss, count, norm, factor)):
        ref[...] = value
    for i in range(2):
        moment, second, weight = states[3 * i : 3 * i + 3]
        for k in range(2):
            new = adamw(
                grads[i][k] * factor, moment[k], second[k], weight[k], RATE_ADAPTER, DECAY_ADAPTER
            )
            for j in range(3):
                outs[4 + 3 * i + j][k] = new[j]


def optimizer_step(summed, grads, states):
    vmem = pl.BlockSpec(memory_space=pltpu.VMEM)
    given = [summed] + grads + states
    outs = [jax.ShapeDtypeStruct((1, 1), F32)] * 4
    outs += [jax.ShapeDtypeStruct(states[i - i % 3].shape, F32) for i in range(6)]
    results = pl.pallas_call(
        step_kernel,
        out_shape=outs,
        in_specs=[vmem] * len(given),
        out_specs=[vmem] * len(outs),
        cost_estimate=pl.CostEstimate(flops=MIB, bytes_accessed=2 * MIB, transcendentals=0),
    )(*given)
    return [r.reshape(()) for r in results[:4]] + list(results[4:])


def scores_of(left, right):
    return lax.dot_general(left, right, (((1,), (1,)), ((), ())), preferred_element_type=F32)


def head_parts(values):
    side = lax.broadcasted_iota(jnp.int32, values.shape, 1) // HEAD_DIM
    count = values.shape[1] // HEAD_DIM
    return [jnp.where(side == h, values, jnp.zeros((), values.dtype)) for h in range(count)]


def head_join(parts):
    side = lax.broadcasted_iota(jnp.int32, (parts[0].shape[0], 128), 1) // HEAD_DIM
    joined = jnp.broadcast_to(parts[0], side.shape)
    for h in range(1, len(parts)):
        joined = jnp.where(side == h, parts[h], joined)
    return joined


def attend_kernel(limit_ref, spot_ref, q_ref, k_ref, v_ref, *rest):
    context_ref, total_ref = rest[-2:]
    queries = head_parts(q_ref[...] * jnp.asarray(0.125, LOW))
    key, value = k_ref[...], v_ref[...]
    allowed = spot_ref[...] < limit_ref[...]
    raw = [scores_of(query, key) for query in queries]
    contexts, totals = [], []
    for scores in raw:
        scores = jnp.where(allowed, scores, MASKED_SCORE)
        highest = jnp.max(scores, -1, keepdims=True)
        exponent = jnp.exp(scores - highest)
        summed = jnp.sum(exponent, -1, keepdims=True)
        contexts.append(jnp.dot(exponent.astype(LOW), value, preferred_element_type=F32) / summed)
        totals.append(highest + jnp.log(summed))
    context_ref[...] = head_join(contexts).astype(LOW)
    total_ref[...] = head_join(totals)


def attend_specs(rows, length, key_at, value_at, count):
    block = pl.BlockSpec((rows, 128), lambda p, j: (j, p))
    return [
        pl.BlockSpec((rows, 1), lambda p, j: (j, 0)),
        pl.BlockSpec((1, length), lambda p, j: (0, 0)),
        block,
        pl.BlockSpec((length, 128), lambda p, j: (0, key_at + p)),
        pl.BlockSpec((length, 128), lambda p, j: (0, value_at + p)),
    ] + [block] * count


def query_rows(length):
    return 512 if length <= 1024 else 256


def attend(query, keys, key_at, value_at, limit, spots, after=()):
    length = query.shape[0]
    width = keys.shape[1] // (2 if key_at == 0 else 3)
    pairs = width // 128
    rows = query_rows(length)
    block = pl.BlockSpec((rows, 128), lambda p, j: (j, p))
    return pl.pallas_call(
        attend_kernel,
        grid=(pairs, length // rows),
        out_shape=[
            jax.ShapeDtypeStruct((length, width), LOW),
            jax.ShapeDtypeStruct((length, width), F32),
        ],
        in_specs=attend_specs(rows, length, key_at, value_at, 0)
        + [pl.BlockSpec(memory_space=pl.ANY)] * len(after),
        out_specs=[block, block],
        compiler_params=pltpu.CompilerParams(vmem_limit_bytes=56 * MIB),
        cost_estimate=pl.CostEstimate(
            flops=8 * length * length * width,
            bytes_accessed=8 * length * width,
            transcendentals=length * length * width // HEAD_DIM,
        ),
    )(limit, spots, query, keys, keys, *after)


def attend_back_part(refs, start, count):
    limit_ref, spot_ref, q_ref, k_ref, v_ref, grad_ref, total_ref, out_ref, dk_sum, dv_sum = refs
    pair, step = pl.program_id(0), pl.program_id(1)
    rows = q_ref.shape[0]
    at = pl.ds(start, count)
    queries = head_parts(q_ref[...] * jnp.asarray(0.125, LOW))
    grads = head_parts(grad_ref[...])
    key, value, totals = k_ref[at, :], v_ref[at, :], total_ref[...]
    allowed = spot_ref[:, at] < limit_ref[...]
    raw = [scores_of(query, key) for query in queries]
    grad_softs = [scores_of(grad, value) for grad in grads]
    grad_scores, soft_lows = [], []
    for h, (scores, grad_soft) in enumerate(zip(raw, grad_softs)):
        scores = jnp.where(allowed, scores, MASKED_SCORE)
        soft = jnp.exp(scores - totals[:, h * HEAD_DIM : h * HEAD_DIM + 1])
        weighted = jnp.sum(soft * grad_soft, -1, keepdims=True)
        grad_scores.append((soft * (grad_soft - weighted)).astype(LOW))
        soft_lows.append(soft.astype(LOW))
    dk_sum[at, :] += inner_rows(jnp.concatenate(grad_scores, 0), jnp.concatenate(queries, 0))
    dv_sum[at, :] += inner_rows(jnp.concatenate(soft_lows, 0), jnp.concatenate(grads, 0))
    grad_query = head_join([jnp.dot(g, key, preferred_element_type=F32) for g in grad_scores])
    column = pl.multiple_of(pair * 128, 128)
    out_ref[pl.ds(pl.multiple_of(step * rows, rows), rows), pl.ds(column, 128)] = (
        grad_query * 0.125
    ).astype(LOW)


def attend_back_step(refs, half=None):
    out_ref, dk_sum, dv_sum = refs[-3:]
    pair, step = pl.program_id(0), pl.program_id(1)
    pairs, steps = pl.num_programs(0), pl.num_programs(1)
    rows, length = refs[2].shape[0], refs[3].shape[0]

    @pl.when(step == 0)
    def _():
        dk_sum[...] = jnp.zeros_like(dk_sum)
        dv_sum[...] = jnp.zeros_like(dv_sum)

    if half is None:
        attend_back_part(refs, 0, length)
    else:

        @pl.when(step == half)
        def _():
            attend_back_part(refs, pl.multiple_of(half * rows, rows), rows)

        @pl.when(step != half)
        def _():
            attend_back_part(refs, 0, length)

    @pl.when(step == steps - 1)
    def _():
        out_ref[:, pl.ds(pl.multiple_of((pairs + pair) * 128, 128), 128)] = dk_sum[...].astype(LOW)
        out_ref[:, pl.ds(pl.multiple_of((2 * pairs + pair) * 128, 128), 128)] = dv_sum[...].astype(
            LOW
        )


def attend_back_kernel(*refs):
    attend_back_step(refs[:7] + refs[-3:])


def attend_sums_kernel(n_blocks, causal, *refs):
    half = refs[0][0] if causal else None
    refs = refs[1:] if causal else refs
    *hat_refs, weight_ref, own_hat_ref, own_grad_ref = refs[7 : 10 + n_blocks]
    sums_ref, out_ref, dk_sum, dv_sum, hats, weights, sem = refs[-7:]
    rows = hat_refs[0].shape[0]
    pair, step = pl.program_id(0), pl.program_id(1)
    copies = [
        pltpu.make_async_copy(ref, hats.at[pl.ds(j * rows, rows), :], sem.at[j])
        for j, ref in enumerate(hat_refs)
    ] + [pltpu.make_async_copy(weight_ref, weights, sem.at[n_blocks])]

    @pl.when((pair == 0) & (step == 0))
    def _():
        for copy in copies:
            copy.start()

    attend_back_step(refs[:7] + (out_ref, dk_sum, dv_sum), half)

    @pl.when((pair == pl.num_programs(0) - 1) & (step == pl.num_programs(1) - 1))
    def _():
        for copy in copies:
            copy.wait()
        weight = weights[...]
        length = out_ref.shape[0]
        coming = scores_of(out_ref[:PART, :], weight)
        own = own_grad_ref[...]
        gain = jnp.sum(own * own_hat_ref[...], 0, keepdims=True)
        shift = jnp.sum(own, 0, keepdims=True)
        for start in range(0, length, PART):
            now = coming
            if start + PART < length:
                coming = scores_of(out_ref[start + PART : start + 2 * PART, :], weight)
            gain += jnp.sum(now * hats[start : start + PART, :].astype(F32), 0, keepdims=True)
            shift += jnp.sum(now, 0, keepdims=True)
        sums_ref[0:1, :] = gain
        sums_ref[1:2, :] = shift


def attend_back(
    query, keys, key_at, value_at, limit, spots, grads, totals, sum_with=None, after=(), half=None
):
    length, width = grads.shape
    pairs = width // 128
    rows = query_rows(length)
    hbm = pl.BlockSpec(memory_space=pl.ANY)
    scratch = [pltpu.VMEM((length, 128), F32), pltpu.VMEM((length, 128), F32)]
    extra = () if sum_with is None else tuple(sum_with[0]) + tuple(sum_with[1:])
    n_blocks = len(extra) - 3
    causal = half is not None and 2 * rows == length
    chosen = [half.reshape(1).astype(jnp.int32)] if causal else []
    if sum_with is None:
        kernel = attend_back_kernel
        out = jax.ShapeDtypeStruct((length, 3 * width), LOW)
    else:

        def kernel(*refs):
            attend_sums_kernel(n_blocks, causal, *refs)

        out = jax.ShapeDtypeStruct((2, extra[0].shape[1]), F32)
        scratch = (
            [pltpu.VMEM((length, 3 * width), LOW)]
            + scratch
            + [pltpu.VMEM((length, extra[0].shape[1]), LOW), pltpu.VMEM(extra[n_blocks].shape, LOW)]
            + [pltpu.SemaphoreType.DMA((n_blocks + 1,))]
        )
    return pl.pallas_call(
        kernel,
        grid=(pairs, length // rows),
        out_shape=out,
        in_specs=[pl.BlockSpec(memory_space=pltpu.SMEM)] * len(chosen)
        + attend_specs(rows, length, key_at, value_at, 2)
        + [hbm] * len(extra[:-2])
        + [pl.BlockSpec(v.shape, lambda p, j: (0, 0)) for v in extra[-2:]]
        + [hbm] * len(after),
        out_specs=pl.BlockSpec(out.shape, lambda p, j: (0, 0)),
        scratch_shapes=scratch,
        compiler_params=pltpu.CompilerParams(vmem_limit_bytes=60 * MIB),
        cost_estimate=pl.CostEstimate(
            flops=20 * length * length * width,
            bytes_accessed=16 * length * width,
            transcendentals=length * length * width // HEAD_DIM,
        ),
    )(*chosen, limit, spots, query, keys, keys, grads, totals, *extra, *after)


def gelu_both(values):
    below = 0.5 * (1.0 + lax.erf(values * 0.7071067811865476))
    bell = jnp.exp(values * values * -0.5) * 0.3989422804014327
    return values * below, below + values * bell


def pack_feed(expand, reduce, down, up):
    rows, width = expand.shape[0], reduce.shape[1]
    parts = [expand[:, q * width : (q + 1) * width] for q in range(4)]
    return jnp.concatenate(
        parts + [reduce, jnp.concatenate([down[: rows // 2], down[rows // 2 :]], 1), up], 0
    )


def gather_feed(expand, reduce, down, up):
    everyone = ("seq", "enc")
    if expand.shape[0] % 32 == 0:
        return lax.all_gather(pack_feed(expand, reduce, down, up), everyone)
    whole = [lax.all_gather(v, everyone, axis=0, tiled=True) for v in (expand, reduce, down, up)]
    return pack_feed(*whole)[None]


def flat(block):
    return block.reshape(block.shape[0] * block.shape[1], block.shape[2])


def adapter_parts(block):
    count, rows, width = block.shape
    half = rows // 2
    down = jnp.stack([block[:, :half, : width // 2], block[:, :half, width // 2 :]], 1)
    return down.reshape(count * rows, width // 2), flat(block[:, half:])


def feed_scratch(packed):
    count, depth, width = packed.shape
    rows = depth // 9
    spread = max(count // 4, 1)
    return (
        [pltpu.VMEM((count, rows, width), LOW) for _ in range(4)]
        + [pltpu.VMEM((spread, width // spread, width), LOW) for _ in range(4)]
        + [pltpu.VMEM((count, rows, width), LOW), pltpu.VMEM((width, width), LOW)]
        + [pltpu.SemaphoreType.DMA((10,))]
    )


def feed_copies(packed_ref, out_ref, scratch):
    *rooms, sem = scratch
    count, depth, width = packed_ref.shape
    rows = depth // 9
    places = [packed_ref.at[:, pl.ds(q * rows, rows), :] for q in range(4)]
    for q in range(4):
        if count >= 4:
            spread = count // 4
            places.append(packed_ref.at[pl.ds(q * spread, spread), pl.ds(4 * rows, 4 * rows), :])
        else:
            places.append(packed_ref.at[:, pl.ds(4 * rows + q * width, width), :])
    places += [packed_ref.at[:, pl.ds(8 * rows, rows), :], out_ref]
    copies = [
        pltpu.make_async_copy(place, room, sem.at[i])
        for i, (place, room) in enumerate(zip(places, rooms))
    ]
    return copies[:4], copies[4:8], copies[8], copies[9]


def norm_stats(values):
    middle = jnp.mean(values, -1, keepdims=True)
    centred = values - middle
    scale = lax.rsqrt(jnp.mean(centred * centred, -1, keepdims=True) + EPSILON)
    return centred * scale, scale


def norm_back(grad, values, gain):
    hat, scale = norm_stats(values)
    scaled = grad * gain
    inner = scaled - jnp.mean(scaled, -1, keepdims=True)
    inner = inner - hat * jnp.mean(scaled * hat, -1, keepdims=True)
    return (
        inner * scale,
        jnp.sum(grad * hat, 0, keepdims=True),
        jnp.sum(grad, 0, keepdims=True),
    )


PART = 256


def branch_kernel(first, n_parts, *refs):
    parts, refs = refs[:n_parts], refs[n_parts:]
    res_ref, norm_ref, packed_ref, proj_ref = refs[:4]
    va_ref, x_ref, slope_ref, act_ref, bend_ref, vb_ref, low_ref = refs[4:11]
    total, slopes, slope_sem = refs[11:14]
    scratch = refs[14:]
    expands, reduces, small, proj = feed_copies(packed_ref, proj_ref, scratch)
    width = res_ref.shape[1]
    for copy in [proj] + [c for pair in zip(expands, reduces) for c in pair] + [small]:
        copy.start()
    proj.wait()
    context = jnp.concatenate([p[...] for p in parts], 1)
    va = res_ref[...] + jnp.dot(context, scratch[9][...], preferred_element_type=F32)
    va_ref[...] = va
    hat, _ = norm_stats(va)
    after = hat * norm_ref[first : first + 1, :] + norm_ref[7 + first : 8 + first, :]
    x = after.astype(LOW)
    x_ref[...] = x
    total[...] = after
    sends = []
    for q in range(4):
        expands[q].wait()
        expand = flat(scratch[q][...])
        pre = jnp.dot(x, expand[:, :PART], preferred_element_type=F32)
        acts = []
        for start in range(0, width, PART):
            now = pre
            if start + PART < width:
                pre = jnp.dot(
                    x, expand[:, start + PART : start + 2 * PART], preferred_element_type=F32
                )
            act, slope = gelu_both(now)
            slopes[q, :, start : start + PART] = slope
            acts.append(act.astype(LOW))
        sends.append(
            pltpu.make_async_copy(
                slopes.at[q], slope_ref.at[:, pl.ds(q * width, width)], slope_sem.at[q]
            )
        )
        sends[q].start()
        reduces[q].wait()
        total[...] += jnp.dot(
            jnp.concatenate(acts, 1), flat(scratch[4 + q][...]), preferred_element_type=F32
        )
    small.wait()
    down, up = adapter_parts(scratch[8][...])
    act, slope = gelu_both(jnp.dot(x, down, preferred_element_type=F32))
    act = act.astype(LOW)
    act_ref[...] = act
    bend_ref[...] = slope
    vb = total[...] + ADAPTER_SCALE * jnp.dot(act, up, preferred_element_type=F32)
    vb_ref[...] = vb
    hat, _ = norm_stats(vb)
    low_ref[...] = (
        hat * norm_ref[first + 1 : first + 2, :] + norm_ref[8 + first : 9 + first, :]
    ).astype(LOW)
    for send in sends:
        send.wait()


def branch(parts, residual, norms, first, packed, proj):
    rows, width = residual.shape
    hidden, small = 4 * width, width // 2
    vmem = pl.BlockSpec(memory_space=pltpu.VMEM)
    hbm = pl.BlockSpec(memory_space=pl.ANY)
    va, x, slope, act, bend, vb, low = pl.pallas_call(
        lambda *refs: branch_kernel(first, len(parts), *refs),
        out_shape=[
            jax.ShapeDtypeStruct((rows, width), F32),
            jax.ShapeDtypeStruct((rows, width), LOW),
            jax.ShapeDtypeStruct((rows, hidden), F32),
            jax.ShapeDtypeStruct((rows, small), LOW),
            jax.ShapeDtypeStruct((rows, small), F32),
            jax.ShapeDtypeStruct((rows, width), F32),
            jax.ShapeDtypeStruct((rows, width), LOW),
        ],
        in_specs=[vmem] * (len(parts) + 2) + [hbm, hbm],
        out_specs=[vmem, vmem, hbm, vmem, vmem, vmem, vmem],
        scratch_shapes=[
            pltpu.VMEM((rows, width), F32),
            pltpu.VMEM((4, rows, width), F32),
            pltpu.SemaphoreType.DMA((4,)),
        ]
        + feed_scratch(packed),
        compiler_params=pltpu.CompilerParams(vmem_limit_bytes=56 * MIB),
        cost_estimate=pl.CostEstimate(
            flops=4 * rows * width * (hidden + small) + 2 * rows * width * width,
            bytes_accessed=4 * width * (hidden + small) + 4 * rows * hidden,
            transcendentals=2 * rows * hidden,
        ),
    )(*parts, residual, norms, packed, proj)
    return low, (va, x, slope, act, bend, vb)


def branch_back_kernel(first, n_parts, *refs):
    n_given, refs = (refs[0], refs[1:])
    given, refs = refs[:n_given], refs[n_given:]
    vb_ref, va_ref, norm_ref, bend_ref, slope_ref, packed_ref, proj_ref = refs[:7]
    dva_ref, sums_ref, dpre_ref, ga_ref = refs[7:11]
    spread_refs, refs = refs[11 : 11 + n_parts], refs[11 + n_parts :]
    total, slopes, slope_sem = refs[:3]
    scratch = refs[3:]
    expands, reduces, small, proj = feed_copies(packed_ref, proj_ref, scratch)
    width = va_ref.shape[1]
    gets = [
        pltpu.make_async_copy(
            slope_ref.at[:, pl.ds(q * width, width)], slopes.at[q], slope_sem.at[q]
        )
        for q in range(4)
    ]
    for copy in [small] + [c for three in zip(reduces, gets, expands) for c in three] + [proj]:
        copy.start()
    if n_given == 2:
        grad = given[0][...].astype(F32) + given[1][...].astype(F32)
    else:
        mean, total_own, other, total_other, label, valid = [r[...] for r in given]
        grad = merge_means((mean, total_own), (other, total_other))[0]
        grad = (grad - label.astype(F32)) * valid
    grad_out, gain, shift = norm_back(grad, vb_ref[...], norm_ref[first + 1 : first + 2, :])
    sums_ref[2:3, :] = gain
    sums_ref[3:4, :] = shift
    g = grad_out.astype(LOW)
    ga = (ADAPTER_SCALE * grad_out).astype(LOW)
    ga_ref[...] = ga
    small.wait()
    down, up = adapter_parts(scratch[8][...])
    pre = (dense_back(ga, up) * bend_ref[...]).astype(LOW)
    dpre_ref[...] = pre
    total[...] = grad_out + dense_back(pre, down)
    for q in range(4):
        reduces[q].wait()
        reduce = flat(scratch[4 + q][...])
        gets[q].wait()
        grad = dense_back(g, reduce[:PART])
        pres = []
        for start in range(0, width, PART):
            now = grad
            if start + PART < width:
                grad = dense_back(g, reduce[start + PART : start + 2 * PART])
            pres.append((now * slopes[q, :, start : start + PART]).astype(LOW))
        expands[q].wait()
        total[...] += dense_back(jnp.concatenate(pres, 1), flat(scratch[q][...]))
    dva, gain, shift = norm_back(total[...], va_ref[...], norm_ref[first : first + 1, :])
    sums_ref[0:1, :] = gain
    sums_ref[1:2, :] = shift
    dva_ref[...] = dva
    proj.wait()
    spread = dense_back(dva.astype(LOW), scratch[9][...]).astype(LOW)
    share = width // n_parts
    for j in range(n_parts):
        spread_refs[j][...] = spread[:, j * share : (j + 1) * share]


def branch_back(given, kept, norms, first, packed, proj, n_parts):
    va, x, slope, act, bend, vb = kept
    rows, width = va.shape
    hidden, small = 4 * width, width // 2
    vmem = pl.BlockSpec(memory_space=pltpu.VMEM)
    hbm = pl.BlockSpec(memory_space=pl.ANY)
    dva, sums, dpre, ga, *spread = pl.pallas_call(
        lambda *refs: branch_back_kernel(first, n_parts, len(given), *refs),
        out_shape=[
            jax.ShapeDtypeStruct((rows, width), F32),
            jax.ShapeDtypeStruct((4, width), F32),
            jax.ShapeDtypeStruct((rows, small), LOW),
            jax.ShapeDtypeStruct((rows, width), LOW),
        ]
        + [jax.ShapeDtypeStruct((rows, width // n_parts), LOW)] * n_parts,
        in_specs=[vmem] * (4 + len(given)) + [hbm] * 3,
        out_specs=[vmem] * (4 + n_parts),
        scratch_shapes=[
            pltpu.VMEM((rows, width), F32),
            pltpu.VMEM((4, rows, width), F32),
            pltpu.SemaphoreType.DMA((4,)),
        ]
        + feed_scratch(packed),
        compiler_params=pltpu.CompilerParams(vmem_limit_bytes=56 * MIB),
        cost_estimate=pl.CostEstimate(
            flops=4 * rows * width * (hidden + small) + 2 * rows * width * width,
            bytes_accessed=4 * width * (hidden + small) + 4 * rows * hidden,
            transcendentals=0,
        ),
    )(*given, vb, va, norms, bend, slope, packed, proj)
    return dva, spread, sums, (x, dpre, act, ga)


def middle_back_kernel(first, n_parts, *refs):
    res_ref, own_ref, far_ref, va_ref, norm_ref, proj_ref = refs[:6]
    dva_ref, sums_ref = refs[6:8]
    room, sem = refs[-2:]
    copy = pltpu.make_async_copy(proj_ref, room, sem)
    copy.start()
    grad = res_ref[...] + own_ref[...].astype(F32) + far_ref[...].astype(F32)
    dva, gain, shift = norm_back(grad, va_ref[...], norm_ref[first : first + 1, :])
    dva_ref[...] = dva
    sums_ref[0:1, :] = gain
    sums_ref[1:2, :] = shift
    copy.wait()
    spread = dense_back(dva.astype(LOW), room[...]).astype(LOW)
    share = spread.shape[1] // n_parts
    for j in range(n_parts):
        refs[8 + j][...] = spread[:, j * share : (j + 1) * share]


def middle_back(residual, own, far, va, norms, first, proj, n_parts):
    rows, width = va.shape
    vmem = pl.BlockSpec(memory_space=pltpu.VMEM)
    dva, sums, *spread = pl.pallas_call(
        lambda *refs: middle_back_kernel(first, n_parts, *refs),
        out_shape=[
            jax.ShapeDtypeStruct((rows, width), F32),
            jax.ShapeDtypeStruct((2, width), F32),
        ]
        + [jax.ShapeDtypeStruct((rows, width // n_parts), LOW)] * n_parts,
        in_specs=[vmem] * 5 + [pl.BlockSpec(memory_space=pl.ANY)],
        out_specs=[vmem] * (2 + n_parts),
        scratch_shapes=[pltpu.VMEM(proj.shape, LOW), pltpu.SemaphoreType.DMA],
        compiler_params=pltpu.CompilerParams(vmem_limit_bytes=52 * MIB),
        cost_estimate=pl.CostEstimate(
            flops=0, bytes_accessed=0, transcendentals=0
        ),
    )(residual, own, far, va, norms, proj)
    return dva, spread, sums


def adapter_grad_kernel(core_ref, *refs):
    given, refs = refs[:8], refs[8:]
    keep_ref, send_ref = refs[:2]
    rooms, (down, up, keep, send, sem, sem_out) = refs[2:10], refs[10:]
    copies = [pltpu.make_async_copy(g, r, sem.at[i]) for i, (g, r) in enumerate(zip(given, rooms))]
    for copy in copies:
        copy.start()
    core = core_ref[0]
    pairs, depth, width = keep.shape
    rows = depth // 2
    half, small = rows // 2, width // 2
    for k in range(2):
        for copy in copies[4 * k : 4 * k + 4]:
            copy.wait()
        x, dpre, act, ga = rooms[4 * k : 4 * k + 4]
        down[...] = inner_rows(x[...], dpre[...])
        up[...] = inner_rows(act[...], ga[...])
        top, middle, end = k * rows, k * rows + half, (k + 1) * rows
        for ref, side in ((send, 1 - core), (keep, core)):
            for pair in range(pairs):
                device = 2 * pair + side
                at = pl.multiple_of(device * rows, rows)
                ref[pair, top:middle, :small] = down[pl.ds(at, half), :].astype(LOW)
                ref[pair, top:middle, small:] = down[pl.ds(at + half, half), :].astype(LOW)
                ref[pair, middle:end, :] = up[
                    pl.ds(pl.multiple_of(device * half, half), half), :
                ].astype(LOW)
    outs = [
        pltpu.make_async_copy(send, send_ref, sem_out.at[0]),
        pltpu.make_async_copy(keep, keep_ref, sem_out.at[1]),
    ]
    for copy in outs:
        copy.start()
    for copy in outs:
        copy.wait()


def adapter_grads(given, core):
    width, small = given[0][0].shape[1], given[0][1].shape[1]
    n_all = lax.axis_size("seq") * lax.axis_size("enc")
    rows = width // n_all
    if rows % 16:
        layers = []
        for x, dpre, act, ga in given:
            down, up = inner_rows(x, dpre), inner_rows(act, ga)
            folded = down.reshape(n_all, 2, rows // 2, small).transpose(0, 2, 1, 3)
            layers += [folded.reshape(n_all, rows // 2, width), up.reshape(n_all, rows // 2, width)]
        both = jnp.concatenate(layers, 1).reshape(n_all // 2, 2, 2 * rows, width)
        first = core == 0
        keep, send = jnp.where(first, both[:, 0], both[:, 1]), jnp.where(first, both[:, 1], both[:, 0])
        return keep.astype(LOW), send.astype(LOW)
    shape = (n_all // 2, 2 * rows, width)
    hbm = pl.BlockSpec(memory_space=pl.ANY)
    loads = list(given[0]) + list(given[1])
    return pl.pallas_call(
        adapter_grad_kernel,
        out_shape=[jax.ShapeDtypeStruct(shape, LOW)] * 2,
        in_specs=[pl.BlockSpec(memory_space=pltpu.SMEM)] + [hbm] * 8,
        out_specs=[hbm] * 2,
        scratch_shapes=[pltpu.VMEM(v.shape, LOW) for v in loads]
        + [pltpu.VMEM((width, small), F32), pltpu.VMEM((small, width), F32)]
        + [pltpu.VMEM(shape, LOW), pltpu.VMEM(shape, LOW)]
        + [pltpu.SemaphoreType.DMA((8,)), pltpu.SemaphoreType.DMA((2,))],
        compiler_params=pltpu.CompilerParams(vmem_limit_bytes=60 * MIB),
        cost_estimate=pl.CostEstimate(flops=0, bytes_accessed=0, transcendentals=0),
    )(core.reshape(1).astype(jnp.int32), *loads)


def head_kernel(n_blocks, *refs):
    o_refs, e_ref = refs[:n_blocks], refs[n_blocks]
    g_refs, lse_refs = refs[n_blocks + 1 : 2 * n_blocks + 1], refs[2 * n_blocks + 1 : -3]
    acc, peak, mass = refs[-3:]
    step = pl.program_id(0)
    rows = o_refs[0].shape[0]
    part = 2 * rows

    @pl.when(step == 0)
    def _():
        acc[...] = jnp.zeros_like(acc)
        peak[...] = jnp.full_like(peak, -1e30)
        mass[...] = jnp.zeros_like(mass)

    table = e_ref[...]
    spans = [pl.ds(start, part) for start in range(0, n_blocks * rows, part)]

    def logits_of(h):
        both = jnp.concatenate([o_refs[2 * h][...], o_refs[2 * h + 1][...]], 0)
        return scores_of(both, table)

    before = [peak[at, :1] for at in spans]
    held = [mass[at, :] for at in spans]
    coming = logits_of(0)
    highest, summed = [], []
    for h, at in enumerate(spans):
        logits = coming
        if h + 1 < len(spans):
            coming = logits_of(h + 1)
        highest.append(jnp.maximum(before[h], jnp.max(logits, -1, keepdims=True)))
        exponent = jnp.exp(logits - highest[h])
        fade = jnp.exp(before[h] - highest[h])
        summed.append(held[h] * fade + jnp.sum(exponent, -1, keepdims=True))
        acc[at, :] = acc[at, :] * fade + jnp.dot(
            exponent.astype(LOW), table, preferred_element_type=F32
        )
    for h, at in enumerate(spans):
        mass[at, :] = summed[h]
        peak[at, :] = jnp.broadcast_to(highest[h], (part, 128))

    @pl.when(step == pl.num_programs(0) - 1)
    def _():
        for j in range(n_blocks):
            at = pl.ds(j * rows, rows)
            g_refs[j][...] = (acc[at, :] / mass[at, :1]).astype(LOW)
            lse_refs[j][...] = peak[at, :1] + jnp.log(mass[at, :1])


def head(blocks, table):
    rows, width = blocks[0].shape
    count = len(blocks)
    entries = table.shape[0]
    tile = next(t for t in (1280, 1024, 640, 512, 256, 128) if entries % t == 0)
    block = pl.BlockSpec((rows, width), lambda j: (0, 0))
    results = pl.pallas_call(
        lambda *refs: head_kernel(count, *refs),
        grid=(entries // tile,),
        out_shape=[jax.ShapeDtypeStruct((rows, width), LOW)] * count
        + [jax.ShapeDtypeStruct((rows, 1), F32)] * count,
        in_specs=[block] * count + [pl.BlockSpec((tile, width), lambda j: (j, 0))],
        out_specs=[block] * count + [pl.BlockSpec((rows, 1), lambda j: (0, 0))] * count,
        scratch_shapes=[
            pltpu.VMEM((count * rows, width), F32),
            pltpu.VMEM((count * rows, 128), F32),
            pltpu.VMEM((count * rows, 128), F32),
        ],
        compiler_params=pltpu.CompilerParams(vmem_limit_bytes=60 * MIB),
        cost_estimate=pl.CostEstimate(
            flops=4 * count * rows * width * entries,
            bytes_accessed=2 * width * entries,
            transcendentals=count * rows * entries,
        ),
    )(*blocks, table)
    return list(results[:count]), list(results[count:])


def adapters_plane(keep, came, seq, enc):
    n_seq, n_enc = lax.axis_size("seq"), lax.axis_size("enc")
    near = n_seq // 4
    rows, width = keep.shape[1:]

    def block(s_off, e_off):
        start = (0, (seq & (near - 1)) ^ s_off, (enc >> 1) ^ (e_off >> 1), 0, 0)
        parts = [v.reshape(4, near, n_enc // 2, rows, width) for v in (keep, came)]
        parts = [lax.dynamic_slice(v, start, (4, 1, 1, rows, width))[:, 0, 0] for v in parts]
        return parts[0].astype(F32) + parts[1].astype(F32)

    return [block(0, 0)] + [flip_both(block(s, e).astype(LOW), s, e) for s, e in plane_offsets()[1:]]


def adapters_line(parts, seq):
    held = tree_sum([p.astype(F32) for p in parts])
    slow = seq // (lax.axis_size("seq") // 4)
    parts = [lax.dynamic_index_in_dim(held, slow ^ k, 0, keepdims=False) for k in range(4)]
    return parts[:1] + [
        flip(p.astype(LOW), "seq", o) for p, o in zip(parts[1:], line_offsets()[1:])
    ]


def sum_everywhere(values):
    values = values + flip(values, "enc", 1)
    values = tree_sum([values] + [flip_both(values, s, e) for s, e in plane_offsets()[1:]])
    return tree_sum([values] + [flip(values, "seq", o) for o in line_offsets()[1:]])


def shards(
    source_ids,
    target_ids,
    labels,
    lengths,
    embedding,
    positions,
    attention_in,
    attention_out,
    feed_in,
    feed_out,
    adapter_down,
    adapter_up,
    norm_params,
    down_moment,
    down_second,
    up_moment,
    up_second,
    norm_moment,
    norm_second,
):
    n_seq, n_enc = lax.axis_size("seq"), lax.axis_size("enc")
    n_all = n_seq * n_enc
    seq, enc = lax.axis_index("seq"), lax.axis_index("enc")
    core = enc & 1
    own_rows = source_ids.shape[1]
    width = embedding.shape[1]
    entries = embedding.shape[0]
    length = own_rows * n_enc
    share = width // n_enc
    source_length, target_length = lengths[0, 0], lengths[0, 1]

    blocks = jnp.arange(n_enc) ^ enc
    spots = (blocks[:, None] * own_rows + jnp.arange(own_rows)[None, :]).reshape(length)
    spots = spots.astype(jnp.int32)
    source_limit = jnp.broadcast_to(source_length, (length, 1)).astype(jnp.int32)
    causal_limit = jnp.minimum(spots + 1, target_length)[:, None].astype(jnp.int32)
    spots = spots[None, :]
    in_strip = share // 128

    def gather_rows(rows_low):
        return jnp.concatenate(gather_enc(rows_low), 0)

    def lookup(ids):
        inside = (ids >= 0) & (ids < entries)
        found = jnp.take(embedding, jnp.clip(ids, 0, entries - 1), axis=0)
        return jnp.where(inside[:, :, None], found, jnp.zeros((), LOW))

    def rows_of(found):
        return scatter_enc([found[j] for j in range(n_enc)])

    def own_parts(context):
        return swap_blocks([context[j * own_rows : (j + 1) * own_rows] for j in range(n_enc)])

    def all_heads(spread):
        return jnp.concatenate(swap_blocks(spread), 0)

    def row_blocks(partial):
        return [partial[j * own_rows : (j + 1) * own_rows] for j in range(n_enc)]

    down_low, up_low = adapter_down.astype(LOW), adapter_up.astype(LOW)
    feeds = [gather_feed(feed_in[k], feed_out[k], down_low[k], up_low[k]) for k in range(2)]

    gains = norm_params.astype(LOW).astype(F32)
    ids = jnp.concatenate([source_ids, target_ids, labels], 0).astype(F32)
    small_own = jnp.concatenate([ids.reshape(1, -1), gains.reshape(1, -1)], 1)
    small_all = unxor([v[0] for v in jnp.split(lax.all_gather(small_own, "enc"), n_enc)], enc)
    small_all = jnp.concatenate(small_all, 0)
    all_ids = small_all[:, : 3 * own_rows].astype(jnp.int32).reshape(n_enc, 3, own_rows)
    all_ids = all_ids - enc * entries
    gains = small_all[:, 3 * own_rows :].astype(LOW)[None]

    triple = attention_in.reshape(3, -1, 3, n_enc, share).transpose(3, 1, 0, 2, 4)
    shard_rows = triple.shape[1]
    strip_rows, pair_rows = n_enc * shard_rows, 2 * shard_rows
    triple = triple.reshape(n_enc, shard_rows, 9 * share)
    strip = lax.all_to_all(triple, "enc", 0, 0, tiled=True).reshape(strip_rows, 9 * share)
    strip, late = strip[:, : 6 * share], strip[:, 6 * share :]
    half = width // 2
    packed = jnp.concatenate(
        [attention_out[k][:, h * half : (h + 1) * half] for h in range(2) for k in range(3)], 1
    )
    pair_out = pair_split(packed, core)

    ids = [all_ids[:, k] for k in range(3)]
    strip, pair_out, *ids = gate([strip, pair_out] + ids)

    slow, slow_out = slow_flips_both(strip, pair_out)
    for mask in bits("seq"):
        gains = jnp.concatenate([gains, flip(gains, "seq", mask)], 0)
    arrived = gate([lookup(v) for v in ids] + slow + (slow_out or []))
    found, slow, slow_out = arrived[:3], arrived[3:6], arrived[6:]
    if not slow_out:
        slow_out = [v[strip_rows:] for v in slow]
        slow = [v[:strip_rows] for v in slow]
    order_seq, order_enc = jnp.arange(n_seq) ^ seq, jnp.arange(n_enc) ^ enc
    gains = jnp.take(jnp.take(gains, order_seq, axis=0), order_enc, axis=1)
    gains = gains.reshape(n_all, 14, width // n_all).transpose(1, 0, 2)
    norms = gains.reshape(2, 7, width).astype(F32)

    strip_offsets, strips = near_flips(jnp.stack([strip] + slow))
    source_rows, target_rows = rows_of(found[0]), rows_of(found[1])

    in_enc, in_dec = assemble_strips(strip_offsets, strips, 2, seq)
    encoder_in, encoder_hat = norm_start(source_rows + positions[0].astype(F32), norms, 0)
    decoder_in, decoder_hat = norm_start(target_rows + positions[1].astype(F32), norms, 3)
    across = gather_across(encoder_in.astype(LOW))
    decoder_low, *across[1:] = gate([decoder_in.astype(LOW)] + across[1:])
    encoder_all = jnp.concatenate(gather_pair(across), 0)
    decoder_all = gather_rows(decoder_low)
    stacked = jnp.stack([pair_out] + slow_out)
    singles = plane_start(stacked)

    triple_encoder = dense(encoder_all, in_enc).astype(LOW)
    enc_args = (triple_encoder, triple_encoder, in_strip, 2 * in_strip, source_limit, spots)
    context_enc, total_encoder = attend(*enc_args)
    slow = slow_flips(late)
    context_enc, *arrived = gate([context_enc] + slow + singles)
    slow, singles = arrived[:3], arrived[3:]
    own, other, mine = plane_finish(stacked, singles, core)
    partners = [flip(v, "enc", 1) for v in mine]
    triple_decoder = dense(decoder_all, in_dec).astype(LOW)
    dec_args = (triple_decoder, triple_decoder, in_strip, 2 * in_strip, causal_limit, spots)
    context_dec, total_decoder = attend(*dec_args, after=[context_enc])

    def out_layout(pair, side):
        row = pair * pair_rows
        block = (row // share) ^ enc
        return [
            (0, k * half, pair_rows, half, k, block * share + row % share, side * half)
            for k in range(3)
        ]

    attend_out = assemble_matrix(
        own, other, mine, partners, out_layout, [(width, width)] * 3, seq, enc
    )
    late_offsets, strips = near_flips(jnp.stack([late] + slow))
    attended = dense(jnp.concatenate(own_parts(context_dec), 1), attend_out[1])
    causal_in = decoder_in + attended
    after_causal = norm_start(causal_in, norms, 4)[0]
    in_cross = assemble_strips(late_offsets, strips, 1, seq)[0]
    attend_in = [in_enc, in_dec, in_cross]
    causal_all = gather_rows(after_causal.astype(LOW))
    norm_rows = norms.reshape(14, width)
    encoded_low, kept_enc = branch(
        own_parts(context_enc), encoder_in, norm_rows, 1, feeds[0], attend_out[0]
    )
    query_cross = dense(causal_all, in_cross[:, :share]).astype(LOW)

    encoded_all = gather_rows(encoded_low)
    pairs_cross = dense(encoded_all, in_cross[:, share:]).astype(LOW)
    cross_args = (query_cross, pairs_cross, 0, in_strip, source_limit, spots)
    context, total_cross = attend(*cross_args)
    context, found_label = gate([context, found[2]])
    label_rows, label_came = scatter_two([found_label[j] for j in range(n_enc)])
    decoded_low, kept_dec = branch(
        own_parts(context), after_causal, norm_rows, 5, feeds[1], attend_out[2]
    )

    decoded_low, label_came = gate([decoded_low, label_came])

    *decoded_all, encoder_low, decoder_low = gate(
        gather_enc(decoded_low) + [encoder_hat.astype(LOW), decoder_hat.astype(LOW)]
    )
    pulled, totals = head(decoded_all, embedding)
    hats = gather_across(encoder_low) + gather_across(decoder_low)
    *results, decoded_low, label_came = gate(
        pulled + totals + hats + [decoded_all[0], label_came]
    )
    pulled, totals, hats = results[:n_enc], results[n_enc : 2 * n_enc], results[2 * n_enc :]
    label_rows = (label_rows.astype(F32) + label_came.astype(F32)).astype(LOW)
    row_spots = enc * own_rows + jnp.arange(own_rows)
    valid = (row_spots < target_length).astype(F32)[:, None]
    picked = jnp.sum(decoded_low.astype(F32) * label_rows.astype(F32), -1, keepdims=True)
    own_mean, far_mean, hats = merge_enc(pulled, totals, hats)
    half_hats = len(hats) // 2
    hats = gather_pair(hats[:half_hats]) + gather_pair(hats[half_hats:])
    far, *hats = gate([far_mean[0]] + hats)
    encoder_hats, decoder_hats = hats[:n_enc], hats[n_enc:]
    highest = jnp.maximum(own_mean[1], far_mean[1])
    log_total = highest + jnp.log(
        jnp.exp(own_mean[1] - highest) + jnp.exp(far_mean[1] - highest)
    )
    loss_own = jnp.sum((log_total - picked) * valid)

    grad_res, spread, sums_dec, given_dec = branch_back(
        [own_mean[0], own_mean[1], far, far_mean[1], label_rows, valid],
        kept_dec,
        norm_rows,
        5,
        feeds[1],
        attend_out[2],
        n_enc,
    )
    grads = attend_back(*cross_args, all_heads(spread), total_cross)
    own_encoded, far_encoded = scatter_two(
        row_blocks(dense_back(grads[:, share:], attend_in[2][:, share:]))
    )
    own_causal, far_causal = scatter_two(
        row_blocks(dense_back(grads[:, :share], attend_in[2][:, :share]))
    )
    grad_enc, spread, sums_enc, given_enc = branch_back(
        [own_encoded, far_encoded], kept_enc, norm_rows, 1, feeds[0], attend_out[0], n_enc
    )
    spread = swap_blocks(spread)
    x, dpre, act, ga = given_enc
    dpre, far_causal = gate([dpre, far_causal])
    keep, send = adapter_grads([(x, dpre, act, ga), given_dec], core)
    came = flip(send, "enc", 1)
    grad_dec, spread_dec, sums_four = middle_back(
        grad_res, own_causal, far_causal, causal_in, norm_rows, 4, attend_out[1], n_enc
    )
    sums_zero = attend_back(
        *enc_args,
        jnp.concatenate(spread, 0),
        total_encoder,
        sum_with=(encoder_hats, in_enc, encoder_hat, grad_enc),
        after=[grad_dec],
    )
    parts = adapters_plane(keep, came, seq, enc)
    sums_zero, *parts[1:] = gate([sums_zero] + parts[1:])
    parts = adapters_line(parts, seq)
    sums_three = attend_back(
        *dec_args,
        all_heads(spread_dec),
        total_decoder,
        sum_with=(decoder_hats, in_dec, decoder_hat, grad_dec),
        after=[sums_zero],
        half=enc >> 1,
    )
    sums_three, *parts[1:] = gate([sums_three] + parts[1:])

    count_own = jnp.clip(target_length - enc * own_rows, 0, own_rows).astype(F32)
    summed, grad_down, grad_up = payload(
        loss_own,
        count_own,
        parts,
        [sums_zero, sums_three, sums_four, sums_enc, sums_dec],
        adapter_down.shape[2],
    )
    summed = sum_everywhere(summed)
    per = width // n_all
    own = lax.dynamic_slice_in_dim(summed, (seq * n_enc + enc) * per, per, 1)[:14]
    loss_sum, token_total, grad_norm, factor, *adapters = optimizer_step(
        summed,
        [grad_down, grad_up],
        [down_moment, down_second, adapter_down, up_moment, up_second, adapter_up],
    )
    new_norms = adamw(
        own.reshape(2, 7, per) * factor, norm_moment, norm_second, norm_params, RATE_NORMS, 0.0
    )
    return (loss_sum, token_total, grad_norm, *adapters, *new_norms)


def solution(mesh):
    everywhere = P(None, ("seq", "enc"), None)
    columns = P(None, None, ("seq", "enc"))
    return jax.shard_map(
        shards,
        mesh=mesh,
        in_specs=(
            P("seq", "enc"),
            P("seq", "enc"),
            P("seq", "enc"),
            P("seq", None),
            P("enc", None),
            P(None, "enc", None),
            everywhere,
            everywhere,
            everywhere,
            everywhere,
            everywhere,
            everywhere,
            columns,
            everywhere,
            everywhere,
            everywhere,
            everywhere,
            columns,
            columns,
        ),
        out_specs=(
            P(),
            P(),
            P(),
            everywhere,
            everywhere,
            everywhere,
            everywhere,
            everywhere,
            everywhere,
            columns,
            columns,
            columns,
        ),
        check_vma=False,
    )
```
